128 devices in a mesh: gz: 32 (over x, z_hi, y), gy: 4 (over z_lo, core).
Axes of the slice: x: 4, y: 4, z: 4 (z_hi: 2, z_lo: 2; z = z_hi * 2 + z_lo), core: 2. Of those that a mesh axis runs over, the one named last changes fastest.
Arguments:
- density_field: float32 [4, 64, 256, 256], P(None, 'gz', 'gy'), may hold values from -42 to 42
- first_weight: bfloat16 [54, 128], replicated, may hold values from -0.875 to 0.875
- first_bias: float32 [128], replicated, may hold values from -3 to 3
- middle_weight: bfloat16 [128, 128], replicated, may hold values from -0.5 to 0.5
- middle_bias: float32 [128], replicated, may hold values from -3 to 3
- output_weight: bfloat16 [108, 128], replicated, may hold values from -0.109375 to 0.109375
- output_bias: float32 [4], replicated, may hold values from -3 to 3
- radial_weights: float32 [16, 8, 32], replicated, may hold values from -1 to 1
Outputs:
- factored: float32 [16, 32, 128, 128], P(None, 'gz', 'gy')
- latent: float32 [16, 32, 128, 128], P(None, 'gz', 'gy')
- log_density: float32 [], replicated
The draws below stay inside these ranges and needn't reach their ends.
All inputs are finite; a program needn't handle non-finite values.
Results may differ from the reference program's by a relative error of at most 0.00065.
The reference program's roundings to bfloat16 on the way (of `lower_half`, `first_layer` and `second_layer`) count: a program that leaves them out, or rounds other values in their place, can miss the bound.
Values may be sent and summed in bfloat16 or wider, within the bound.
A program may use at most 128 MiB of HBM per device.

```python
import math
import jax
import jax.numpy as jnp
from jax import lax

CZ = 2
NX = 256
H = 128
BASIS = 32
NZ = 64
NY = 256


def draw_density_field(key, part):
    key = jax.random.fold_in(key, 7)
    normal_key, rough_key, block_key, offset_key = jax.random.split(key, 4)
    full_shape = (4, NZ, NY, NX)
    depth_ramp = jnp.exp(jnp.log(3.0) * jnp.arange(NZ, dtype=jnp.float32) / NZ).reshape(1, NZ, 1, 1)
    block_scale = jnp.exp(jax.random.uniform(block_key, (NZ // CZ,), jnp.float32, jnp.log(0.5), jnp.log(2.0)))
    block_scale = jnp.repeat(block_scale, CZ).reshape(1, NZ, 1, 1)
    block_offset = jax.random.uniform(offset_key, (NZ // CZ,), jnp.float32, -1.5, 1.5)
    block_offset = jnp.repeat(block_offset, CZ).reshape(1, NZ, 1, 1)
    roughness = jax.random.uniform(rough_key, full_shape, jnp.float32, 0.7, 1.4)
    baseline = jnp.clip(jax.random.normal(normal_key, full_shape, jnp.float32), -3.5, 3.5)
    return (baseline * roughness + block_offset) * depth_ramp * block_scale


def noise(rng, dims, deviation, bound, held_as=jnp.bfloat16):
    result = jax.random.normal(rng, dims, jnp.float32) * deviation
    return jnp.minimum(jnp.maximum(result, -bound), bound).astype(held_as)


def setup_inputs(seed: int = 0) -> dict:
    splits = jax.random.split(jax.random.key(seed), 9)
    return {
        "density_field": draw_density_field(jax.random.fold_in(splits[8], 71), 0),
        "first_weight": noise(splits[1], (54, H), 54 ** -0.5, 0.875),
        "first_bias": noise(splits[2], (H,), 0.5, 3.0, jnp.float32),
        "middle_weight": noise(splits[3], (H, H), H ** -0.5, 0.5),
        "middle_bias": noise(splits[4], (H,), 0.5, 3.0, jnp.float32),
        "output_weight": noise(splits[5], (108, H), (27 * H) ** -0.5, 0.109375),
        "output_bias": noise(splits[6], (4,), 0.5, 3.0, jnp.float32),
        "radial_weights": noise(splits[7], (16, 8, BASIS), 0.15, 1.0, jnp.float32),
    }


precise = lax.Precision.HIGHEST

def signed_freq(counting, length):
    return jnp.where(2 * counting >= length, counting - length, counting).astype(jnp.float32) / length

def radial_basis(kappa_norm, count_basis):
    centres = jnp.arange(count_basis, dtype=jnp.float32).reshape((count_basis,) + (1,) * kappa_norm.ndim)
    scaled = kappa_norm[None] * (count_basis - 1) - centres
    return jnp.exp(-scaled * scaled)

def reference(density_field, first_weight, first_bias, middle_weight, middle_bias, output_weight, output_bias, radial_weights):
    lower_half = density_field[0:2].astype(jnp.bfloat16)
    padded = jnp.pad(lower_half, ((0, 0), (2, 2), (1, 1), (1, 1)))

    def hidden_plane(plane_index):
        window = lax.dynamic_slice_in_dim(padded, plane_index, 3, 1)
        columns = jnp.stack([window[channel, z_tap, y_tap:y_tap + NY, x_tap:x_tap + NX] for channel in range(2) for z_tap in range(3) for y_tap in range(3) for x_tap in range(3)]).reshape(54, NY * NX)
        first_layer = jnp.dot(first_weight.T, columns, preferred_element_type=jnp.float32)
        first_layer = jax.nn.relu(first_layer + first_bias[:, None]).astype(jnp.bfloat16)
        second_layer = jnp.dot(middle_weight.T, first_layer, preferred_element_type=jnp.float32)
        second_layer = jax.nn.relu(second_layer + middle_bias[:, None]).astype(jnp.bfloat16)
        inside = jnp.logical_and(plane_index >= 1, plane_index <= NZ)
        return jnp.where(inside, second_layer, jnp.zeros_like(second_layer))

    def plane_output(previous, current, following, field_plane):
        raw_affine = jnp.zeros((4, NY, NX), jnp.float32)
        for z_tap, hidden_now in enumerate((previous, current, following)):
            projected = jnp.dot(output_weight[36 * z_tap:36 * (z_tap + 1)], hidden_now, preferred_element_type=jnp.float32)
            projected = jnp.pad(projected.reshape(3, 3, 4, NY, NX), ((0, 0), (0, 0), (0, 0), (1, 1), (1, 1)))
            for y_tap in range(3):
                for x_tap in range(3):
                    raw_affine = raw_affine + projected[y_tap, x_tap, :, y_tap:y_tap + NY, x_tap:x_tap + NX]
        raw_affine = raw_affine + output_bias[:, None, None]
        log_first = jnp.tanh(raw_affine[0:2])
        upper_half = field_plane[2:4] * jnp.exp(log_first) + raw_affine[2:4]
        return (upper_half, jnp.sum(log_first))

    def advance(carried, inputs):
        previous, current = carried
        plane_index, field_plane = inputs
        following = hidden_plane(plane_index + 2)
        upper_half, plane_total = plane_output(previous, current, following, field_plane)
        return ((current, following), (upper_half, plane_total))
    start_pair = (jnp.zeros((H, NY * NX), jnp.bfloat16), hidden_plane(jnp.int32(1)))
    planes_first = jnp.transpose(density_field, (1, 0, 2, 3))
    final_carry, (uppers, plane_totals) = lax.scan(advance, start_pair, (jnp.arange(NZ, dtype=jnp.int32), planes_first))
    coupled = jnp.concatenate([density_field[0:2], jnp.transpose(uppers, (1, 0, 2, 3))], axis=0)
    half_z, half_y, half_x = (NZ // 2, NY // 2, NX // 2)
    squeezed = coupled.reshape(4, half_z, 2, half_y, 2, half_x, 2).transpose(2, 4, 6, 0, 1, 3, 5).reshape(32, half_z, half_y, half_x)
    factored = squeezed[0:16]
    source = squeezed[16:24]
    target = squeezed[24:32]
    spectrum = jnp.fft.fftn(source, axes=(1, 2, 3))
    freq_z = signed_freq(jnp.arange(half_z, dtype=jnp.int32), half_z)
    freq_y = signed_freq(jnp.arange(half_y, dtype=jnp.int32), half_y)
    freq_x = signed_freq(jnp.arange(half_x, dtype=jnp.int32), half_x)
    kappa_norm = jnp.sqrt(freq_z[:, None, None] ** 2 + freq_y[None, :, None] ** 2 + freq_x[None, None, :] ** 2) * (2.0 / math.sqrt(3.0))
    basis_values = radial_basis(kappa_norm, BASIS)

    def mix_output(weights):
        profile = jnp.einsum('cj,jabd->cabd', weights, basis_values, precision=precise)
        return lax.optimization_barrier(jnp.sum(profile * spectrum, axis=0))
    mixed_modes = lax.map(mix_output, radial_weights)
    shifts = jnp.real(jnp.fft.ifftn(mixed_modes, axes=(1, 2, 3))).astype(jnp.float32)
    log_second = jnp.tanh(shifts[0:8])
    latent = jnp.concatenate([source, target * jnp.exp(log_second) + shifts[8:16]], axis=0)
    whole_sum = jnp.sum(plane_totals) + jnp.sum(log_second) - 0.5 * jnp.sum(factored * factored) - 0.5 * jnp.sum(latent * latent)
    log_density = whole_sum / (4.0 * NZ * NY * NX) - 0.5 * math.log(2.0 * math.pi)
    return (factored, latent, log_density)
```

```python
import functools
import math

import jax
import jax.numpy as jnp
import ml_dtypes
import numpy as np
from jax import lax
from jax.experimental import pallas as pl
from jax.experimental.pallas import tpu as pltpu
from jax.sharding import PartitionSpec as P

MESH = pl.DeviceIdType.MESH
F32 = jnp.float32
BF16 = jnp.bfloat16

SLOTS = 40
ROWS = 64
WIDE = 256
GZ = 32
GY = 4
OWN_ROWS = ROWS + 2


def real_basis(length):
    cells = np.arange(length)
    rows = [np.full(length, 1.0 / math.sqrt(length))]
    for m in range(1, length // 2):
        rows.append(math.sqrt(2.0 / length) * np.cos(2.0 * math.pi * m * cells / length))
        rows.append(math.sqrt(2.0 / length) * np.sin(2.0 * math.pi * m * cells / length))
    rows.append(np.where(cells % 2 == 0, 1.0, -1.0) / math.sqrt(length))
    return np.stack(rows)


def split_pair(table):
    table = np.asarray(table, np.float32)
    high = table.astype(ml_dtypes.bfloat16)
    low = (table - high.astype(np.float32)).astype(ml_dtypes.bfloat16)
    return np.stack([high, low])


def tables():
    fx, fy, fz = real_basis(128), real_basis(128), real_basis(32)
    forward_x = np.zeros((128, 2, 128, 2))
    for k in range(2):
        forward_x[:, k, :, k] = fx
    forward_x = forward_x.reshape(256, 256)
    forward_z = np.einsum("kz,qp->qkzp", fz, np.eye(8)).reshape(256, 256)
    forward_y = np.einsum("kgy,cd->gcydk", fy.reshape(128, 4, 32), np.eye(4)).reshape(512, 512)
    spread = np.zeros((128, 2, 2, 128))
    for k in range(2):
        spread[np.arange(128), k, k, np.arange(128)] = 1.0
    spread = spread.reshape(256, 256).astype(ml_dtypes.bfloat16)
    pick = np.zeros((64, 4, 128))
    for plane in range(4):
        for c in range(2):
            for a in range(3):
                for b in range(3):
                    for e in range(3):
                        row = 27 * c + 9 * a + 3 * b + e
                        pick[row, plane, b * SLOTS + e * 12 + (a + plane) * 2 + c] = 1.0
        for piece in range(3):
            pick[54 + piece, plane, piece * SLOTS + 36] = 1.0
    pick = pick.reshape(64, 512).astype(ml_dtypes.bfloat16)
    half_z = (np.arange(32) + 1) // 2 / 32.0
    half_y = (np.arange(128) + 1) // 2 / 128.0
    squares = (half_z[:, None] ** 2 + half_y[None, :] ** 2).reshape(1, 4096).astype(np.float32)
    return {
        "forward_x": split_pair(forward_x),
        "forward_z": split_pair(forward_z),
        "backward_z": split_pair(forward_z.T),
        "forward_y": split_pair(forward_y),
        "backward_x": split_pair(fx.T),
        "spread": spread,
        "pick": pick,
        "squares": squares,
    }


def split2(values):
    high = values.astype(BF16)
    return high, (values - high.astype(F32)).astype(BF16)


def split3(values):
    high = values.astype(BF16)
    rest = values - high.astype(F32)
    mid = rest.astype(BF16)
    return high, mid, (rest - mid.astype(F32)).astype(BF16)


def mul(a, b, dims=((1,), (0,))):
    return lax.dot_general(a, b, (dims, ((), ())), preferred_element_type=F32)


def mul3(a, b, dims=((1,), (0,))):
    return mul(a[0], b[0], dims) + (mul(a[0], b[1], dims) + mul(a[1], b[0], dims))


def shift_right(values):
    lane = lax.broadcasted_iota(jnp.int32, values.shape, values.ndim - 1)
    return jnp.where(lane == 0, 0.0, pltpu.roll(values, 1, values.ndim - 1))


def shift_left(values):
    last = values.shape[-1] - 1
    lane = lax.broadcasted_iota(jnp.int32, values.shape, values.ndim - 1)
    return jnp.where(lane == last, 0.0, pltpu.roll(values, last, values.ndim - 1))


def flow_kernel(
    dens, first_w, first_b, middle_w, middle_b, output_w, output_b, radial,
    forward_x, forward_z, backward_z, forward_y, backward_x, spread, pick, squares,
    factored, latent, log_density,
    lower_send, edge_send, lower_prev, lower_next, edge_recv,
    window, hidden, acc0, acc1, wide_w, w1, w2, b2, w3, ow32, profile,
    x_send, z_recv, z_send, y_recv, mixed, y_send, yb_recv, zb_send, x_recv, flat,
    kept, sum_send, sum_gz, sum_gy, dens2,
    halo_ssem, halo_rsem, gz_ssem, gz_rsem, gy_ssem, gy_rsem,
):
    me_z = lax.axis_index("gz")
    me_y = lax.axis_index("gy")

    def near_z(step):
        return lax.rem(me_z + step + GZ, GZ)

    def near_y(step):
        return lax.rem(me_y + step + GY, GY)

    barrier = pltpu.get_barrier_semaphore()

    def greet_z(i, carry):
        pl.semaphore_signal(barrier, inc=1, device_id=(near_z(i), me_y), device_id_type=MESH)
        return carry

    lax.fori_loop(1, GZ, greet_z, 0)
    for i in range(1, GY):
        pl.semaphore_signal(barrier, inc=1, device_id=(me_z, near_y(i)), device_id_type=MESH)
    for dz in (-1, 1):
        for dy in (-1, 1):
            pl.semaphore_signal(
                barrier, inc=1, device_id=(near_z(dz), near_y(dy)), device_id_type=MESH
            )

    for z in range(2):
        for c in range(2):
            lower_send[z, c] = dens[c, z].astype(BF16)
    for side in range(2):
        for row in range(2):
            for z in range(2):
                for c in range(2):
                    source_row = row if side == 0 else ROWS - 2 + row
                    line = dens[c, z, pl.ds(source_row, 1), :]
                    edge_send[side, pl.ds(row * 4 + z * 2 + c, 1), :] = line.astype(BF16).astype(F32)

    pl.semaphore_wait(barrier, (GZ - 1) + (GY - 1) + 4)

    halo = []

    def send_halo(src, dst, index, to):
        copy = pltpu.make_async_remote_copy(
            src_ref=src, dst_ref=dst, send_sem=halo_ssem.at[index], recv_sem=halo_rsem.at[index],
            device_id=to, device_id_type=MESH,
        )
        copy.start()
        halo.append(copy)

    send_halo(lower_send.at[1], lower_prev.at[1], 0, (near_z(1), me_y))
    send_halo(lower_send.at[0], lower_next.at[0], 1, (near_z(-1), me_y))
    send_halo(lower_send.at[1], lower_next.at[1], 2, (near_z(-1), me_y))
    send_halo(lower_send.at[0], lower_prev.at[0], 3, (near_z(1), me_y))
    index = 4
    for side in range(2):
        to_y = near_y(-1) if side == 0 else near_y(1)
        for dz in (-1, 0, 1):
            send_halo(
                edge_send.at[side], edge_recv.at[1 - side, 1 - dz], index, (near_z(dz), to_y)
            )
            index += 1

    for half in range(2):
        dens2[half] = dens[:, :, :, pl.ds(half * 128, 128)]

    wide_w[...] = jnp.zeros_like(wide_w)
    wide_w[pl.ds(0, 54), :] = first_w[...].astype(F32)
    for piece, part in enumerate(split3(first_b[...])):
        wide_w[pl.ds(54 + piece, 1), :] = part.astype(F32)
    turned = jnp.transpose(wide_w[...]).astype(BF16)
    for plane in range(4):
        w1[pl.ds(plane * 128, 128), :] = mul(
            turned, pick[:, pl.ds(plane * 128, 128)]
        ).astype(BF16)
    w2[...] = jnp.transpose(middle_w[...].astype(F32)).astype(BF16)
    b2[...] = jnp.transpose(jnp.broadcast_to(middle_b[...], (128, 128)))
    ow32[...] = output_w[...].astype(F32)
    w3[...] = jnp.zeros_like(w3)
    for a in range(3):
        for b in range(3):
            w3[pl.ds(b * 16, 12), pl.ds(a * 128, 128)] = ow32[pl.ds(36 * a + 12 * b, 12), :]

    step_x = (me_z * 4 + me_y + 1) // 2
    freq_x = step_x.astype(F32) * (1.0 / 128.0)
    weights = radial[...]
    centres = lax.broadcasted_iota(jnp.int32, (32, 512), 0).astype(F32)

    def filter_part(part, carry):
        lanes = pl.ds(pl.multiple_of(part * 512, 512), 512)
        kappa = jnp.sqrt(squares[:, lanes] + freq_x * freq_x) * (2.0 / math.sqrt(3.0))
        scaled = kappa * 31.0 - centres
        basis = jnp.exp(-scaled * scaled)
        values = mul3(split2(weights), split2(basis))
        for j in range(4):
            profile[pl.ds(part * 4 + j, 128, stride=32), :] = values[:, j * 128 : (j + 1) * 128]
        return carry

    lax.fori_loop(0, 8, filter_part, 0)

    def put(first, count, slot, values):
        for e, shifted in enumerate((shift_right(values), values, shift_left(values))):
            for half in range(2):
                window[half, pl.ds(first * SLOTS + e * 12 + slot, count, stride=SLOTS), :] = shifted[
                    :, half * 128 : (half + 1) * 128
                ]

    for half in range(2):
        window[half, pl.ds(36, 72, stride=SLOTS), :] = jnp.ones((72, 128), F32)
        for slot in range(37, 40):
            window[half, pl.ds(slot, 72, stride=SLOTS), :] = jnp.zeros((72, 128), F32)
        window[half, pl.ds(68 * SLOTS, 36), :] = jnp.zeros((36, 128), F32)
    for z in range(2):
        for c in range(2):
            put(2, ROWS, (z + 2) * 2 + c, dens[c, z].astype(BF16).astype(F32))

    for copy in halo:
        copy.wait()

    has_prev = me_z > 0
    has_next = me_z < GZ - 1
    has_up = me_y > 0
    has_down = me_y < GY - 1
    for z in range(2):
        for c in range(2):
            put(2, ROWS, z * 2 + c, jnp.where(has_prev, lower_prev[z, c].astype(F32), 0.0))
            put(2, ROWS, (z + 4) * 2 + c, jnp.where(has_next, lower_next[z, c].astype(F32), 0.0))
    for side in range(2):
        for offset in range(3):
            valid = has_up if side == 0 else has_down
            if offset == 0:
                valid = jnp.logical_and(valid, has_prev)
            if offset == 2:
                valid = jnp.logical_and(valid, has_next)
            for row in range(2):
                lines = edge_recv[side, offset, pl.ds(row * 4, 4), :]
                lines = jnp.where(valid, lines, 0.0)
                at = (row if side == 0 else ROWS + 2 + row) * SLOTS + offset * 4
                for e, shifted in enumerate((shift_right(lines), lines, shift_left(lines))):
                    for half in range(2):
                        window[half, pl.ds(at + e * 12, 4), :] = shifted[
                            :, half * 128 : (half + 1) * 128
                        ]

    w3_lane = lax.broadcasted_iota(jnp.int32, (48, 384), 1)
    w3_first = jnp.where(jnp.logical_and(w3_lane < 128, me_z == 0), 0.0, w3[...]).astype(BF16)
    w3_second = jnp.where(
        jnp.logical_and(w3_lane >= 256, me_z == GZ - 1), 0.0, w3[...]
    ).astype(BF16)

    def columns(r):
        start = pl.multiple_of((r - 1) * SLOTS, 8)
        return jnp.concatenate(
            [window[0, pl.ds(start, 128), :], window[1, pl.ds(start, 128), :]], axis=1
        ).astype(BF16)

    def second(first_layer):
        values = mul(w2[...], first_layer) + jnp.concatenate([b2[...]] * 2, axis=1)
        return jnp.maximum(values, 0.0).astype(BF16)

    def add_taps(acc, r, taps):
        valid = jnp.logical_not(
            jnp.logical_or(
                jnp.logical_and(r == 1, me_y == 0),
                jnp.logical_and(r == OWN_ROWS, me_y == GY - 1),
            )
        )
        taps = jnp.where(valid, taps, 0.0)
        for half in range(2):
            part = taps[:, half * 128 : (half + 1) * 128]
            at = [pl.ds(pl.multiple_of((r + 1 - b) * 16, 16), 16) for b in range(3)]
            acc[half, at[0], :] = part[0:16]
            acc[half, at[1], :] += part[16:32]
            acc[half, at[2], :] += part[32:48]

    for acc in (acc0, acc1):
        for half in range(2):
            acc[half, pl.ds(0, 32), :] = jnp.zeros((32, 128), F32)

    def later_planes(pair, carry):
        for sub in range(2):
            r = pair * 2 + 1 + sub
            first_layer = jnp.maximum(mul(w1[pl.ds(128, 384), :], columns(r)), 0.0).astype(BF16)
            layers = [second(first_layer[p * 128 : (p + 1) * 128]) for p in range(3)]
            stacked = jnp.concatenate(layers, axis=0)
            hidden[r] = stacked[0:256]
            add_taps(acc1, r, mul(w3_second, stacked))
        return carry

    def first_plane(pair, carry):
        for sub in range(2):
            r = pair * 2 + 1 + sub
            first_layer = jnp.maximum(mul(w1[pl.ds(0, 128), :], columns(r)), 0.0).astype(BF16)
            stacked = jnp.concatenate([second(first_layer), hidden[r]], axis=0)
            add_taps(acc0, r, mul(w3_first, stacked))
        return carry

    lax.fori_loop(0, OWN_ROWS // 2, later_planes, 0)

    def couple(acc, z, parity):
        raw = []
        for o in range(4):
            taps = [
                jnp.concatenate(
                    [
                        acc[half, pl.ds((2 + parity) * 16 + e * 4 + o, 32, stride=32), :]
                        for half in range(2)
                    ],
                    axis=1,
                )
                for e in range(3)
            ]
            raw.append(shift_right(taps[0]) + taps[1] + shift_left(taps[2]) + output_b[o])
        lines = [
            jnp.concatenate(
                [
                    dens2[half, c, z, pl.ds(parity, 32, stride=2), :]
                    for half in range(2)
                ],
                axis=1,
            )
            for c in range(4)
        ]
        scales = [jnp.tanh(raw[0]), jnp.tanh(raw[1])]
        for o in range(2):
            lines[2 + o] = lines[2 + o] * jnp.exp(scales[o]) + raw[2 + o]
        return jnp.concatenate(lines, axis=0), scales[0] + scales[1]

    def spread_x(values):
        high, mid, low = split3(values)
        return mul(high, spread[...]) + (mul(mid, spread[...]) + mul(low, spread[...]))

    def fold(values):
        rows, lanes = values.shape
        total = values[:, 0:128]
        for at in range(128, lanes, 128):
            total = total + values[:, at : at + 128]
        return jnp.sum(total.reshape(rows // 8, 8, 128), axis=0)

    source, scale_sum = couple(acc1, 1, 0)
    kept[0] = source
    total = fold(scale_sum)
    x_modes = mul3(
        (forward_x[0], forward_x[1]), split2(source), ((1,), (1,))
    )
    x_send[...] = x_modes.reshape(GZ, 8, 128)

    def send_all_gz(src, dst, stage):
        def one(i, carry):
            to = near_z(i)
            pltpu.make_async_remote_copy(
                src_ref=src.at[to], dst_ref=dst.at[me_z], send_sem=gz_ssem.at[stage], recv_sem=gz_rsem.at[stage],
                device_id=(to, me_y), device_id_type=MESH,
            ).start()
            return carry

        lax.fori_loop(1, GZ, one, 0)
        dst[me_z] = src[me_z]

    def wait_all_gz(src, dst, stage):
        copy = pltpu.make_async_remote_copy(
            src_ref=src.at[pl.ds(0, GZ - 1)], dst_ref=dst.at[pl.ds(0, GZ - 1)],
            send_sem=gz_ssem.at[stage], recv_sem=gz_rsem.at[stage],
            device_id=(near_z(1), me_y), device_id_type=MESH,
        )
        copy.wait()

    def send_all_gy(src, dst, stage):
        for i in range(1, GY):
            to = near_y(i)
            pltpu.make_async_remote_copy(
                src_ref=src.at[to], dst_ref=dst.at[me_y], send_sem=gy_ssem.at[stage], recv_sem=gy_rsem.at[stage],
                device_id=(me_z, to), device_id_type=MESH,
            ).start()
        dst[me_y] = src[me_y]

    def wait_all_gy(src, dst, stage):
        copy = pltpu.make_async_remote_copy(
            src_ref=src.at[pl.ds(0, GY - 1)], dst_ref=dst.at[pl.ds(0, GY - 1)],
            send_sem=gy_ssem.at[stage], recv_sem=gy_rsem.at[stage],
            device_id=(me_z, near_y(1)), device_id_type=MESH,
        )
        copy.wait()

    send_all_gz(x_send, z_recv, 0)
    kept[1], scale_sum = couple(acc1, 1, 1)
    total = total + fold(scale_sum)
    lax.fori_loop(0, 8, first_plane, 0)
    wait_all_gz(x_send, z_recv, 0)

    z_modes = mul3((forward_z[0], forward_z[1]), split2(z_recv[...].reshape(256, 128)))
    z_send[...] = z_modes.reshape(GY, 64, 128)
    send_all_gy(z_send, y_recv, 0)
    lax.fori_loop(8, 16, first_plane, 0)
    wait_all_gy(z_send, y_recv, 0)

    lines = jnp.concatenate([y_recv[g] for g in range(GY)], axis=1)
    modes = mul3(split2(lines), (forward_y[0], forward_y[1]))
    parts = [
        modes[k * 32 : (k + 1) * 32, c * 128 : (c + 1) * 128] for k in range(2) for c in range(4)
    ]
    for o in range(16):
        value = profile[pl.ds(o * 256, 32), :] * parts[0]
        for c in range(1, 8):
            value = value + profile[pl.ds(o * 256 + c * 32, 32), :] * parts[c]
        mixed[pl.ds((o // 4) * 32, 32), pl.ds((o % 4) * 128, 128)] = value
    back = mul3(split2(mixed[...]), (forward_y[0], forward_y[1]), ((1,), (1,)))
    for g in range(GY):
        y_send[g] = back[:, g * 128 : (g + 1) * 128]
    send_all_gy(y_send, yb_recv, 1)
    lax.fori_loop(16, 24, first_plane, 0)
    wait_all_gy(y_send, yb_recv, 1)

    for pair in range(2):
        lines = yb_recv[pl.ds(pair * 2, 2)].reshape(256, 128)
        planes = mul3((backward_z[0], backward_z[1]), split2(lines))
        zb_send[:, pl.ds(pair * 8, 8), :] = planes.reshape(GZ, 8, 128)
    send_all_gz(zb_send, x_recv, 1)

    lax.fori_loop(24, OWN_ROWS // 2, first_plane, 0)
    squares_sum = jnp.zeros((8, 128), F32)
    for parity in range(2):
        coupled, scale_sum = couple(acc0, 0, parity)
        total = total + fold(scale_sum)
        squares_sum = squares_sum + fold(coupled * coupled)
        coupled = spread_x(coupled)
        for k in range(2):
            at = (2 * parity + k) * 4
            factored[pl.ds(at, 4), 0] = coupled[:, k * 128 : (k + 1) * 128].reshape(4, 32, 128)
    source = spread_x(kept[0])
    squares_sum = squares_sum + fold(source * source)
    for k in range(2):
        latent[pl.ds(k * 4, 4), 0] = source[:, k * 128 : (k + 1) * 128].reshape(4, 32, 128)
    target = spread_x(kept[1])
    wait_all_gz(zb_send, x_recv, 1)

    flat[...] = x_recv[...].reshape(512, 128)
    shifts = []
    for og in range(4):
        lines = flat[pl.ds(og, 128, stride=4), :]
        shifts.append(jnp.transpose(mul3((backward_x[0], backward_x[1]), split2(lines))))
    for k in range(2):
        scale = jnp.tanh(shifts[k])
        total = total + fold(scale)
        moved = target[:, k * 128 : (k + 1) * 128] * jnp.exp(scale) + shifts[2 + k]
        squares_sum = squares_sum + fold(moved * moved)
        latent[pl.ds(8 + k * 4, 4), 0] = moved.reshape(4, 32, 128)

    total = total - 0.5 * squares_sum
    sum_send[...] = jnp.broadcast_to(total[None], sum_send.shape)
    send_all_gz(sum_send, sum_gz, 2)
    wait_all_gz(sum_send, sum_gz, 2)
    total = jnp.sum(sum_gz[...], axis=0)
    sum_send[pl.ds(0, GY)] = jnp.broadcast_to(total[None], (GY, 8, 128))
    send_all_gy(sum_send, sum_gy, 2)
    wait_all_gy(sum_send, sum_gy, 2)
    total = jnp.sum(sum_gy[...], axis=0)
    count = 4.0 * 64 * 256 * 256
    log_density[0, 0] = jnp.sum(total) / count - 0.5 * math.log(2.0 * math.pi)


def shards(consts, density_field, first_weight, first_bias, middle_weight, middle_bias, output_weight, output_bias, radial_weights):
    vmem = pl.BlockSpec(memory_space=pltpu.VMEM)
    smem = pl.BlockSpec(memory_space=pltpu.SMEM)
    operands = [
        density_field, first_weight, first_bias.reshape(1, 128), middle_weight,
        middle_bias.reshape(1, 128), output_weight, output_bias, radial_weights.reshape(128, 32),
    ] + [jnp.asarray(value) for value in consts.values()]
    specs = [vmem] * len(operands)
    specs[6] = smem
    buffers = [
        pltpu.VMEM((2, 2, ROWS, WIDE), BF16),
        pltpu.VMEM((2, 8, WIDE), F32),
        pltpu.VMEM((2, 2, ROWS, WIDE), BF16),
        pltpu.VMEM((2, 2, ROWS, WIDE), BF16),
        pltpu.VMEM((2, 3, 8, WIDE), F32),
        pltpu.VMEM((2, 72 * SLOTS, 128), F32),
        pltpu.VMEM((OWN_ROWS + 2, 256, WIDE), BF16),
        pltpu.VMEM((2, 70 * 16, 128), F32),
        pltpu.VMEM((2, 70 * 16, 128), F32),
        pltpu.VMEM((64, 128), F32),
        pltpu.VMEM((512, 128), BF16),
        pltpu.VMEM((128, 128), BF16),
        pltpu.VMEM((128, 128), F32),
        pltpu.VMEM((48, 384), F32),
        pltpu.VMEM((108, 128), F32),
        pltpu.VMEM((128 * 32, 128), F32),
        pltpu.VMEM((GZ, 8, 128), F32),
        pltpu.VMEM((GZ, 8, 128), F32),
        pltpu.VMEM((GY, 64, 128), F32),
        pltpu.VMEM((GY, 64, 128), F32),
        pltpu.VMEM((128, 512), F32),
        pltpu.VMEM((GY, 128, 128), F32),
        pltpu.VMEM((GY, 128, 128), F32),
        pltpu.VMEM((GZ, 16, 128), F32),
        pltpu.VMEM((GZ, 16, 128), F32),
        pltpu.VMEM((512, 128), F32),
        pltpu.VMEM((2, 128, WIDE), F32),
        pltpu.VMEM((GZ, 8, 128), F32),
        pltpu.VMEM((GZ, 8, 128), F32),
        pltpu.VMEM((GY, 8, 128), F32),
        pltpu.VMEM((2, 4, 2, ROWS, 128), F32),
        pltpu.SemaphoreType.DMA((10,)),
        pltpu.SemaphoreType.DMA((10,)),
        pltpu.SemaphoreType.DMA((3,)),
        pltpu.SemaphoreType.DMA((3,)),
        pltpu.SemaphoreType.DMA((3,)),
        pltpu.SemaphoreType.DMA((3,)),
    ]
    factored, latent, log_density = pl.pallas_call(
        flow_kernel,
        out_shape=(
            jax.ShapeDtypeStruct((16, 1, 32, 128), F32),
            jax.ShapeDtypeStruct((16, 1, 32, 128), F32),
            jax.ShapeDtypeStruct((1, 1), F32),
        ),
        in_specs=specs,
        out_specs=(vmem, vmem, smem),
        scratch_shapes=buffers,
        compiler_params=pltpu.CompilerParams(
            collective_id=0, has_side_effects=True, vmem_limit_bytes=48 * 1024 * 1024
        ),
        name="flow",
    )(*operands)
    return factored, latent, log_density.reshape(())


def solution(mesh):
    assert mesh.shape["gz"] == GZ and mesh.shape["gy"] == GY
    in_specs = (P(None, "gz", "gy", None), P(), P(), P(), P(), P(), P(), P())
    out_specs = (P(None, "gz", "gy", None), P(None, "gz", "gy", None), P())
    return jax.shard_map(
        functools.partial(shards, tables()),
        mesh=mesh, in_specs=in_specs, out_specs=out_specs, check_vma=False,
    )
```

```python
import functools
import math

import jax
import jax.numpy as jnp
import ml_dtypes
import numpy as np
from jax import lax
from jax.experimental import pallas as pl
from jax.experimental.pallas import tpu as pltpu
from jax.sharding import PartitionSpec as P

MESH = pl.DeviceIdType.MESH
F32 = jnp.float32
BF16 = jnp.bfloat16

SLOTS = 40
ROWS = 64
WIDE = 256
GZ = 32
GY = 4
OWN_ROWS = ROWS + 2
GROUP = 6
GROUPS = OWN_ROWS // GROUP


def real_basis(length):
    cells = np.arange(length)
    rows = [np.full(length, 1.0 / math.sqrt(length))]
    for m in range(1, length // 2):
        rows.append(math.sqrt(2.0 / length) * np.cos(2.0 * math.pi * m * cells / length))
        rows.append(math.sqrt(2.0 / length) * np.sin(2.0 * math.pi * m * cells / length))
    rows.append(np.where(cells % 2 == 0, 1.0, -1.0) / math.sqrt(length))
    return np.stack(rows)


def split_pair(table):
    table = np.asarray(table, np.float32)
    high = table.astype(ml_dtypes.bfloat16)
    low = (table - high.astype(np.float32)).astype(ml_dtypes.bfloat16)
    return np.stack([high, low])


def tables():
    fx, fy, fz = real_basis(128), real_basis(128), real_basis(32)
    forward_x = np.zeros((128, 2, 128, 2))
    for k in range(2):
        forward_x[:, k, :, k] = fx
    forward_x = forward_x.reshape(256, 256)
    forward_z = np.einsum("kz,qp->qkzp", fz, np.eye(8)).reshape(256, 256)
    forward_y = np.einsum("kgy,cd->gcydk", fy.reshape(128, 4, 32), np.eye(4)).reshape(512, 512)
    spread = np.zeros((128, 2, 2, 128))
    for k in range(2):
        spread[np.arange(128), k, k, np.arange(128)] = 1.0
    spread = spread.reshape(256, 256).astype(ml_dtypes.bfloat16)
    pick = np.zeros((64, 4, 128))
    for plane in range(4):
        for c in range(2):
            for a in range(3):
                for b in range(3):
                    for e in range(3):
                        row = 27 * c + 9 * a + 3 * b + e
                        pick[row, plane, b * SLOTS + e * 12 + (a + plane) * 2 + c] = 1.0
        for piece in range(3):
            pick[54 + piece, plane, piece * SLOTS + 36] = 1.0
    pick = pick.reshape(64, 512).astype(ml_dtypes.bfloat16)
    half_z = (np.arange(32) + 1) // 2 / 32.0
    half_y = (np.arange(128) + 1) // 2 / 128.0
    squares = (half_z[:, None] ** 2 + half_y[None, :] ** 2).reshape(1, 4096).astype(np.float32)
    return {
        "forward_x": split_pair(forward_x),
        "forward_z": split_pair(forward_z),
        "backward_z": split_pair(forward_z.T),
        "forward_y": split_pair(forward_y),
        "backward_x": split_pair(fx.T),
        "spread": spread,
        "pick": pick,
        "squares": squares,
    }


def split2(values):
    high = values.astype(BF16)
    return high, (values - high.astype(F32)).astype(BF16)


def split3(values):
    high = values.astype(BF16)
    rest = values - high.astype(F32)
    mid = rest.astype(BF16)
    return high, mid, (rest - mid.astype(F32)).astype(BF16)


def mul(a, b, dims=((1,), (0,))):
    return lax.dot_general(a, b, (dims, ((), ())), preferred_element_type=F32)


def mul3(a, b, dims=((1,), (0,))):
    return mul(a[0], b[0], dims) + (mul(a[0], b[1], dims) + mul(a[1], b[0], dims))


def shift_right(values):
    lane = lax.broadcasted_iota(jnp.int32, values.shape, values.ndim - 1)
    return jnp.where(lane == 0, 0.0, pltpu.roll(values, 1, values.ndim - 1))


def shift_left(values):
    last = values.shape[-1] - 1
    lane = lax.broadcasted_iota(jnp.int32, values.shape, values.ndim - 1)
    return jnp.where(lane == last, 0.0, pltpu.roll(values, last, values.ndim - 1))


def flow_kernel(
    dens_hbm, first_w_hbm, first_b_hbm, middle_w_hbm, middle_b_hbm, output_w_hbm, output_b_hbm,
    radial_hbm, forward_x_hbm, forward_z_hbm, backward_z_hbm, forward_y_hbm, backward_x_hbm,
    spread_hbm, pick_hbm, squares_hbm,
    factored, latent, log_density,
    lower_send, edge_send, lower_prev, lower_next, edge_recv,
    window, hidden, acc0, acc1, wide_w, w1, w2, b2, w3, ow32, profile,
    x_send, z_recv, z_send, y_recv, mixed, y_send, yb_recv, zb_send, x_recv, flat,
    kept, first_held, last_held, sum_send, sum_send2, sum_gz, sum_gy, dens2,
    first_w, first_b, middle_w, middle_b, output_w, output_b,
    radial, forward_x, forward_z, backward_z, forward_y, backward_x, spread, pick, squares,
    halo_ssem, halo_rsem, gz_ssem, gz_rsem, gy_ssem, gy_rsem, in_sem,
):
    me_z = lax.axis_index("gz")
    me_y = lax.axis_index("gy")

    def near_z(step):
        return lax.rem(me_z + step + GZ, GZ)

    def near_y(step):
        return lax.rem(me_y + step + GY, GY)

    def fetch(src, dst, index):
        copy = pltpu.make_async_copy(src, dst, in_sem.at[index])
        copy.start()
        return copy

    lower_in = [
        fetch(
            dens_hbm.at[pl.ds(0, 2), :, :, pl.ds(half * 128, 128)],
            dens2.at[half, pl.ds(0, 2)], half,
        )
        for half in range(2)
    ]
    weights_in = [
        fetch(src, dst, 2 + i)
        for i, (src, dst) in enumerate(
            (
                (first_w_hbm, first_w), (first_b_hbm, first_b), (pick_hbm, pick),
                (middle_w_hbm, middle_w), (middle_b_hbm, middle_b), (output_w_hbm, output_w),
            )
        )
    ]
    filter_in = [fetch(radial_hbm, radial, 8), fetch(squares_hbm, squares, 9)]
    late_in = [
        fetch(
            dens_hbm.at[pl.ds(2, 2), :, :, pl.ds(half * 128, 128)],
            dens2.at[half, pl.ds(2, 2)], 10 + half,
        )
        for half in range(2)
    ] + [
        fetch(src, dst, 12 + i)
        for i, (src, dst) in enumerate(
            (
                (output_b_hbm, output_b), (forward_x_hbm, forward_x), (forward_z_hbm, forward_z),
                (forward_y_hbm, forward_y), (backward_z_hbm, backward_z),
                (backward_x_hbm, backward_x), (spread_hbm, spread),
            )
        )
    ]

    barrier = pltpu.get_barrier_semaphore()

    def greet_z(i, carry):
        pl.semaphore_signal(barrier, inc=1, device_id=(near_z(i), me_y), device_id_type=MESH)
        return carry

    lax.fori_loop(1, GZ, greet_z, 0)
    for i in range(1, GY):
        pl.semaphore_signal(barrier, inc=1, device_id=(me_z, near_y(i)), device_id_type=MESH)
    for dz in (-1, 1):
        for dy in (-1, 1):
            pl.semaphore_signal(
                barrier, inc=1, device_id=(near_z(dz), near_y(dy)), device_id_type=MESH
            )

    for copy in lower_in:
        copy.wait()
    for z in range(2):
        for c in range(2):
            for half in range(2):
                lower_send[z, c, :, pl.ds(half * 128, 128)] = dens2[half, c, z].astype(BF16)
    for side in range(2):
        for row in range(2):
            for z in range(2):
                for c in range(2):
                    source_row = row if side == 0 else ROWS - 2 + row
                    for half in range(2):
                        line = dens2[half, c, z, pl.ds(source_row, 1), :]
                        edge_send[
                            side, pl.ds(row * 4 + z * 2 + c, 1), pl.ds(half * 128, 128)
                        ] = line.astype(BF16).astype(F32)

    pl.semaphore_wait(barrier, (GZ - 1) + (GY - 1) + 4)

    halo = []

    def send_halo(src, dst, index, to):
        copy = pltpu.make_async_remote_copy(
            src_ref=src, dst_ref=dst, send_sem=halo_ssem.at[index], recv_sem=halo_rsem.at[index],
            device_id=to, device_id_type=MESH,
        )
        copy.start()
        halo.append(copy)

    send_halo(lower_send.at[1], lower_prev.at[1], 0, (near_z(1), me_y))
    send_halo(lower_send.at[0], lower_next.at[0], 1, (near_z(-1), me_y))
    send_halo(lower_send.at[1], lower_next.at[1], 2, (near_z(-1), me_y))
    send_halo(lower_send.at[0], lower_prev.at[0], 3, (near_z(1), me_y))
    index = 4
    for side in range(2):
        to_y = near_y(-1) if side == 0 else near_y(1)
        for dz in (-1, 0, 1):
            send_halo(
                edge_send.at[side], edge_recv.at[1 - side, 1 - dz], index, (near_z(dz), to_y)
            )
            index += 1

    for copy in weights_in:
        copy.wait()
    wide_w[...] = jnp.zeros_like(wide_w)
    wide_w[pl.ds(0, 54), :] = first_w[...].astype(F32)
    for piece, part in enumerate(split3(first_b[...])):
        wide_w[pl.ds(54 + piece, 1), :] = part.astype(F32)
    turned = jnp.transpose(wide_w[...]).astype(BF16)
    for plane in range(4):
        w1[pl.ds(plane * 128, 128), :] = mul(
            turned, pick[:, pl.ds(plane * 128, 128)]
        ).astype(BF16)
    w2[...] = jnp.transpose(middle_w[...].astype(F32)).astype(BF16)
    b2[...] = jnp.transpose(jnp.broadcast_to(middle_b[...], (128, 128)))
    ow32[...] = output_w[...].astype(F32)
    w3[...] = jnp.zeros_like(w3)
    for a in range(3):
        for b in range(3):
            w3[pl.ds(b * 16, 12), pl.ds(a * 128, 128)] = ow32[pl.ds(36 * a + 12 * b, 12), :]

    def put(first, count, slot, values):
        for e, shifted in enumerate((shift_right(values), values, shift_left(values))):
            for half in range(2):
                window[half, pl.ds(first * SLOTS + e * 12 + slot, count, stride=SLOTS), :] = shifted[
                    :, half * 128 : (half + 1) * 128
                ]

    for half in range(2):
        window[half, pl.ds(36, 72, stride=SLOTS), :] = jnp.ones((72, 128), F32)
        for slot in range(37, 40):
            window[half, pl.ds(slot, 72, stride=SLOTS), :] = jnp.zeros((72, 128), F32)
        window[half, pl.ds(68 * SLOTS, 36), :] = jnp.zeros((36, 128), F32)
    for z in range(2):
        for c in range(2):
            put(2, ROWS, (z + 2) * 2 + c, lower_send[z, c].astype(F32))

    for copy in late_in:
        copy.wait()
    for copy in halo:
        copy.wait_recv()
    for copy in halo:
        copy.wait_send()

    has_prev = me_z > 0
    has_next = me_z < GZ - 1
    has_up = me_y > 0
    has_down = me_y < GY - 1
    for z in range(2):
        for c in range(2):
            put(2, ROWS, z * 2 + c, jnp.where(has_prev, lower_prev[z, c].astype(F32), 0.0))
            put(2, ROWS, (z + 4) * 2 + c, jnp.where(has_next, lower_next[z, c].astype(F32), 0.0))
    for side in range(2):
        for offset in range(3):
            valid = has_up if side == 0 else has_down
            if offset == 0:
                valid = jnp.logical_and(valid, has_prev)
            if offset == 2:
                valid = jnp.logical_and(valid, has_next)
            for row in range(2):
                lines = edge_recv[side, offset, pl.ds(row * 4, 4), :]
                lines = jnp.where(valid, lines, 0.0)
                at = (row if side == 0 else ROWS + 2 + row) * SLOTS + offset * 4
                for e, shifted in enumerate((shift_right(lines), lines, shift_left(lines))):
                    for half in range(2):
                        window[half, pl.ds(at + e * 12, 4), :] = shifted[
                            :, half * 128 : (half + 1) * 128
                        ]

    w3_lane = lax.broadcasted_iota(jnp.int32, (48, 384), 1)
    w3_first = jnp.where(jnp.logical_and(w3_lane < 128, me_z == 0), 0.0, w3[...]).astype(BF16)
    w3_second = jnp.where(
        jnp.logical_and(w3_lane >= 256, me_z == GZ - 1), 0.0, w3[...]
    ).astype(BF16)

    def columns(r):
        start = pl.multiple_of((r - 1) * SLOTS, 8)
        return jnp.concatenate(
            [window[0, pl.ds(start, 128), :], window[1, pl.ds(start, 128), :]], axis=1
        ).astype(BF16)

    def second(first_layer):
        values = mul(w2[...], first_layer) + jnp.concatenate([b2[...]] * 2, axis=1)
        return jnp.maximum(values, 0.0).astype(BF16)

    def add_taps(acc, r, taps):
        valid = jnp.logical_not(
            jnp.logical_or(
                jnp.logical_and(r == 1, me_y == 0),
                jnp.logical_and(r == OWN_ROWS, me_y == GY - 1),
            )
        )
        taps = jnp.where(valid, taps, 0.0)
        for half in range(2):
            part = taps[:, half * 128 : (half + 1) * 128]
            at = [pl.ds(pl.multiple_of((r + 1 - b) * 16, 16), 16) for b in range(3)]
            acc[half, at[0], :] = part[0:16]
            acc[half, at[1], :] += part[16:32]
            acc[half, at[2], :] += part[32:48]

    for acc in (acc0, acc1):
        for half in range(2):
            acc[half, pl.ds(0, 32), :] = jnp.zeros((32, 128), F32)

    def group_rows(group):
        return [(sub, group * GROUP + 1 + sub) for sub in range(GROUP)]

    def later_first(group):
        for sub, r in group_rows(group):
            values = mul(w1[pl.ds(128, 384), :], columns(r))
            first_held[sub] = jnp.maximum(values, 0.0).astype(BF16)

    def later_second(group):
        for sub, r in group_rows(group):
            first_layer = first_held[sub]
            layers = [second(first_layer[p * 128 : (p + 1) * 128]) for p in range(3)]
            hidden[r] = jnp.concatenate(layers[0:2], axis=0)
            last_held[sub] = layers[2]

    def later_last(group):
        for sub, r in group_rows(group):
            stacked = jnp.concatenate([hidden[r], last_held[sub]], axis=0)
            add_taps(acc1, r, mul(w3_second, stacked))

    def early_first(group):
        for sub, r in group_rows(group):
            values = mul(w1[pl.ds(0, 128), :], columns(r))
            first_held[sub, pl.ds(0, 128)] = jnp.maximum(values, 0.0).astype(BF16)

    def early_second(group):
        for sub, r in group_rows(group):
            last_held[sub] = second(first_held[sub, pl.ds(0, 128)])

    def early_last(group):
        for sub, r in group_rows(group):
            stacked = jnp.concatenate([last_held[sub], hidden[r]], axis=0)
            add_taps(acc0, r, mul(w3_first, stacked))

    def start_groups(first, middle, last):
        first(0)
        middle(0)
        first(1)

    def run_groups(first, middle, last, begin, end):
        def step(group, carry):
            last(group - 2)
            middle(group - 1)
            first(group)
            return carry

        lax.fori_loop(begin, end, step, 0)

    def end_groups(first, middle, last):
        last(GROUPS - 2)
        middle(GROUPS - 1)
        last(GROUPS - 1)

    later = (later_first, later_second, later_last)
    early = (early_first, early_second, early_last)

    start_groups(*later)
    run_groups(*later, 2, GROUPS)
    end_groups(*later)

    def couple(acc, z, parity):
        raw = []
        for o in range(4):
            taps = [
                jnp.concatenate(
                    [
                        acc[half, pl.ds((2 + parity) * 16 + e * 4 + o, 32, stride=32), :]
                        for half in range(2)
                    ],
                    axis=1,
                )
                for e in range(3)
            ]
            raw.append(shift_right(taps[0]) + taps[1] + shift_left(taps[2]) + output_b[o])
        lines = [
            jnp.concatenate(
                [
                    dens2[half, c, z, pl.ds(parity, 32, stride=2), :]
                    for half in range(2)
                ],
                axis=1,
            )
            for c in range(4)
        ]
        scales = [jnp.tanh(raw[0]), jnp.tanh(raw[1])]
        for o in range(2):
            lines[2 + o] = lines[2 + o] * jnp.exp(scales[o]) + raw[2 + o]
        return jnp.concatenate(lines, axis=0), scales[0] + scales[1]

    def spread_x(values):
        high, mid, low = split3(values)
        return mul(high, spread[...]) + (mul(mid, spread[...]) + mul(low, spread[...]))

    def fold(values):
        rows, lanes = values.shape
        total = values[:, 0:128]
        for at in range(128, lanes, 128):
            total = total + values[:, at : at + 128]
        return jnp.sum(total.reshape(rows // 8, 8, 128), axis=0)

    def make_filter():
        step_x = (me_z * 4 + me_y + 1) // 2
        freq_x = step_x.astype(F32) * (1.0 / 128.0)
        for copy in filter_in:
            copy.wait()
        weights = radial[...]
        centres = lax.broadcasted_iota(jnp.int32, (32, 512), 0).astype(F32)

        def filter_part(part, carry):
            lanes = pl.ds(pl.multiple_of(part * 512, 512), 512)
            kappa = jnp.sqrt(squares[:, lanes] + freq_x * freq_x) * (2.0 / math.sqrt(3.0))
            scaled = kappa * 31.0 - centres
            basis = jnp.exp(-scaled * scaled)
            values = mul3(split2(weights), split2(basis))
            for j in range(4):
                profile[pl.ds(part * 4 + j, 128, stride=32), :] = values[:, j * 128 : (j + 1) * 128]
            return carry

        lax.fori_loop(0, 8, filter_part, 0)

    source, scale_sum = couple(acc1, 1, 0)
    kept[0] = source
    total = fold(scale_sum)
    x_modes = mul3(
        (forward_x[0], forward_x[1]), split2(source), ((1,), (1,))
    )
    x_send[...] = x_modes.reshape(GZ, 8, 128)

    sent = []

    def send_all_gz(src, dst, stage):
        def one(i, carry):
            to = near_z(i)
            pltpu.make_async_remote_copy(
                src_ref=src.at[to], dst_ref=dst.at[me_z], send_sem=gz_ssem.at[stage], recv_sem=gz_rsem.at[stage],
                device_id=(to, me_y), device_id_type=MESH,
            ).start()
            return carry

        lax.fori_loop(1, GZ, one, 0)
        dst[me_z] = src[me_z]

    def wait_all_gz(src, dst, stage):
        copy = pltpu.make_async_remote_copy(
            src_ref=src.at[pl.ds(0, GZ - 1)], dst_ref=dst.at[pl.ds(0, GZ - 1)],
            send_sem=gz_ssem.at[stage], recv_sem=gz_rsem.at[stage],
            device_id=(near_z(1), me_y), device_id_type=MESH,
        )
        copy.wait_recv()
        sent.append(copy)

    def send_all_gy(src, dst, stage):
        for i in range(1, GY):
            to = near_y(i)
            pltpu.make_async_remote_copy(
                src_ref=src.at[to], dst_ref=dst.at[me_y], send_sem=gy_ssem.at[stage], recv_sem=gy_rsem.at[stage],
                device_id=(me_z, to), device_id_type=MESH,
            ).start()
        dst[me_y] = src[me_y]

    def wait_all_gy(src, dst, stage):
        copy = pltpu.make_async_remote_copy(
            src_ref=src.at[pl.ds(0, GY - 1)], dst_ref=dst.at[pl.ds(0, GY - 1)],
            send_sem=gy_ssem.at[stage], recv_sem=gy_rsem.at[stage],
            device_id=(me_z, near_y(1)), device_id_type=MESH,
        )
        copy.wait_recv()
        sent.append(copy)

    send_all_gz(x_send, z_recv, 0)
    kept[1], scale_sum = couple(acc1, 1, 1)
    total = total + fold(scale_sum)
    make_filter()
    wait_all_gz(x_send, z_recv, 0)

    z_modes = mul3((forward_z[0], forward_z[1]), split2(z_recv[...].reshape(256, 128)))
    z_send[...] = z_modes.reshape(GY, 64, 128)
    send_all_gy(z_send, y_recv, 0)
    start_groups(*early)
    run_groups(*early, 2, 6)
    wait_all_gy(z_send, y_recv, 0)

    lines = jnp.concatenate([y_recv[g] for g in range(GY)], axis=1)
    modes = mul3(split2(lines), (forward_y[0], forward_y[1]))
    parts = [
        modes[k * 32 : (k + 1) * 32, c * 128 : (c + 1) * 128] for k in range(2) for c in range(4)
    ]
    for o in range(16):
        value = profile[pl.ds(o * 256, 32), :] * parts[0]
        for c in range(1, 8):
            value = value + profile[pl.ds(o * 256 + c * 32, 32), :] * parts[c]
        mixed[pl.ds((o // 4) * 32, 32), pl.ds((o % 4) * 128, 128)] = value
    back = mul3(split2(mixed[...]), (forward_y[0], forward_y[1]), ((1,), (1,)))
    for g in range(GY):
        y_send[g] = back[:, g * 128 : (g + 1) * 128]
    send_all_gy(y_send, yb_recv, 1)
    run_groups(*early, 6, GROUPS)
    end_groups(*early)
    wait_all_gy(y_send, yb_recv, 1)

    for pair in range(2):
        lines = yb_recv[pl.ds(pair * 2, 2)].reshape(256, 128)
        planes = mul3((backward_z[0], backward_z[1]), split2(lines))
        zb_send[:, pl.ds(pair * 8, 8), :] = planes.reshape(GZ, 8, 128)
    send_all_gz(zb_send, x_recv, 1)

    squares_sum = jnp.zeros((8, 128), F32)
    for parity in range(2):
        coupled, scale_sum = couple(acc0, 0, parity)
        total = total + fold(scale_sum)
        squares_sum = squares_sum + fold(coupled * coupled)
        coupled = spread_x(coupled)
        for k in range(2):
            at = (2 * parity + k) * 4
            factored[pl.ds(at, 4), 0] = coupled[:, k * 128 : (k + 1) * 128].reshape(4, 32, 128)
    source = spread_x(kept[0])
    squares_sum = squares_sum + fold(source * source)
    for k in range(2):
        latent[pl.ds(k * 4, 4), 0] = source[:, k * 128 : (k + 1) * 128].reshape(4, 32, 128)
    target = spread_x(kept[1])
    wait_all_gz(zb_send, x_recv, 1)

    flat[...] = x_recv[...].reshape(512, 128)
    shifts = []
    for og in range(4):
        lines = flat[pl.ds(og, 128, stride=4), :]
        shifts.append(jnp.transpose(mul3((backward_x[0], backward_x[1]), split2(lines))))
    for k in range(2):
        scale = jnp.tanh(shifts[k])
        total = total + fold(scale)
        moved = target[:, k * 128 : (k + 1) * 128] * jnp.exp(scale) + shifts[2 + k]
        squares_sum = squares_sum + fold(moved * moved)
        latent[pl.ds(8 + k * 4, 4), 0] = moved.reshape(4, 32, 128)

    total = total - 0.5 * squares_sum
    sum_send[...] = jnp.broadcast_to(total[None], sum_send.shape)
    send_all_gz(sum_send, sum_gz, 2)
    wait_all_gz(sum_send, sum_gz, 2)
    total = jnp.sum(sum_gz[...], axis=0)
    sum_send2[...] = jnp.broadcast_to(total[None], sum_send2.shape)
    send_all_gy(sum_send2, sum_gy, 2)
    wait_all_gy(sum_send2, sum_gy, 2)
    total = jnp.sum(sum_gy[...], axis=0)
    for copy in sent:
        copy.wait_send()
    count = 4.0 * 64 * 256 * 256
    log_density[0, 0] = jnp.sum(total) / count - 0.5 * math.log(2.0 * math.pi)


def shards(consts, density_field, first_weight, first_bias, middle_weight, middle_bias, output_weight, output_bias, radial_weights):
    vmem = pl.BlockSpec(memory_space=pltpu.VMEM)
    smem = pl.BlockSpec(memory_space=pltpu.SMEM)
    hbm = pl.BlockSpec(memory_space=pltpu.HBM)
    operands = [
        density_field, first_weight, first_bias.reshape(1, 128), middle_weight,
        middle_bias.reshape(1, 128), output_weight, output_bias, radial_weights.reshape(128, 32),
    ] + [jnp.asarray(value) for value in consts.values()]
    specs = [hbm] * len(operands)
    held = [pltpu.VMEM(value.shape, value.dtype) for value in operands]
    held[6] = pltpu.SMEM(output_bias.shape, F32)
    buffers = [
        pltpu.VMEM((2, 2, ROWS, WIDE), BF16),
        pltpu.VMEM((2, 8, WIDE), F32),
        pltpu.VMEM((2, 2, ROWS, WIDE), BF16),
        pltpu.VMEM((2, 2, ROWS, WIDE), BF16),
        pltpu.VMEM((2, 3, 8, WIDE), F32),
        pltpu.VMEM((2, 72 * SLOTS, 128), F32),
        pltpu.VMEM((OWN_ROWS + 2, 256, WIDE), BF16),
        pltpu.VMEM((2, 70 * 16, 128), F32),
        pltpu.VMEM((2, 70 * 16, 128), F32),
        pltpu.VMEM((64, 128), F32),
        pltpu.VMEM((512, 128), BF16),
        pltpu.VMEM((128, 128), BF16),
        pltpu.VMEM((128, 128), F32),
        pltpu.VMEM((48, 384), F32),
        pltpu.VMEM((108, 128), F32),
        pltpu.VMEM((128 * 32, 128), F32),
        pltpu.VMEM((GZ, 8, 128), F32),
        pltpu.VMEM((GZ, 8, 128), F32),
        pltpu.VMEM((GY, 64, 128), F32),
        pltpu.VMEM((GY, 64, 128), F32),
        pltpu.VMEM((128, 512), F32),
        pltpu.VMEM((GY, 128, 128), F32),
        pltpu.VMEM((GY, 128, 128), F32),
        pltpu.VMEM((GZ, 16, 128), F32),
        pltpu.VMEM((GZ, 16, 128), F32),
        pltpu.VMEM((512, 128), F32),
        pltpu.VMEM((2, 128, WIDE), F32),
        pltpu.VMEM((GROUP, 384, WIDE), BF16),
        pltpu.VMEM((GROUP, 128, WIDE), BF16),
        pltpu.VMEM((GZ, 8, 128), F32),
        pltpu.VMEM((GY, 8, 128), F32),
        pltpu.VMEM((GZ, 8, 128), F32),
        pltpu.VMEM((GY, 8, 128), F32),
        pltpu.VMEM((2, 4, 2, ROWS, 128), F32),
    ] + held[1:] + [
        pltpu.SemaphoreType.DMA((10,)),
        pltpu.SemaphoreType.DMA((10,)),
        pltpu.SemaphoreType.DMA((3,)),
        pltpu.SemaphoreType.DMA((3,)),
        pltpu.SemaphoreType.DMA((3,)),
        pltpu.SemaphoreType.DMA((3,)),
        pltpu.SemaphoreType.DMA((19,)),
    ]
    factored, latent, log_density = pl.pallas_call(
        flow_kernel,
        out_shape=(
            jax.ShapeDtypeStruct((16, 1, 32, 128), F32),
            jax.ShapeDtypeStruct((16, 1, 32, 128), F32),
            jax.ShapeDtypeStruct((1, 1), F32),
        ),
        in_specs=specs,
        out_specs=(vmem, vmem, smem),
        scratch_shapes=buffers,
        compiler_params=pltpu.CompilerParams(
            collective_id=0, has_side_effects=True, vmem_limit_bytes=60 * 1024 * 1024
        ),
        name="flow",
    )(*operands)
    return factored, latent, log_density.reshape(())


def solution(mesh):
    assert mesh.shape["gz"] == GZ and mesh.shape["gy"] == GY
    in_specs = (P(None, "gz", "gy", None), P(), P(), P(), P(), P(), P(), P())
    out_specs = (P(None, "gz", "gy", None), P(None, "gz", "gy", None), P())
    return jax.shard_map(
        functools.partial(shards, tables()),
        mesh=mesh, in_specs=in_specs, out_specs=out_specs, check_vma=False,
    )
```

```python
import functools
import math

import jax
import jax.numpy as jnp
import ml_dtypes
import numpy as np
from jax import lax
from jax.experimental import pallas as pl
from jax.experimental.pallas import tpu as pltpu
from jax.sharding import PartitionSpec as P

MESH = pl.DeviceIdType.MESH
LOGICAL = pl.DeviceIdType.LOGICAL
F32 = jnp.float32
BF16 = jnp.bfloat16

SLOTS = 40
ROWS = 64
WIDE = 256
GZ = 32
GY = 4
COUNT = GZ * GY
OWN_ROWS = ROWS + 2
GROUP = 6
GROUPS = OWN_ROWS // GROUP


def real_basis(length):
    cells = np.arange(length)
    rows = [np.full(length, 1.0 / math.sqrt(length))]
    for m in range(1, length // 2):
        rows.append(math.sqrt(2.0 / length) * np.cos(2.0 * math.pi * m * cells / length))
        rows.append(math.sqrt(2.0 / length) * np.sin(2.0 * math.pi * m * cells / length))
    rows.append(np.where(cells % 2 == 0, 1.0, -1.0) / math.sqrt(length))
    return np.stack(rows)


def split_pair(table):
    table = np.asarray(table, np.float32)
    high = table.astype(ml_dtypes.bfloat16)
    low = (table - high.astype(np.float32)).astype(ml_dtypes.bfloat16)
    return np.stack([high, low])


def tables():
    fx, fy, fz = real_basis(128), real_basis(128), real_basis(32)
    forward_x = np.zeros((128, 2, 128, 2))
    for k in range(2):
        forward_x[:, k, :, k] = fx
    forward_x = forward_x.reshape(256, 256)
    forward_z = np.einsum("kz,qp->qkzp", fz, np.eye(8)).reshape(256, 256)
    forward_y = np.einsum("kgy,cd->gcydk", fy.reshape(128, 4, 32), np.eye(4)).reshape(512, 512)
    spread = np.zeros((128, 2, 2, 128))
    for k in range(2):
        spread[np.arange(128), k, k, np.arange(128)] = 1.0
    spread = spread.reshape(256, 256).astype(ml_dtypes.bfloat16)
    pick = np.zeros((64, 4, 128))
    for plane in range(4):
        for c in range(2):
            for a in range(3):
                for b in range(3):
                    for e in range(3):
                        row = 27 * c + 9 * a + 3 * b + e
                        pick[row, plane, b * SLOTS + e * 12 + (a + plane) * 2 + c] = 1.0
        for piece in range(3):
            pick[54 + piece, plane, piece * SLOTS + 36] = 1.0
    pick = pick.reshape(64, 512).astype(ml_dtypes.bfloat16)
    half_z = (np.arange(32) + 1) // 2 / 32.0
    half_y = (np.arange(128) + 1) // 2 / 128.0
    squares = (half_z[:, None] ** 2 + half_y[None, :] ** 2).reshape(1, 4096).astype(np.float32)
    return {
        "forward_x": split_pair(forward_x),
        "forward_z": split_pair(forward_z),
        "backward_z": split_pair(forward_z.T),
        "forward_y": split_pair(forward_y),
        "backward_x": split_pair(fx.T),
        "spread": spread,
        "pick": pick,
        "squares": squares,
    }


def split2(values):
    high = values.astype(BF16)
    return high, (values - high.astype(F32)).astype(BF16)


def split3(values):
    high = values.astype(BF16)
    rest = values - high.astype(F32)
    mid = rest.astype(BF16)
    return high, mid, (rest - mid.astype(F32)).astype(BF16)


def mul(a, b, dims=((1,), (0,))):
    return lax.dot_general(a, b, (dims, ((), ())), preferred_element_type=F32)


def mul3(a, b, dims=((1,), (0,))):
    return mul(a[0], b[0], dims) + (mul(a[0], b[1], dims) + mul(a[1], b[0], dims))


def shift_right(values):
    lane = lax.broadcasted_iota(jnp.int32, values.shape, values.ndim - 1)
    return jnp.where(lane == 0, 0.0, pltpu.roll(values, 1, values.ndim - 1))


def shift_left(values):
    last = values.shape[-1] - 1
    lane = lax.broadcasted_iota(jnp.int32, values.shape, values.ndim - 1)
    return jnp.where(lane == last, 0.0, pltpu.roll(values, last, values.ndim - 1))


def flow_kernel(
    dens_hbm, first_w_hbm, first_b_hbm, middle_w_hbm, middle_b_hbm, output_w_hbm, output_b_hbm,
    radial_hbm, forward_x_hbm, forward_z_hbm, backward_z_hbm, forward_y_hbm, backward_x_hbm,
    spread_hbm, pick_hbm, squares_hbm,
    factored, latent, log_density,
    lower_send, edge_send, lower_prev, lower_next, edge_recv,
    window, hidden, acc0, acc1, wide_w, w1, w2, b2, w3, ow32, profile,
    x_send, z_recv, mixed, zb_send, x_recv,
    kept, first_held, last_held, sum_send, sum_recv, dens2,
    first_w, first_b, middle_w, middle_b, output_w, output_b,
    radial, forward_x, forward_z, backward_z, forward_y, backward_x, spread, pick, squares,
    halo_ssem, halo_rsem, all_ssem, all_rsem, in_sem,
):
    me_z = lax.axis_index("gz")
    me_y = lax.axis_index("gy")

    me = me_z * GY + me_y

    def near(step):
        return lax.rem(me + step, COUNT)

    def near_z(step):
        return lax.rem(me_z + step + GZ, GZ)

    def near_y(step):
        return lax.rem(me_y + step + GY, GY)

    barrier = pltpu.get_barrier_semaphore()
    sides = [(dz, dy) for dz in (-1, 0, 1) for dy in (-1, 0, 1) if (dz, dy) != (0, 0)]
    for dz, dy in sides:
        pl.semaphore_signal(
            barrier, inc=1, device_id=(near_z(dz), near_y(dy)), device_id_type=MESH
        )
    def fetch(src, dst, index):
        copy = pltpu.make_async_copy(src, dst, in_sem.at[index])
        copy.start()
        return copy

    lower_in = [
        fetch(
            dens_hbm.at[pl.ds(0, 2), :, :, pl.ds(half * 128, 128)],
            dens2.at[half, pl.ds(0, 2)], half,
        )
        for half in range(2)
    ]

    def greet(i, carry):
        pl.semaphore_signal(barrier, inc=1, device_id=near(i), device_id_type=LOGICAL)
        return carry

    lax.fori_loop(1, COUNT, greet, 0)

    for copy in lower_in:
        copy.wait()
    for z in range(2):
        for c in range(2):
            for half in range(2):
                lower_send[z, c, :, pl.ds(half * 128, 128)] = dens2[half, c, z].astype(BF16)
    for side in range(2):
        for row in range(2):
            for z in range(2):
                for c in range(2):
                    source_row = row if side == 0 else ROWS - 2 + row
                    for half in range(2):
                        line = dens2[half, c, z, pl.ds(source_row, 1), :]
                        edge_send[
                            side, pl.ds(row * 4 + z * 2 + c, 1), pl.ds(half * 128, 128)
                        ] = line.astype(BF16).astype(F32)

    pl.semaphore_wait(barrier, COUNT - 1 + len(sides))

    halo = []

    def send_halo(src, dst, index, to):
        copy = pltpu.make_async_remote_copy(
            src_ref=src, dst_ref=dst, send_sem=halo_ssem.at[index], recv_sem=halo_rsem.at[index],
            device_id=to, device_id_type=MESH,
        )
        copy.start()
        halo.append(copy)

    index = 0
    for side in range(2):
        to_y = near_y(-1) if side == 0 else near_y(1)
        for dz in (-1, 1, 0):
            send_halo(
                edge_send.at[side], edge_recv.at[1 - side, 1 - dz], index, (near_z(dz), to_y)
            )
            index += 1
    send_halo(lower_send.at[1], lower_prev.at[1], 6, (near_z(1), me_y))
    send_halo(lower_send.at[0], lower_next.at[0], 7, (near_z(-1), me_y))
    send_halo(lower_send.at[1], lower_next.at[1], 8, (near_z(-1), me_y))
    send_halo(lower_send.at[0], lower_prev.at[0], 9, (near_z(1), me_y))

    weights_in = [
        fetch(src, dst, 2 + i)
        for i, (src, dst) in enumerate(
            (
                (first_w_hbm, first_w), (first_b_hbm, first_b), (pick_hbm, pick),
                (middle_w_hbm, middle_w), (middle_b_hbm, middle_b), (output_w_hbm, output_w),
            )
        )
    ]
    filter_in = [fetch(radial_hbm, radial, 8), fetch(squares_hbm, squares, 9)]
    late_in = [
        fetch(
            dens_hbm.at[pl.ds(2, 2), :, :, pl.ds(half * 128, 128)],
            dens2.at[half, pl.ds(2, 2)], 10 + half,
        )
        for half in range(2)
    ] + [
        fetch(src, dst, 12 + i)
        for i, (src, dst) in enumerate(
            (
                (output_b_hbm, output_b), (forward_x_hbm, forward_x), (forward_z_hbm, forward_z),
                (forward_y_hbm, forward_y), (backward_z_hbm, backward_z),
                (backward_x_hbm, backward_x), (spread_hbm, spread),
            )
        )
    ]

    for copy in weights_in:
        copy.wait()
    wide_w[...] = jnp.zeros_like(wide_w)
    wide_w[pl.ds(0, 54), :] = first_w[...].astype(F32)
    for piece, part in enumerate(split3(first_b[...])):
        wide_w[pl.ds(54 + piece, 1), :] = part.astype(F32)
    turned = jnp.transpose(wide_w[...]).astype(BF16)
    for plane in range(4):
        w1[pl.ds(plane * 128, 128), :] = mul(
            turned, pick[:, pl.ds(plane * 128, 128)]
        ).astype(BF16)
    w2[...] = jnp.transpose(middle_w[...].astype(F32)).astype(BF16)
    b2[...] = jnp.transpose(jnp.broadcast_to(middle_b[...], (128, 128)))
    ow32[...] = output_w[...].astype(F32)
    w3[...] = jnp.zeros_like(w3)
    for a in range(3):
        for b in range(3):
            w3[pl.ds(b * 16, 12), pl.ds(a * 128, 128)] = ow32[pl.ds(36 * a + 12 * b, 12), :]

    def put(first, count, slot, values):
        for e, shifted in enumerate((shift_right(values), values, shift_left(values))):
            for half in range(2):
                window[half, pl.ds(first * SLOTS + e * 12 + slot, count, stride=SLOTS), :] = shifted[
                    :, half * 128 : (half + 1) * 128
                ]

    for half in range(2):
        window[half, pl.ds(36, 72, stride=SLOTS), :] = jnp.ones((72, 128), F32)
        for slot in range(37, 40):
            window[half, pl.ds(slot, 72, stride=SLOTS), :] = jnp.zeros((72, 128), F32)
        window[half, pl.ds(68 * SLOTS, 36), :] = jnp.zeros((36, 128), F32)
        for slot in (0, 1, 12, 13, 24, 25):
            window[half, pl.ds(2 * SLOTS + slot, ROWS, stride=SLOTS), :] = jnp.zeros((ROWS, 128), F32)
    for z in range(2):
        for c in range(2):
            put(2, ROWS, (z + 2) * 2 + c, lower_send[z, c].astype(F32))

    step_x = (me + 1) // 2
    freq_x = step_x.astype(F32) * (1.0 / 128.0)
    for copy in filter_in:
        copy.wait()
    weights = radial[...]
    centres = lax.broadcasted_iota(jnp.int32, (32, 512), 0).astype(F32)

    def filter_part(part, carry):
        lanes = pl.ds(pl.multiple_of(part * 512, 512), 512)
        kappa = jnp.sqrt(squares[:, lanes] + freq_x * freq_x) * (2.0 / math.sqrt(3.0))
        scaled = kappa * 31.0 - centres
        basis = jnp.exp(-scaled * scaled)
        values = mul3(split2(weights), split2(basis))
        for j in range(4):
            profile[pl.ds(part * 4 + j, 128, stride=32), :] = values[:, j * 128 : (j + 1) * 128]
        return carry

    lax.fori_loop(0, 8, filter_part, 0)

    for copy in late_in:
        copy.wait()
    for copy in halo[:9]:
        copy.wait_recv()

    has_prev = me_z > 0
    has_next = me_z < GZ - 1
    has_up = me_y > 0
    has_down = me_y < GY - 1
    for z in range(2):
        for c in range(2):
            if z == 1:
                put(2, ROWS, z * 2 + c, jnp.where(has_prev, lower_prev[z, c].astype(F32), 0.0))
            put(2, ROWS, (z + 4) * 2 + c, jnp.where(has_next, lower_next[z, c].astype(F32), 0.0))
    for side in range(2):
        for offset in range(3):
            valid = has_up if side == 0 else has_down
            if offset == 0:
                valid = jnp.logical_and(valid, has_prev)
            if offset == 2:
                valid = jnp.logical_and(valid, has_next)
            for row in range(2):
                lines = edge_recv[side, offset, pl.ds(row * 4, 4), :]
                lines = jnp.where(valid, lines, 0.0)
                at = (row if side == 0 else ROWS + 2 + row) * SLOTS + offset * 4
                for e, shifted in enumerate((shift_right(lines), lines, shift_left(lines))):
                    for half in range(2):
                        window[half, pl.ds(at + e * 12, 4), :] = shifted[
                            :, half * 128 : (half + 1) * 128
                        ]

    w3_lane = lax.broadcasted_iota(jnp.int32, (48, 384), 1)
    w3_first = jnp.where(jnp.logical_and(w3_lane < 128, me_z == 0), 0.0, w3[...]).astype(BF16)
    w3_second = jnp.where(
        jnp.logical_and(w3_lane >= 256, me_z == GZ - 1), 0.0, w3[...]
    ).astype(BF16)

    def columns(r):
        start = pl.multiple_of((r - 1) * SLOTS, 8)
        return jnp.concatenate(
            [window[0, pl.ds(start, 128), :], window[1, pl.ds(start, 128), :]], axis=1
        ).astype(BF16)

    def second(first_layer):
        values = mul(w2[...], first_layer) + jnp.concatenate([b2[...]] * 2, axis=1)
        return jnp.maximum(values, 0.0).astype(BF16)

    def add_taps(acc, r, taps):
        valid = jnp.logical_not(
            jnp.logical_or(
                jnp.logical_and(r == 1, me_y == 0),
                jnp.logical_and(r == OWN_ROWS, me_y == GY - 1),
            )
        )
        taps = jnp.where(valid, taps, 0.0)
        for half in range(2):
            part = taps[:, half * 128 : (half + 1) * 128]
            at = [pl.ds(pl.multiple_of((r + 1 - b) * 16, 16), 16) for b in range(3)]
            acc[half, at[0], :] = part[0:16]
            acc[half, at[1], :] += part[16:32]
            acc[half, at[2], :] += part[32:48]

    for acc in (acc0, acc1):
        for half in range(2):
            acc[half, pl.ds(0, 32), :] = jnp.zeros((32, 128), F32)

    def group_rows(group):
        return [(sub, group * GROUP + 1 + sub) for sub in range(GROUP)]

    def later_first(group):
        for sub, r in group_rows(group):
            values = mul(w1[pl.ds(128, 384), :], columns(r))
            first_held[sub] = jnp.maximum(values, 0.0).astype(BF16)

    def later_second(group):
        for sub, r in group_rows(group):
            first_layer = first_held[sub]
            layers = [second(first_layer[p * 128 : (p + 1) * 128]) for p in range(3)]
            hidden[r] = jnp.concatenate(layers[0:2], axis=0)
            last_held[sub] = layers[2]

    def later_last(group):
        for sub, r in group_rows(group):
            stacked = jnp.concatenate([hidden[r], last_held[sub]], axis=0)
            add_taps(acc1, r, mul(w3_second, stacked))

    def early_first(group):
        for sub, r in group_rows(group):
            values = mul(w1[pl.ds(0, 128), :], columns(r))
            first_held[sub, pl.ds(0, 128)] = jnp.maximum(values, 0.0).astype(BF16)

    def early_second(group):
        for sub, r in group_rows(group):
            last_held[sub] = second(first_held[sub, pl.ds(0, 128)])

    def early_last(group):
        for sub, r in group_rows(group):
            stacked = jnp.concatenate([last_held[sub], hidden[r]], axis=0)
            add_taps(acc0, r, mul(w3_first, stacked))

    def start_groups(first, middle, last):
        first(0)
        middle(0)
        first(1)

    def run_groups(first, middle, last, begin, end):
        def step(group, carry):
            last(group - 2)
            middle(group - 1)
            first(group)
            return carry

        lax.fori_loop(begin, end, step, 0)

    def end_groups(first, middle, last):
        last(GROUPS - 2)
        middle(GROUPS - 1)
        last(GROUPS - 1)

    later = (later_first, later_second, later_last)
    early = (early_first, early_second, early_last)

    start_groups(*later)
    run_groups(*later, 2, GROUPS)
    end_groups(*later)

    def couple(acc, z, parity):
        raw = []
        for o in range(4):
            taps = [
                jnp.concatenate(
                    [
                        acc[half, pl.ds((2 + parity) * 16 + e * 4 + o, 32, stride=32), :]
                        for half in range(2)
                    ],
                    axis=1,
                )
                for e in range(3)
            ]
            raw.append(shift_right(taps[0]) + taps[1] + shift_left(taps[2]) + output_b[o])
        lines = [
            jnp.concatenate(
                [
                    dens2[half, c, z, pl.ds(parity, 32, stride=2), :]
                    for half in range(2)
                ],
                axis=1,
            )
            for c in range(4)
        ]
        scales = [jnp.tanh(raw[0]), jnp.tanh(raw[1])]
        for o in range(2):
            lines[2 + o] = lines[2 + o] * jnp.exp(scales[o]) + raw[2 + o]
        return jnp.concatenate(lines, axis=0), scales[0] + scales[1]

    def spread_x(values):
        high, mid, low = split3(values)
        return mul(high, spread[...]) + (mul(mid, spread[...]) + mul(low, spread[...]))

    def fold(values):
        rows, lanes = values.shape
        total = values[:, 0:128]
        for at in range(128, lanes, 128):
            total = total + values[:, at : at + 128]
        return jnp.sum(total.reshape(rows // 8, 8, 128), axis=0)

    source, scale_sum = couple(acc1, 1, 0)
    kept[0] = source
    total = fold(scale_sum)
    x_modes = mul3(
        (forward_x[0], forward_x[1]), split2(source), ((1,), (1,))
    )
    x_send[...] = x_modes.reshape(COUNT, 2, 128)

    sent = list(halo)

    def send_all(part, dst, stage):
        def one(i, carry):
            to = near(i)
            pltpu.make_async_remote_copy(
                src_ref=part(to), dst_ref=dst.at[me], send_sem=all_ssem.at[stage],
                recv_sem=all_rsem.at[stage], device_id=to, device_id_type=LOGICAL,
            ).start()
            return carry

        lax.fori_loop(1, COUNT, one, 0)
        dst[me] = part(me)[...]

    def wait_all(dst, stage):
        copy = pltpu.make_async_remote_copy(
            src_ref=dst.at[pl.ds(0, COUNT - 1)], dst_ref=dst.at[pl.ds(0, COUNT - 1)],
            send_sem=all_ssem.at[stage], recv_sem=all_rsem.at[stage],
            device_id=near(1), device_id_type=LOGICAL,
        )
        copy.wait_recv()
        sent.append(copy)

    send_all(lambda to: x_send.at[to], z_recv, 0)
    kept[1], scale_sum = couple(acc1, 1, 1)
    total = total + fold(scale_sum)
    halo[9].wait_recv()
    for c in range(2):
        put(2, ROWS, c, jnp.where(has_prev, lower_prev[0, c].astype(F32), 0.0))
    start_groups(*early)
    run_groups(*early, 2, 6)
    wait_all(z_recv, 0)

    z_modes = mul3((forward_z[0], forward_z[1]), split2(z_recv[...].reshape(256, 128)))

    lines = jnp.concatenate([z_modes[g * 64 : (g + 1) * 64] for g in range(GY)], axis=1)
    modes = mul3(split2(lines), (forward_y[0], forward_y[1]))
    parts = [
        modes[k * 32 : (k + 1) * 32, c * 128 : (c + 1) * 128] for k in range(2) for c in range(4)
    ]
    for o in range(16):
        value = profile[pl.ds(o * 256, 32), :] * parts[0]
        for c in range(1, 8):
            value = value + profile[pl.ds(o * 256 + c * 32, 32), :] * parts[c]
        mixed[pl.ds((o // 4) * 32, 32), pl.ds((o % 4) * 128, 128)] = value
    back = mul3(split2(mixed[...]), (forward_y[0], forward_y[1]), ((1,), (1,)))
    for pair in range(2):
        lines = jnp.concatenate(
            [back[:, g * 128 : (g + 1) * 128] for g in (2 * pair, 2 * pair + 1)], axis=0
        )
        planes = mul3((backward_z[0], backward_z[1]), split2(lines))
        zb_send[:, pl.ds(pair * 2, 2)] = planes.reshape(GZ, 2, 4, 128)

    send_all(lambda to: zb_send.at[to // GY, lax.rem(to, GY)], x_recv, 1)
    run_groups(*early, 6, GROUPS)
    end_groups(*early)

    squares_sum = jnp.zeros((8, 128), F32)
    for parity in range(2):
        coupled, scale_sum = couple(acc0, 0, parity)
        total = total + fold(scale_sum)
        squares_sum = squares_sum + fold(coupled * coupled)
        coupled = spread_x(coupled)
        for k in range(2):
            at = (2 * parity + k) * 4
            factored[pl.ds(at, 4), 0] = coupled[:, k * 128 : (k + 1) * 128].reshape(4, 32, 128)
    source = spread_x(kept[0])
    squares_sum = squares_sum + fold(source * source)
    for k in range(2):
        latent[pl.ds(k * 4, 4), 0] = source[:, k * 128 : (k + 1) * 128].reshape(4, 32, 128)
    target = spread_x(kept[1])
    wait_all(x_recv, 1)

    shifts = []
    for og in range(4):
        lines = x_recv[:, og, :]
        shifts.append(jnp.transpose(mul3((backward_x[0], backward_x[1]), split2(lines))))
    for k in range(2):
        scale = jnp.tanh(shifts[k])
        total = total + fold(scale)
        moved = target[:, k * 128 : (k + 1) * 128] * jnp.exp(scale) + shifts[2 + k]
        squares_sum = squares_sum + fold(moved * moved)
        latent[pl.ds(8 + k * 4, 4), 0] = moved.reshape(4, 32, 128)

    total = total - 0.5 * squares_sum
    sum_send[0] = jnp.sum(total, axis=0, keepdims=True)

    send_all(lambda to: sum_send.at[0], sum_recv, 2)
    wait_all(sum_recv, 2)
    total = jnp.sum(sum_recv[...], axis=0)
    for copy in sent:
        copy.wait_send()
    count = 4.0 * 64 * 256 * 256
    log_density[0, 0] = jnp.sum(total) / count - 0.5 * math.log(2.0 * math.pi)


def shards(consts, density_field, first_weight, first_bias, middle_weight, middle_bias, output_weight, output_bias, radial_weights):
    vmem = pl.BlockSpec(memory_space=pltpu.VMEM)
    smem = pl.BlockSpec(memory_space=pltpu.SMEM)
    hbm = pl.BlockSpec(memory_space=pltpu.HBM)
    operands = [
        density_field, first_weight, first_bias.reshape(1, 128), middle_weight,
        middle_bias.reshape(1, 128), output_weight, output_bias, radial_weights.reshape(128, 32),
    ] + [jnp.asarray(value) for value in consts.values()]
    specs = [hbm] * len(operands)
    held = [pltpu.VMEM(value.shape, value.dtype) for value in operands]
    held[6] = pltpu.SMEM(output_bias.shape, F32)
    buffers = [
        pltpu.VMEM((2, 2, ROWS, WIDE), BF16),
        pltpu.VMEM((2, 8, WIDE), F32),
        pltpu.VMEM((2, 2, ROWS, WIDE), BF16),
        pltpu.VMEM((2, 2, ROWS, WIDE), BF16),
        pltpu.VMEM((2, 3, 8, WIDE), F32),
        pltpu.VMEM((2, 72 * SLOTS, 128), F32),
        pltpu.VMEM((OWN_ROWS + 2, 256, WIDE), BF16),
        pltpu.VMEM((2, 70 * 16, 128), F32),
        pltpu.VMEM((2, 70 * 16, 128), F32),
        pltpu.VMEM((64, 128), F32),
        pltpu.VMEM((512, 128), BF16),
        pltpu.VMEM((128, 128), BF16),
        pltpu.VMEM((128, 128), F32),
        pltpu.VMEM((48, 384), F32),
        pltpu.VMEM((108, 128), F32),
        pltpu.VMEM((128 * 32, 128), F32),
        pltpu.VMEM((COUNT, 2, 128), F32),
        pltpu.VMEM((COUNT, 2, 128), F32),
        pltpu.VMEM((128, 512), F32),
        pltpu.VMEM((GZ, GY, 4, 128), F32),
        pltpu.VMEM((COUNT, 4, 128), F32),
        pltpu.VMEM((2, 128, WIDE), F32),
        pltpu.VMEM((GROUP, 384, WIDE), BF16),
        pltpu.VMEM((GROUP, 128, WIDE), BF16),
        pltpu.VMEM((1, 1, 128), F32),
        pltpu.VMEM((COUNT, 1, 128), F32),
        pltpu.VMEM((2, 4, 2, ROWS, 128), F32),
    ] + held[1:] + [
        pltpu.SemaphoreType.DMA((10,)),
        pltpu.SemaphoreType.DMA((10,)),
        pltpu.SemaphoreType.DMA((3,)),
        pltpu.SemaphoreType.DMA((3,)),
        pltpu.SemaphoreType.DMA((19,)),
    ]
    factored, latent, log_density = pl.pallas_call(
        flow_kernel,
        out_shape=(
            jax.ShapeDtypeStruct((16, 1, 32, 128), F32),
            jax.ShapeDtypeStruct((16, 1, 32, 128), F32),
            jax.ShapeDtypeStruct((1, 1), F32),
        ),
        in_specs=specs,
        out_specs=(vmem, vmem, smem),
        scratch_shapes=buffers,
        compiler_params=pltpu.CompilerParams(
            collective_id=0, has_side_effects=True, vmem_limit_bytes=60 * 1024 * 1024
        ),
        name="flow",
    )(*operands)
    return factored, latent, log_density.reshape(())


def solution(mesh):
    assert mesh.shape["gz"] == GZ and mesh.shape["gy"] == GY
    in_specs = (P(None, "gz", "gy", None), P(), P(), P(), P(), P(), P(), P())
    out_specs = (P(None, "gz", "gy", None), P(None, "gz", "gy", None), P())
    return jax.shard_map(
        functools.partial(shards, tables()),
        mesh=mesh, in_specs=in_specs, out_specs=out_specs, check_vma=False,
    )
```

```python
import functools
import math

import jax
import jax.numpy as jnp
import ml_dtypes
import numpy as np
from jax import lax
from jax.experimental import pallas as pl
from jax.experimental.pallas import tpu as pltpu
from jax.sharding import PartitionSpec as P

MESH = pl.DeviceIdType.MESH
LOGICAL = pl.DeviceIdType.LOGICAL
F32 = jnp.float32
BF16 = jnp.bfloat16

SLOTS = 40
ROWS = 64
WIDE = 256
GZ = 32
GY = 4
COUNT = GZ * GY
OWN_ROWS = ROWS + 2
CHUNK = 16
CHUNKS = ROWS // CHUNK
GROUP = 6
GROUPS = OWN_ROWS // GROUP


def real_basis(length):
    cells = np.arange(length)
    rows = [np.full(length, 1.0 / math.sqrt(length))]
    for m in range(1, length // 2):
        rows.append(math.sqrt(2.0 / length) * np.cos(2.0 * math.pi * m * cells / length))
        rows.append(math.sqrt(2.0 / length) * np.sin(2.0 * math.pi * m * cells / length))
    rows.append(np.where(cells % 2 == 0, 1.0, -1.0) / math.sqrt(length))
    return np.stack(rows)


def split_pair(table):
    table = np.asarray(table, np.float32)
    high = table.astype(ml_dtypes.bfloat16)
    low = (table - high.astype(np.float32)).astype(ml_dtypes.bfloat16)
    return np.stack([high, low])


def tables():
    fx, fy, fz = real_basis(128), real_basis(128), real_basis(32)
    forward_x = np.zeros((128, 2, 128, 2))
    for k in range(2):
        forward_x[:, k, :, k] = fx
    forward_x = forward_x.reshape(256, 256)
    forward_z = np.einsum("kz,qp->qkzp", fz, np.eye(8)).reshape(256, 256)
    forward_y = np.einsum("kgy,cd->gcydk", fy.reshape(128, 4, 32), np.eye(4)).reshape(512, 512)
    spread = np.zeros((128, 2, 2, 128))
    for k in range(2):
        spread[np.arange(128), k, k, np.arange(128)] = 1.0
    spread = spread.reshape(256, 256).astype(ml_dtypes.bfloat16)
    pick = np.zeros((64, 4, 128))
    for plane in range(4):
        for c in range(2):
            for a in range(3):
                for b in range(3):
                    for e in range(3):
                        row = 27 * c + 9 * a + 3 * b + e
                        pick[row, plane, b * SLOTS + e * 12 + (a + plane) * 2 + c] = 1.0
        for piece in range(3):
            pick[54 + piece, plane, piece * SLOTS + 36] = 1.0
    pick = pick.reshape(64, 512).astype(ml_dtypes.bfloat16)
    half_z = (np.arange(32) + 1) // 2 / 32.0
    half_y = (np.arange(128) + 1) // 2 / 128.0
    squares = (half_z[:, None] ** 2 + half_y[None, :] ** 2).reshape(1, 4096).astype(np.float32)
    return {
        "forward_x": split_pair(forward_x),
        "forward_z": split_pair(forward_z),
        "backward_z": split_pair(forward_z.T),
        "forward_y": split_pair(forward_y),
        "backward_x": split_pair(fx.T),
        "spread": spread,
        "pick": pick,
        "squares": squares,
    }


def split2(values):
    high = values.astype(BF16)
    return high, (values - high.astype(F32)).astype(BF16)


def split3(values):
    high = values.astype(BF16)
    rest = values - high.astype(F32)
    mid = rest.astype(BF16)
    return high, mid, (rest - mid.astype(F32)).astype(BF16)


def mul(a, b, dims=((1,), (0,))):
    return lax.dot_general(a, b, (dims, ((), ())), preferred_element_type=F32)


def mul3(a, b, dims=((1,), (0,))):
    return mul(a[0], b[0], dims) + (mul(a[0], b[1], dims) + mul(a[1], b[0], dims))


def shift_right(values):
    lane = lax.broadcasted_iota(jnp.int32, values.shape, values.ndim - 1)
    return jnp.where(lane == 0, 0.0, pltpu.roll(values, 1, values.ndim - 1))


def shift_left(values):
    last = values.shape[-1] - 1
    lane = lax.broadcasted_iota(jnp.int32, values.shape, values.ndim - 1)
    return jnp.where(lane == last, 0.0, pltpu.roll(values, last, values.ndim - 1))


def flow_kernel(
    dens_hbm, first_w_hbm, first_b_hbm, middle_w_hbm, middle_b_hbm, output_w_hbm, output_b_hbm,
    radial_hbm, forward_x_hbm, forward_z_hbm, backward_z_hbm, forward_y_hbm, backward_x_hbm,
    spread_hbm, pick_hbm, squares_hbm,
    factored, latent, log_density,
    lower_send, edge_send, lower_prev, lower_next, edge_recv,
    window, hidden, acc0, acc1, wide_w, w1, w2, b2, w3, ow32, profile,
    x_send, z_recv, mixed, zb_send, x_recv,
    kept, first_held, last_held, sum_send, sum_recv, dens2,
    first_w, first_b, middle_w, middle_b, output_w, output_b,
    radial, forward_x, forward_z, backward_z, forward_y, backward_x, spread, pick, squares,
    halo_ssem, halo_rsem, all_ssem, all_rsem, in_sem,
):
    me_z = lax.axis_index("gz")
    me_y = lax.axis_index("gy")

    me = me_z * GY + me_y

    def near(step):
        return lax.rem(me + step, COUNT)

    def near_z(step):
        return lax.rem(me_z + step + GZ, GZ)

    def near_y(step):
        return lax.rem(me_y + step + GY, GY)

    barrier = pltpu.get_barrier_semaphore()
    sides = [(dz, dy) for dz in (-1, 0, 1) for dy in (-1, 0, 1) if (dz, dy) != (0, 0)]
    for dz, dy in sides:
        pl.semaphore_signal(
            barrier, inc=1, device_id=(near_z(dz), near_y(dy)), device_id_type=MESH
        )
    def fetch(src, dst, index):
        copy = pltpu.make_async_copy(src, dst, in_sem.at[index])
        copy.start()
        return copy

    lower_in = [
        fetch(
            dens_hbm.at[pl.ds(0, 2), :, :, pl.ds(half * 128, 128)],
            dens2.at[half, pl.ds(0, 2)], half,
        )
        for half in range(2)
    ]

    def greet(i, carry):
        pl.semaphore_signal(barrier, inc=1, device_id=near(i), device_id_type=LOGICAL)
        return carry

    lax.fori_loop(1, COUNT, greet, 0)

    for copy in lower_in:
        copy.wait()
    for z in range(2):
        for c in range(2):
            for half in range(2):
                lower_send[z, c, :, pl.ds(half * 128, 128)] = dens2[half, c, z].astype(BF16)
    for side in range(2):
        for row in range(2):
            for z in range(2):
                for c in range(2):
                    source_row = row if side == 0 else ROWS - 2 + row
                    for half in range(2):
                        line = dens2[half, c, z, pl.ds(source_row, 1), :]
                        edge_send[
                            side, pl.ds(row * 4 + z * 2 + c, 1), pl.ds(half * 128, 128)
                        ] = line.astype(BF16).astype(F32)

    pl.semaphore_wait(barrier, COUNT - 1 + len(sides))

    halo = []

    def halo_copy(src, dst, index, to):
        return pltpu.make_async_remote_copy(
            src_ref=src, dst_ref=dst, send_sem=halo_ssem.at[index], recv_sem=halo_rsem.at[index],
            device_id=to, device_id_type=MESH,
        )

    def chunk_copies(chunk):
        rows = pl.ds(pl.multiple_of(chunk * CHUNK, CHUNK), CHUNK)
        return (
            halo_copy(
                lower_send.at[:, :, rows], lower_next.at[:, :, rows], 6 + chunk,
                (near_z(-1), me_y),
            ),
            halo_copy(
                lower_send.at[1, :, rows], lower_prev.at[1, :, rows], 10 + chunk,
                (near_z(1), me_y),
            ),
        )

    def start_halo(copies):
        for copy in copies:
            copy.start()
            halo.append(copy)

    edges = [
        [
            halo_copy(
                edge_send.at[side], edge_recv.at[1 - side, 1 - dz], side * 3 + dz + 1,
                (near_z(dz), near_y(-1) if side == 0 else near_y(1)),
            )
            for dz in (-1, 0, 1)
        ]
        for side in range(2)
    ]
    far_plane = halo_copy(lower_send.at[0], lower_prev.at[0], 14, (near_z(1), me_y))
    start_halo(edges[1])
    start_halo(chunk_copies(0))
    start_halo(edges[0])
    for chunk in range(1, CHUNKS):
        start_halo(chunk_copies(chunk))
    start_halo([far_plane])

    weights_in = [
        fetch(src, dst, 2 + i)
        for i, (src, dst) in enumerate(
            (
                (first_w_hbm, first_w), (first_b_hbm, first_b), (pick_hbm, pick),
                (middle_w_hbm, middle_w), (middle_b_hbm, middle_b), (output_w_hbm, output_w),
            )
        )
    ]
    filter_in = [fetch(radial_hbm, radial, 8), fetch(squares_hbm, squares, 9)]
    late_in = [
        fetch(
            dens_hbm.at[pl.ds(2, 2), :, :, pl.ds(half * 128, 128)],
            dens2.at[half, pl.ds(2, 2)], 10 + half,
        )
        for half in range(2)
    ] + [
        fetch(src, dst, 12 + i)
        for i, (src, dst) in enumerate(
            (
                (output_b_hbm, output_b), (forward_x_hbm, forward_x), (forward_z_hbm, forward_z),
                (forward_y_hbm, forward_y), (backward_z_hbm, backward_z),
                (backward_x_hbm, backward_x), (spread_hbm, spread),
            )
        )
    ]

    for copy in weights_in:
        copy.wait()
    wide_w[...] = jnp.zeros_like(wide_w)
    wide_w[pl.ds(0, 54), :] = first_w[...].astype(F32)
    for piece, part in enumerate(split3(first_b[...])):
        wide_w[pl.ds(54 + piece, 1), :] = part.astype(F32)
    turned = jnp.transpose(wide_w[...]).astype(BF16)
    for plane in range(4):
        w1[pl.ds(plane * 128, 128), :] = mul(
            turned, pick[:, pl.ds(plane * 128, 128)]
        ).astype(BF16)
    w2[...] = jnp.transpose(middle_w[...].astype(F32)).astype(BF16)
    b2[...] = jnp.transpose(jnp.broadcast_to(middle_b[...], (128, 128)))
    ow32[...] = output_w[...].astype(F32)
    w3[...] = jnp.zeros_like(w3)
    for a in range(3):
        for b in range(3):
            w3[pl.ds(b * 16, 12), pl.ds(a * 128, 128)] = ow32[pl.ds(36 * a + 12 * b, 12), :]

    def put(first, count, slot, values):
        for e, shifted in enumerate((shift_right(values), values, shift_left(values))):
            for half in range(2):
                window[half, pl.ds(first * SLOTS + e * 12 + slot, count, stride=SLOTS), :] = shifted[
                    :, half * 128 : (half + 1) * 128
                ]

    for half in range(2):
        window[half, pl.ds(36, 72, stride=SLOTS), :] = jnp.ones((72, 128), F32)
        for slot in range(37, 40):
            window[half, pl.ds(slot, 72, stride=SLOTS), :] = jnp.zeros((72, 128), F32)
        window[half, pl.ds(68 * SLOTS, 36), :] = jnp.zeros((36, 128), F32)
        for slot in (0, 1, 12, 13, 24, 25):
            window[half, pl.ds(2 * SLOTS + slot, ROWS, stride=SLOTS), :] = jnp.zeros((ROWS, 128), F32)
    for z in range(2):
        for c in range(2):
            put(2, ROWS, (z + 2) * 2 + c, lower_send[z, c].astype(F32))

    step_x = (me + 1) // 2
    freq_x = step_x.astype(F32) * (1.0 / 128.0)
    for copy in filter_in:
        copy.wait()
    weights = radial[...]
    centres = lax.broadcasted_iota(jnp.int32, (32, 512), 0).astype(F32)

    def filter_part(part, carry):
        lanes = pl.ds(pl.multiple_of(part * 512, 512), 512)
        kappa = jnp.sqrt(squares[:, lanes] + freq_x * freq_x) * (2.0 / math.sqrt(3.0))
        scaled = kappa * 31.0 - centres
        basis = jnp.exp(-scaled * scaled)
        values = mul3(split2(weights), split2(basis))
        for j in range(4):
            profile[pl.ds(part * 4 + j, 128, stride=32), :] = values[:, j * 128 : (j + 1) * 128]
        return carry

    lax.fori_loop(0, 8, filter_part, 0)

    for copy in late_in:
        copy.wait()

    has_prev = me_z > 0
    has_next = me_z < GZ - 1
    has_up = me_y > 0
    has_down = me_y < GY - 1

    def fill_chunk(chunk):
        for copy in chunk_copies(chunk):
            copy.wait_recv()
        rows = pl.ds(pl.multiple_of(chunk * CHUNK, CHUNK), CHUNK)
        first = 2 + chunk * CHUNK
        for c in range(2):
            values = lower_prev[1, c, rows, :].astype(F32)
            put(first, CHUNK, 2 + c, jnp.where(has_prev, values, 0.0))
            for z in range(2):
                values = lower_next[z, c, rows, :].astype(F32)
                put(first, CHUNK, (z + 4) * 2 + c, jnp.where(has_next, values, 0.0))

    def fill_edge(side):
        for copy in edges[1 - side]:
            copy.wait_recv()
        for offset in range(3):
            valid = has_up if side == 0 else has_down
            if offset == 0:
                valid = jnp.logical_and(valid, has_prev)
            if offset == 2:
                valid = jnp.logical_and(valid, has_next)
            for row in range(2):
                lines = edge_recv[side, offset, pl.ds(row * 4, 4), :]
                lines = jnp.where(valid, lines, 0.0)
                at = (row if side == 0 else ROWS + 2 + row) * SLOTS + offset * 4
                for e, shifted in enumerate((shift_right(lines), lines, shift_left(lines))):
                    for half in range(2):
                        window[half, pl.ds(at + e * 12, 4), :] = shifted[
                            :, half * 128 : (half + 1) * 128
                        ]

    fill_edge(0)
    fill_chunk(0)

    w3_lane = lax.broadcasted_iota(jnp.int32, (48, 384), 1)
    w3_first = jnp.where(jnp.logical_and(w3_lane < 128, me_z == 0), 0.0, w3[...]).astype(BF16)
    w3_second = jnp.where(
        jnp.logical_and(w3_lane >= 256, me_z == GZ - 1), 0.0, w3[...]
    ).astype(BF16)

    def columns(r):
        start = pl.multiple_of((r - 1) * SLOTS, 8)
        return jnp.concatenate(
            [window[0, pl.ds(start, 128), :], window[1, pl.ds(start, 128), :]], axis=1
        ).astype(BF16)

    def second(first_layer):
        values = mul(w2[...], first_layer) + jnp.concatenate([b2[...]] * 2, axis=1)
        return jnp.maximum(values, 0.0).astype(BF16)

    def add_taps(acc, r, taps):
        valid = jnp.logical_not(
            jnp.logical_or(
                jnp.logical_and(r == 1, me_y == 0),
                jnp.logical_and(r == OWN_ROWS, me_y == GY - 1),
            )
        )
        taps = jnp.where(valid, taps, 0.0)
        for half in range(2):
            part = taps[:, half * 128 : (half + 1) * 128]
            at = [pl.ds(pl.multiple_of((r + 1 - b) * 16, 16), 16) for b in range(3)]
            acc[half, at[0], :] = part[0:16]
            acc[half, at[1], :] += part[16:32]
            acc[half, at[2], :] += part[32:48]

    for acc in (acc0, acc1):
        for half in range(2):
            acc[half, pl.ds(0, 32), :] = jnp.zeros((32, 128), F32)

    def group_rows(group):
        return [(sub, group * GROUP + 1 + sub) for sub in range(GROUP)]

    def later_first(group):
        for sub, r in group_rows(group):
            values = mul(w1[pl.ds(128, 384), :], columns(r))
            first_held[sub] = jnp.maximum(values, 0.0).astype(BF16)

    def later_second(group):
        for sub, r in group_rows(group):
            first_layer = first_held[sub]
            layers = [second(first_layer[p * 128 : (p + 1) * 128]) for p in range(3)]
            hidden[r] = jnp.concatenate(layers[0:2], axis=0)
            last_held[sub] = layers[2]

    def later_last(group):
        for sub, r in group_rows(group):
            stacked = jnp.concatenate([hidden[r], last_held[sub]], axis=0)
            add_taps(acc1, r, mul(w3_second, stacked))

    def early_first(group):
        for sub, r in group_rows(group):
            values = mul(w1[pl.ds(0, 128), :], columns(r))
            first_held[sub, pl.ds(0, 128)] = jnp.maximum(values, 0.0).astype(BF16)

    def early_second(group):
        for sub, r in group_rows(group):
            last_held[sub] = second(first_held[sub, pl.ds(0, 128)])

    def early_last(group):
        for sub, r in group_rows(group):
            stacked = jnp.concatenate([last_held[sub], hidden[r]], axis=0)
            add_taps(acc0, r, mul(w3_first, stacked))

    def start_groups(first, middle, last):
        first(0)
        middle(0)
        first(1)

    def run_groups(first, middle, last, begin, end, beside=lambda group: None):
        def step(group, carry):
            beside(group)
            last(group - 2)
            middle(group - 1)
            first(group)
            return carry

        lax.fori_loop(begin, end, step, 0)

    def end_groups(first, middle, last):
        last(GROUPS - 2)
        middle(GROUPS - 1)
        last(GROUPS - 1)

    later = (later_first, later_second, later_last)
    early = (early_first, early_second, early_last)

    start_groups(*later)
    fill_edge(1)

    def later_chunk(chunk, carry):
        fill_chunk(chunk)
        run_groups(*later, 3 * chunk - 1, 3 * chunk + 2)
        return carry

    lax.fori_loop(1, CHUNKS, later_chunk, 0)
    end_groups(*later)

    def couple(acc, z, parity):
        raw = []
        for o in range(4):
            taps = [
                jnp.concatenate(
                    [
                        acc[half, pl.ds((2 + parity) * 16 + e * 4 + o, 32, stride=32), :]
                        for half in range(2)
                    ],
                    axis=1,
                )
                for e in range(3)
            ]
            raw.append(shift_right(taps[0]) + taps[1] + shift_left(taps[2]) + output_b[o])
        lines = [
            jnp.concatenate(
                [
                    dens2[half, c, z, pl.ds(parity, 32, stride=2), :]
                    for half in range(2)
                ],
                axis=1,
            )
            for c in range(4)
        ]
        scales = [jnp.tanh(raw[0]), jnp.tanh(raw[1])]
        for o in range(2):
            lines[2 + o] = lines[2 + o] * jnp.exp(scales[o]) + raw[2 + o]
        return jnp.concatenate(lines, axis=0), scales[0] + scales[1]

    def spread_x(values):
        high, mid, low = split3(values)
        return mul(high, spread[...]) + (mul(mid, spread[...]) + mul(low, spread[...]))

    def fold(values):
        rows, lanes = values.shape
        total = values[:, 0:128]
        for at in range(128, lanes, 128):
            total = total + values[:, at : at + 128]
        return jnp.sum(total.reshape(rows // 8, 8, 128), axis=0)

    source, scale_sum = couple(acc1, 1, 0)
    kept[0] = source
    total = fold(scale_sum)
    x_modes = mul3(
        (forward_x[0], forward_x[1]), split2(source), ((1,), (1,))
    )
    x_send[...] = x_modes.reshape(COUNT, 2, 128)

    sent = list(halo)

    def send_one(part, dst, stage, step):
        to = near(step)
        pltpu.make_async_remote_copy(
            src_ref=part(to), dst_ref=dst.at[me], send_sem=all_ssem.at[stage],
            recv_sem=all_rsem.at[stage], device_id=to, device_id_type=LOGICAL,
        ).start()

    def send_all(part, dst, stage, end=COUNT):
        def one(i, carry):
            send_one(part, dst, stage, i)
            return carry

        lax.fori_loop(1, end, one, 0)
        dst[me] = part(me)[...]

    def wait_all(dst, stage):
        copy = pltpu.make_async_remote_copy(
            src_ref=dst.at[pl.ds(0, COUNT - 1)], dst_ref=dst.at[pl.ds(0, COUNT - 1)],
            send_sem=all_ssem.at[stage], recv_sem=all_rsem.at[stage],
            device_id=near(1), device_id_type=LOGICAL,
        )
        copy.wait_recv()
        sent.append(copy)

    def x_part(to):
        return x_send.at[to]

    each = (COUNT - 1) // (GROUPS - 2)
    before = COUNT - each * (GROUPS - 2)

    def send_some(group):
        for i in range(each):
            send_one(x_part, z_recv, 0, before + (group - 2) * each + i)

    send_all(x_part, z_recv, 0, before)
    far_plane.wait_recv()
    for c in range(2):
        put(2, ROWS, c, jnp.where(has_prev, lower_prev[0, c].astype(F32), 0.0))
    start_groups(*early)
    run_groups(*early, 2, GROUPS, send_some)
    end_groups(*early)
    kept[1], scale_sum = couple(acc1, 1, 1)
    total = total + fold(scale_sum)
    wait_all(z_recv, 0)

    z_modes = mul3((forward_z[0], forward_z[1]), split2(z_recv[...].reshape(256, 128)))

    lines = jnp.concatenate([z_modes[g * 64 : (g + 1) * 64] for g in range(GY)], axis=1)
    modes = mul3(split2(lines), (forward_y[0], forward_y[1]))
    parts = [
        modes[k * 32 : (k + 1) * 32, c * 128 : (c + 1) * 128] for k in range(2) for c in range(4)
    ]
    for o in range(16):
        value = profile[pl.ds(o * 256, 32), :] * parts[0]
        for c in range(1, 8):
            value = value + profile[pl.ds(o * 256 + c * 32, 32), :] * parts[c]
        mixed[pl.ds((o // 4) * 32, 32), pl.ds((o % 4) * 128, 128)] = value
    back = mul3(split2(mixed[...]), (forward_y[0], forward_y[1]), ((1,), (1,)))
    for pair in range(2):
        lines = jnp.concatenate(
            [back[:, g * 128 : (g + 1) * 128] for g in (2 * pair, 2 * pair + 1)], axis=0
        )
        planes = mul3((backward_z[0], backward_z[1]), split2(lines))
        zb_send[:, pl.ds(pair * 2, 2)] = planes.reshape(GZ, 2, 4, 128)

    send_all(lambda to: zb_send.at[to // GY, lax.rem(to, GY)], x_recv, 1)

    squares_sum = fold(kept[0] * kept[0])
    for parity in range(2):
        coupled, scale_sum = couple(acc0, 0, parity)
        kept[2 + parity] = coupled
        total = total + fold(scale_sum)
        squares_sum = squares_sum + fold(coupled * coupled)
    target = spread_x(kept[1])
    wait_all(x_recv, 1)

    shifts = []
    for og in range(4):
        lines = x_recv[:, og, :]
        shifts.append(jnp.transpose(mul3((backward_x[0], backward_x[1]), split2(lines))))
    for k in range(2):
        scale = jnp.tanh(shifts[k])
        total = total + fold(scale)
        moved = target[:, k * 128 : (k + 1) * 128] * jnp.exp(scale) + shifts[2 + k]
        squares_sum = squares_sum + fold(moved * moved)
        latent[pl.ds(8 + k * 4, 4), 0] = moved.reshape(4, 32, 128)

    total = total - 0.5 * squares_sum
    sum_send[0] = jnp.sum(total, axis=0, keepdims=True)

    send_all(lambda to: sum_send.at[0], sum_recv, 2)
    for parity in range(2):
        coupled = spread_x(kept[2 + parity])
        for k in range(2):
            at = (2 * parity + k) * 4
            factored[pl.ds(at, 4), 0] = coupled[:, k * 128 : (k + 1) * 128].reshape(4, 32, 128)
    source = spread_x(kept[0])
    for k in range(2):
        latent[pl.ds(k * 4, 4), 0] = source[:, k * 128 : (k + 1) * 128].reshape(4, 32, 128)
    wait_all(sum_recv, 2)
    total = jnp.sum(sum_recv[...], axis=0)
    for copy in sent:
        copy.wait_send()
    count = 4.0 * 64 * 256 * 256
    log_density[0, 0] = jnp.sum(total) / count - 0.5 * math.log(2.0 * math.pi)


def shards(consts, density_field, first_weight, first_bias, middle_weight, middle_bias, output_weight, output_bias, radial_weights):
    vmem = pl.BlockSpec(memory_space=pltpu.VMEM)
    smem = pl.BlockSpec(memory_space=pltpu.SMEM)
    hbm = pl.BlockSpec(memory_space=pltpu.HBM)
    operands = [
        density_field, first_weight, first_bias.reshape(1, 128), middle_weight,
        middle_bias.reshape(1, 128), output_weight, output_bias, radial_weights.reshape(128, 32),
    ] + [jnp.asarray(value) for value in consts.values()]
    specs = [hbm] * len(operands)
    held = [pltpu.VMEM(value.shape, value.dtype) for value in operands]
    held[6] = pltpu.SMEM(output_bias.shape, F32)
    buffers = [
        pltpu.VMEM((2, 2, ROWS, WIDE), BF16),
        pltpu.VMEM((2, 8, WIDE), F32),
        pltpu.VMEM((2, 2, ROWS, WIDE), BF16),
        pltpu.VMEM((2, 2, ROWS, WIDE), BF16),
        pltpu.VMEM((2, 3, 8, WIDE), F32),
        pltpu.VMEM((2, 72 * SLOTS, 128), F32),
        pltpu.VMEM((OWN_ROWS + 2, 256, WIDE), BF16),
        pltpu.VMEM((2, 70 * 16, 128), F32),
        pltpu.VMEM((2, 70 * 16, 128), F32),
        pltpu.VMEM((64, 128), F32),
        pltpu.VMEM((512, 128), BF16),
        pltpu.VMEM((128, 128), BF16),
        pltpu.VMEM((128, 128), F32),
        pltpu.VMEM((48, 384), F32),
        pltpu.VMEM((108, 128), F32),
        pltpu.VMEM((128 * 32, 128), F32),
        pltpu.VMEM((COUNT, 2, 128), F32),
        pltpu.VMEM((COUNT, 2, 128), F32),
        pltpu.VMEM((128, 512), F32),
        pltpu.VMEM((GZ, GY, 4, 128), F32),
        pltpu.VMEM((COUNT, 4, 128), F32),
        pltpu.VMEM((4, 128, WIDE), F32),
        pltpu.VMEM((GROUP, 384, WIDE), BF16),
        pltpu.VMEM((GROUP, 128, WIDE), BF16),
        pltpu.VMEM((1, 1, 128), F32),
        pltpu.VMEM((COUNT, 1, 128), F32),
        pltpu.VMEM((2, 4, 2, ROWS, 128), F32),
    ] + held[1:] + [
        pltpu.SemaphoreType.DMA((15,)),
        pltpu.SemaphoreType.DMA((15,)),
        pltpu.SemaphoreType.DMA((3,)),
        pltpu.SemaphoreType.DMA((3,)),
        pltpu.SemaphoreType.DMA((19,)),
    ]
    factored, latent, log_density = pl.pallas_call(
        flow_kernel,
        out_shape=(
            jax.ShapeDtypeStruct((16, 1, 32, 128), F32),
            jax.ShapeDtypeStruct((16, 1, 32, 128), F32),
            jax.ShapeDtypeStruct((1, 1), F32),
        ),
        in_specs=specs,
        out_specs=(vmem, vmem, smem),
        scratch_shapes=buffers,
        compiler_params=pltpu.CompilerParams(
            collective_id=0, has_side_effects=True, vmem_limit_bytes=60 * 1024 * 1024
        ),
        name="flow",
    )(*operands)
    return factored, latent, log_density.reshape(())


def solution(mesh):
    assert mesh.shape["gz"] == GZ and mesh.shape["gy"] == GY
    in_specs = (P(None, "gz", "gy", None), P(), P(), P(), P(), P(), P(), P())
    out_specs = (P(None, "gz", "gy", None), P(None, "gz", "gy", None), P())
    return jax.shard_map(
        functools.partial(shards, tables()),
        mesh=mesh, in_specs=in_specs, out_specs=out_specs, check_vma=False,
    )
```

```python
import functools
import math

import jax
import jax.numpy as jnp
import ml_dtypes
import numpy as np
from jax import lax
from jax.experimental import pallas as pl
from jax.experimental.pallas import tpu as pltpu
from jax.sharding import PartitionSpec as P

MESH = pl.DeviceIdType.MESH
LOGICAL = pl.DeviceIdType.LOGICAL
F32 = jnp.float32
BF16 = jnp.bfloat16

SLOTS = 40
ROWS = 64
WIDE = 256
GZ = 32
GY = 4
COUNT = GZ * GY
OWN_ROWS = ROWS + 2
CHUNK = 16
CHUNKS = ROWS // CHUNK
GROUP = 6
GROUPS = OWN_ROWS // GROUP


def real_basis(length):
    cells = np.arange(length)
    rows = [np.full(length, 1.0 / math.sqrt(length))]
    for m in range(1, length // 2):
        rows.append(math.sqrt(2.0 / length) * np.cos(2.0 * math.pi * m * cells / length))
        rows.append(math.sqrt(2.0 / length) * np.sin(2.0 * math.pi * m * cells / length))
    rows.append(np.where(cells % 2 == 0, 1.0, -1.0) / math.sqrt(length))
    return np.stack(rows)


def split_pair(table):
    table = np.asarray(table, np.float32)
    high = table.astype(ml_dtypes.bfloat16)
    low = (table - high.astype(np.float32)).astype(ml_dtypes.bfloat16)
    return np.stack([high, low])


def tables():
    fx, fy, fz = real_basis(128), real_basis(128), real_basis(32)
    forward_x = np.zeros((128, 2, 128, 2))
    for k in range(2):
        forward_x[:, k, :, k] = fx
    forward_x = forward_x.reshape(256, 256)
    forward_z = np.einsum("kz,qp->qkzp", fz, np.eye(8)).reshape(256, 256)
    forward_y = np.einsum("kgy,cd->gcydk", fy.reshape(128, 4, 32), np.eye(4)).reshape(512, 512)
    spread = np.zeros((128, 2, 2, 128))
    for k in range(2):
        spread[np.arange(128), k, k, np.arange(128)] = 1.0
    spread = spread.reshape(256, 256).astype(ml_dtypes.bfloat16)
    pick = np.zeros((64, 4, 128))
    for plane in range(4):
        for c in range(2):
            for a in range(3):
                for b in range(3):
                    for e in range(3):
                        row = 27 * c + 9 * a + 3 * b + e
                        pick[row, plane, b * SLOTS + e * 12 + (a + plane) * 2 + c] = 1.0
        for piece in range(3):
            pick[54 + piece, plane, piece * SLOTS + 36] = 1.0
    pick = pick.reshape(64, 512).astype(ml_dtypes.bfloat16)
    half_z = (np.arange(32) + 1) // 2 / 32.0
    half_y = (np.arange(128) + 1) // 2 / 128.0
    squares = (half_z[:, None] ** 2 + half_y[None, :] ** 2).reshape(1, 4096).astype(np.float32)
    return {
        "forward_x": split_pair(forward_x),
        "forward_z": split_pair(forward_z),
        "backward_z": split_pair(forward_z.T),
        "forward_y": split_pair(forward_y),
        "backward_x": split_pair(fx.T),
        "spread": spread,
        "pick": pick,
        "squares": squares,
    }


def split2(values):
    high = values.astype(BF16)
    return high, (values - high.astype(F32)).astype(BF16)


def split3(values):
    high = values.astype(BF16)
    rest = values - high.astype(F32)
    mid = rest.astype(BF16)
    return high, mid, (rest - mid.astype(F32)).astype(BF16)


def mul(a, b, dims=((1,), (0,))):
    return lax.dot_general(a, b, (dims, ((), ())), preferred_element_type=F32)


def mul3(a, b, dims=((1,), (0,))):
    return mul(a[0], b[0], dims) + (mul(a[0], b[1], dims) + mul(a[1], b[0], dims))


def shift_right(values):
    lane = lax.broadcasted_iota(jnp.int32, values.shape, values.ndim - 1)
    return jnp.where(lane == 0, 0.0, pltpu.roll(values, 1, values.ndim - 1))


def shift_left(values):
    last = values.shape[-1] - 1
    lane = lax.broadcasted_iota(jnp.int32, values.shape, values.ndim - 1)
    return jnp.where(lane == last, 0.0, pltpu.roll(values, last, values.ndim - 1))


def flow_kernel(
    dens_hbm, first_w_hbm, first_b_hbm, middle_w_hbm, middle_b_hbm, output_w_hbm, output_b_hbm,
    radial_hbm, forward_x_hbm, forward_z_hbm, backward_z_hbm, forward_y_hbm, backward_x_hbm,
    spread_hbm, pick_hbm, squares_hbm,
    factored, latent, log_density,
    lower_send, edge_send, lower_prev, lower_next, edge_recv,
    window, hidden, acc0, acc1, wide_w, w1, w2, b2, w3, ow32, profile,
    x_send, z_recv, mixed, zb_send, x_recv,
    kept, first_held, last_held, sum_send, sum_recv, dens2,
    first_w, first_b, middle_w, middle_b, output_w, output_b,
    radial, forward_x, forward_z, backward_z, forward_y, backward_x, spread, pick, squares,
    halo_ssem, halo_rsem, all_ssem, all_rsem, in_sem,
):
    me_z = lax.axis_index("gz")
    me_y = lax.axis_index("gy")

    me = me_z * GY + me_y

    def near(step):
        return lax.rem(me + step, COUNT)

    def near_z(step):
        return lax.rem(me_z + step + GZ, GZ)

    def near_y(step):
        return lax.rem(me_y + step + GY, GY)

    barrier = pltpu.get_barrier_semaphore()
    sides = [(dz, dy) for dz in (-1, 0, 1) for dy in (-1, 0, 1) if (dz, dy) != (0, 0)]
    for dz, dy in sides:
        pl.semaphore_signal(
            barrier, inc=1, device_id=(near_z(dz), near_y(dy)), device_id_type=MESH
        )
    def fetch(src, dst, index):
        copy = pltpu.make_async_copy(src, dst, in_sem.at[index])
        copy.start()
        return copy

    lower_in = [
        fetch(
            dens_hbm.at[pl.ds(0, 2), :, :, pl.ds(half * 128, 128)],
            dens2.at[half, pl.ds(0, 2)], half,
        )
        for half in range(2)
    ]

    def greet(i, carry):
        pl.semaphore_signal(barrier, inc=1, device_id=near(i), device_id_type=LOGICAL)
        return carry

    lax.fori_loop(1, COUNT, greet, 0)

    for copy in lower_in:
        copy.wait()
    for z in range(2):
        for c in range(2):
            for half in range(2):
                lower_send[z, c, :, pl.ds(half * 128, 128)] = dens2[half, c, z].astype(BF16)
    for side in range(2):
        for row in range(2):
            for z in range(2):
                for c in range(2):
                    source_row = row if side == 0 else ROWS - 2 + row
                    for half in range(2):
                        line = dens2[half, c, z, pl.ds(source_row, 1), :]
                        edge_send[
                            side, pl.ds(row * 4 + z * 2 + c, 1), pl.ds(half * 128, 128)
                        ] = line.astype(BF16).astype(F32)

    pl.semaphore_wait(barrier, COUNT - 1 + len(sides))

    halo = []

    def halo_copy(src, dst, index, to):
        return pltpu.make_async_remote_copy(
            src_ref=src, dst_ref=dst, send_sem=halo_ssem.at[index], recv_sem=halo_rsem.at[index],
            device_id=to, device_id_type=MESH,
        )

    def chunk_copies(chunk):
        rows = pl.ds(pl.multiple_of(chunk * CHUNK, CHUNK), CHUNK)
        return (
            halo_copy(
                lower_send.at[:, :, rows], lower_next.at[:, :, rows], 6 + chunk,
                (near_z(-1), me_y),
            ),
            halo_copy(
                lower_send.at[1, :, rows], lower_prev.at[1, :, rows], 10 + chunk,
                (near_z(1), me_y),
            ),
        )

    def start_halo(copies):
        for copy in copies:
            copy.start()
            halo.append(copy)

    edges = [
        [
            halo_copy(
                edge_send.at[side], edge_recv.at[1 - side, 1 - dz], side * 3 + dz + 1,
                (near_z(dz), near_y(-1) if side == 0 else near_y(1)),
            )
            for dz in (-1, 0, 1)
        ]
        for side in range(2)
    ]
    far_plane = halo_copy(lower_send.at[0], lower_prev.at[0], 14, (near_z(1), me_y))
    start_halo(edges[1])
    start_halo(chunk_copies(0))
    start_halo(edges[0])
    for chunk in range(1, CHUNKS):
        start_halo(chunk_copies(chunk))
    start_halo([far_plane])

    weights_in = [
        fetch(src, dst, 2 + i)
        for i, (src, dst) in enumerate(
            (
                (first_w_hbm, first_w), (first_b_hbm, first_b), (pick_hbm, pick),
                (middle_w_hbm, middle_w), (middle_b_hbm, middle_b), (output_w_hbm, output_w),
            )
        )
    ]
    filter_in = [fetch(radial_hbm, radial, 8), fetch(squares_hbm, squares, 9)]
    late_in = [
        fetch(
            dens_hbm.at[pl.ds(2, 2), :, :, pl.ds(half * 128, 128)],
            dens2.at[half, pl.ds(2, 2)], 10 + half,
        )
        for half in range(2)
    ] + [
        fetch(src, dst, 12 + i)
        for i, (src, dst) in enumerate(
            (
                (output_b_hbm, output_b), (forward_x_hbm, forward_x), (forward_z_hbm, forward_z),
                (forward_y_hbm, forward_y), (backward_z_hbm, backward_z),
                (backward_x_hbm, backward_x), (spread_hbm, spread),
            )
        )
    ]

    for copy in weights_in:
        copy.wait()
    wide_w[...] = jnp.zeros_like(wide_w)
    wide_w[pl.ds(0, 54), :] = first_w[...].astype(F32)
    for piece, part in enumerate(split3(first_b[...])):
        wide_w[pl.ds(54 + piece, 1), :] = part.astype(F32)
    turned = jnp.transpose(wide_w[...]).astype(BF16)
    for plane in range(4):
        w1[pl.ds(plane * 128, 128), :] = mul(
            turned, pick[:, pl.ds(plane * 128, 128)]
        ).astype(BF16)
    w2[...] = jnp.transpose(middle_w[...].astype(F32)).astype(BF16)
    b2[...] = jnp.transpose(jnp.broadcast_to(middle_b[...], (128, 128)))
    ow32[...] = output_w[...].astype(F32)
    w3[...] = jnp.zeros_like(w3)
    for a in range(3):
        for b in range(3):
            w3[pl.ds(b * 16, 12), pl.ds(a * 128, 128)] = ow32[pl.ds(36 * a + 12 * b, 12), :]

    def put(first, count, slot, values):
        for e, shifted in enumerate((shift_right(values), values, shift_left(values))):
            for half in range(2):
                window[half, pl.ds(first * SLOTS + e * 12 + slot, count, stride=SLOTS), :] = shifted[
                    :, half * 128 : (half + 1) * 128
                ]

    for half in range(2):
        window[half, pl.ds(36, 72, stride=SLOTS), :] = jnp.ones((72, 128), F32)
        for slot in range(37, 40):
            window[half, pl.ds(slot, 72, stride=SLOTS), :] = jnp.zeros((72, 128), F32)
        window[half, pl.ds(68 * SLOTS, 36), :] = jnp.zeros((36, 128), F32)
        for slot in (0, 1, 12, 13, 24, 25):
            window[half, pl.ds(2 * SLOTS + slot, ROWS, stride=SLOTS), :] = jnp.zeros((ROWS, 128), F32)
    for z in range(2):
        for c in range(2):
            put(2, ROWS, (z + 2) * 2 + c, lower_send[z, c].astype(F32))

    step_x = (me + 1) // 2
    freq_x = step_x.astype(F32) * (1.0 / 128.0)
    for copy in filter_in:
        copy.wait()
    weights = radial[...]
    centres = lax.broadcasted_iota(jnp.int32, (32, 512), 0).astype(F32)

    def filter_part(part, carry):
        lanes = pl.ds(pl.multiple_of(part * 512, 512), 512)
        kappa = jnp.sqrt(squares[:, lanes] + freq_x * freq_x) * (2.0 / math.sqrt(3.0))
        scaled = kappa * 31.0 - centres
        basis = jnp.exp(-scaled * scaled)
        values = mul3(split2(weights), split2(basis))
        for j in range(4):
            profile[pl.ds(part * 4 + j, 128, stride=32), :] = values[:, j * 128 : (j + 1) * 128]
        return carry

    lax.fori_loop(0, 8, filter_part, 0)

    for copy in late_in:
        copy.wait()

    has_prev = me_z > 0
    has_next = me_z < GZ - 1
    has_up = me_y > 0
    has_down = me_y < GY - 1

    def fill_chunk(chunk):
        for copy in chunk_copies(chunk):
            copy.wait_recv()
        rows = pl.ds(pl.multiple_of(chunk * CHUNK, CHUNK), CHUNK)
        first = 2 + chunk * CHUNK
        for c in range(2):
            values = lower_prev[1, c, rows, :].astype(F32)
            put(first, CHUNK, 2 + c, jnp.where(has_prev, values, 0.0))
            for z in range(2):
                values = lower_next[z, c, rows, :].astype(F32)
                put(first, CHUNK, (z + 4) * 2 + c, jnp.where(has_next, values, 0.0))

    def fill_edge(side):
        for copy in edges[1 - side]:
            copy.wait_recv()
        for offset in range(3):
            valid = has_up if side == 0 else has_down
            if offset == 0:
                valid = jnp.logical_and(valid, has_prev)
            if offset == 2:
                valid = jnp.logical_and(valid, has_next)
            for row in range(2):
                lines = edge_recv[side, offset, pl.ds(row * 4, 4), :]
                lines = jnp.where(valid, lines, 0.0)
                at = (row if side == 0 else ROWS + 2 + row) * SLOTS + offset * 4
                for e, shifted in enumerate((shift_right(lines), lines, shift_left(lines))):
                    for half in range(2):
                        window[half, pl.ds(at + e * 12, 4), :] = shifted[
                            :, half * 128 : (half + 1) * 128
                        ]

    fill_edge(0)
    fill_chunk(0)

    w3_lane = lax.broadcasted_iota(jnp.int32, (48, 384), 1)
    w3_first = jnp.where(jnp.logical_and(w3_lane < 128, me_z == 0), 0.0, w3[...]).astype(BF16)
    w3_second = jnp.where(
        jnp.logical_and(w3_lane >= 256, me_z == GZ - 1), 0.0, w3[...]
    ).astype(BF16)

    def columns(r):
        start = pl.multiple_of((r - 1) * SLOTS, 8)
        return jnp.concatenate(
            [window[0, pl.ds(start, 128), :], window[1, pl.ds(start, 128), :]], axis=1
        ).astype(BF16)

    def second(first_layer):
        values = mul(w2[...], first_layer) + jnp.concatenate([b2[...]] * 2, axis=1)
        return jnp.maximum(values, 0.0).astype(BF16)

    def add_taps(acc, r, taps):
        valid = jnp.logical_not(
            jnp.logical_or(
                jnp.logical_and(r == 1, me_y == 0),
                jnp.logical_and(r == OWN_ROWS, me_y == GY - 1),
            )
        )
        taps = jnp.where(valid, taps, 0.0)
        for half in range(2):
            part = taps[:, half * 128 : (half + 1) * 128]
            at = [pl.ds(pl.multiple_of((r + 1 - b) * 16, 16), 16) for b in range(3)]
            acc[half, at[0], :] = part[0:16]
            acc[half, at[1], :] += part[16:32]
            acc[half, at[2], :] += part[32:48]

    for acc in (acc0, acc1):
        for half in range(2):
            acc[half, pl.ds(0, 32), :] = jnp.zeros((32, 128), F32)

    def group_rows(group):
        return [(sub, group * GROUP + 1 + sub) for sub in range(GROUP)]

    def later_first(group):
        for sub, r in group_rows(group):
            values = mul(w1[pl.ds(128, 384), :], columns(r))
            first_held[sub] = jnp.maximum(values, 0.0).astype(BF16)

    def later_second(group):
        for sub, r in group_rows(group):
            first_layer = first_held[sub]
            layers = [second(first_layer[p * 128 : (p + 1) * 128]) for p in range(3)]
            hidden[r] = jnp.concatenate(layers[0:2], axis=0)
            last_held[sub] = layers[2]

    def later_last(group):
        for sub, r in group_rows(group):
            stacked = jnp.concatenate([hidden[r], last_held[sub]], axis=0)
            add_taps(acc1, r, mul(w3_second, stacked))

    def early_first(group):
        for sub, r in group_rows(group):
            values = mul(w1[pl.ds(0, 128), :], columns(r))
            first_held[sub, pl.ds(0, 128)] = jnp.maximum(values, 0.0).astype(BF16)

    def early_second(group):
        for sub, r in group_rows(group):
            last_held[sub] = second(first_held[sub, pl.ds(0, 128)])

    def early_last(group):
        for sub, r in group_rows(group):
            stacked = jnp.concatenate([last_held[sub], hidden[r]], axis=0)
            add_taps(acc0, r, mul(w3_first, stacked))

    def start_groups(first, middle, last):
        first(0)
        middle(0)
        first(1)

    def run_groups(first, middle, last, begin, end):
        def step(group, carry):
            last(group - 2)
            middle(group - 1)
            first(group)
            return carry

        lax.fori_loop(begin, end, step, 0)

    def end_groups(first, middle, last):
        last(GROUPS - 2)
        middle(GROUPS - 1)
        last(GROUPS - 1)

    later = (later_first, later_second, later_last)
    early = (early_first, early_second, early_last)

    start_groups(*later)
    fill_edge(1)

    def later_chunk(chunk, carry):
        fill_chunk(chunk)
        run_groups(*later, 3 * chunk - 1, 3 * chunk + 2)
        return carry

    lax.fori_loop(1, CHUNKS, later_chunk, 0)
    end_groups(*later)

    def couple(acc, z, parity):
        raw = []
        for o in range(4):
            taps = [
                jnp.concatenate(
                    [
                        acc[half, pl.ds((2 + parity) * 16 + e * 4 + o, 32, stride=32), :]
                        for half in range(2)
                    ],
                    axis=1,
                )
                for e in range(3)
            ]
            raw.append(shift_right(taps[0]) + taps[1] + shift_left(taps[2]) + output_b[o])
        lines = [
            jnp.concatenate(
                [
                    dens2[half, c, z, pl.ds(parity, 32, stride=2), :]
                    for half in range(2)
                ],
                axis=1,
            )
            for c in range(4)
        ]
        scales = [jnp.tanh(raw[0]), jnp.tanh(raw[1])]
        for o in range(2):
            lines[2 + o] = lines[2 + o] * jnp.exp(scales[o]) + raw[2 + o]
        return jnp.concatenate(lines, axis=0), scales[0] + scales[1]

    def spread_x(values):
        high, mid, low = split3(values)
        return mul(high, spread[...]) + (mul(mid, spread[...]) + mul(low, spread[...]))

    def fold(values):
        rows, lanes = values.shape
        total = values[:, 0:128]
        for at in range(128, lanes, 128):
            total = total + values[:, at : at + 128]
        return jnp.sum(total.reshape(rows // 8, 8, 128), axis=0)

    source, scale_sum = couple(acc1, 1, 0)
    kept[0] = source
    total = fold(scale_sum)
    x_modes = mul3(
        (forward_x[0], forward_x[1]), split2(source), ((1,), (1,))
    )
    x_send[...] = x_modes.reshape(COUNT, 2, 128)

    sent = list(halo)

    def send_one(part, dst, stage, step):
        to = near(step)
        pltpu.make_async_remote_copy(
            src_ref=part(to), dst_ref=dst.at[me], send_sem=all_ssem.at[stage],
            recv_sem=all_rsem.at[stage], device_id=to, device_id_type=LOGICAL,
        ).start()

    def send_all(part, dst, stage):
        def one(i, carry):
            send_one(part, dst, stage, i)
            return carry

        lax.fori_loop(1, COUNT, one, 0)
        dst[me] = part(me)[...]

    def wait_all(dst, stage):
        copy = pltpu.make_async_remote_copy(
            src_ref=dst.at[pl.ds(0, COUNT - 1)], dst_ref=dst.at[pl.ds(0, COUNT - 1)],
            send_sem=all_ssem.at[stage], recv_sem=all_rsem.at[stage],
            device_id=near(1), device_id_type=LOGICAL,
        )
        copy.wait_recv()
        sent.append(copy)

    def x_part(to):
        return x_send.at[to]

    send_all(x_part, z_recv, 0)
    far_plane.wait_recv()
    for c in range(2):
        put(2, ROWS, c, jnp.where(has_prev, lower_prev[0, c].astype(F32), 0.0))
    start_groups(*early)
    run_groups(*early, 2, 6)
    kept[1], scale_sum = couple(acc1, 1, 1)
    total = total + fold(scale_sum)
    wait_all(z_recv, 0)

    z_modes = mul3((forward_z[0], forward_z[1]), split2(z_recv[...].reshape(256, 128)))

    lines = jnp.concatenate([z_modes[g * 64 : (g + 1) * 64] for g in range(GY)], axis=1)
    modes = mul3(split2(lines), (forward_y[0], forward_y[1]))
    parts = [
        modes[k * 32 : (k + 1) * 32, c * 128 : (c + 1) * 128] for k in range(2) for c in range(4)
    ]
    for o in range(16):
        value = profile[pl.ds(o * 256, 32), :] * parts[0]
        for c in range(1, 8):
            value = value + profile[pl.ds(o * 256 + c * 32, 32), :] * parts[c]
        mixed[pl.ds((o // 4) * 32, 32), pl.ds((o % 4) * 128, 128)] = value
    back = mul3(split2(mixed[...]), (forward_y[0], forward_y[1]), ((1,), (1,)))
    for pair in range(2):
        lines = jnp.concatenate(
            [back[:, g * 128 : (g + 1) * 128] for g in (2 * pair, 2 * pair + 1)], axis=0
        )
        planes = mul3((backward_z[0], backward_z[1]), split2(lines))
        zb_send[:, pl.ds(pair * 2, 2)] = planes.reshape(GZ, 2, 4, 128)

    send_all(lambda to: zb_send.at[to // GY, lax.rem(to, GY)], x_recv, 1)

    run_groups(*early, 6, GROUPS)
    end_groups(*early)
    squares_sum = fold(kept[0] * kept[0])
    for parity in range(2):
        coupled, scale_sum = couple(acc0, 0, parity)
        kept[2 + parity] = coupled
        total = total + fold(scale_sum)
        squares_sum = squares_sum + fold(coupled * coupled)
    target = spread_x(kept[1])
    wait_all(x_recv, 1)

    shifts = []
    for og in range(4):
        lines = x_recv[:, og, :]
        shifts.append(jnp.transpose(mul3((backward_x[0], backward_x[1]), split2(lines))))
    for k in range(2):
        scale = jnp.tanh(shifts[k])
        total = total + fold(scale)
        moved = target[:, k * 128 : (k + 1) * 128] * jnp.exp(scale) + shifts[2 + k]
        squares_sum = squares_sum + fold(moved * moved)
        latent[pl.ds(8 + k * 4, 4), 0] = moved.reshape(4, 32, 128)

    total = total - 0.5 * squares_sum
    sum_send[0] = jnp.sum(total, axis=0, keepdims=True)

    send_all(lambda to: sum_send.at[0], sum_recv, 2)
    for parity in range(2):
        coupled = spread_x(kept[2 + parity])
        for k in range(2):
            at = (2 * parity + k) * 4
            factored[pl.ds(at, 4), 0] = coupled[:, k * 128 : (k + 1) * 128].reshape(4, 32, 128)
    source = spread_x(kept[0])
    for k in range(2):
        latent[pl.ds(k * 4, 4), 0] = source[:, k * 128 : (k + 1) * 128].reshape(4, 32, 128)
    wait_all(sum_recv, 2)
    total = jnp.sum(sum_recv[...], axis=0)
    for copy in sent:
        copy.wait_send()
    count = 4.0 * 64 * 256 * 256
    log_density[0, 0] = jnp.sum(total) / count - 0.5 * math.log(2.0 * math.pi)


def shards(consts, density_field, first_weight, first_bias, middle_weight, middle_bias, output_weight, output_bias, radial_weights):
    vmem = pl.BlockSpec(memory_space=pltpu.VMEM)
    smem = pl.BlockSpec(memory_space=pltpu.SMEM)
    hbm = pl.BlockSpec(memory_space=pltpu.HBM)
    operands = [
        density_field, first_weight, first_bias.reshape(1, 128), middle_weight,
        middle_bias.reshape(1, 128), output_weight, output_bias, radial_weights.reshape(128, 32),
    ] + [jnp.asarray(value) for value in consts.values()]
    specs = [hbm] * len(operands)
    held = [pltpu.VMEM(value.shape, value.dtype) for value in operands]
    held[6] = pltpu.SMEM(output_bias.shape, F32)
    buffers = [
        pltpu.VMEM((2, 2, ROWS, WIDE), BF16),
        pltpu.VMEM((2, 8, WIDE), F32),
        pltpu.VMEM((2, 2, ROWS, WIDE), BF16),
        pltpu.VMEM((2, 2, ROWS, WIDE), BF16),
        pltpu.VMEM((2, 3, 8, WIDE), F32),
        pltpu.VMEM((2, 72 * SLOTS, 128), F32),
        pltpu.VMEM((OWN_ROWS + 2, 256, WIDE), BF16),
        pltpu.VMEM((2, 70 * 16, 128), F32),
        pltpu.VMEM((2, 70 * 16, 128), F32),
        pltpu.VMEM((64, 128), F32),
        pltpu.VMEM((512, 128), BF16),
        pltpu.VMEM((128, 128), BF16),
        pltpu.VMEM((128, 128), F32),
        pltpu.VMEM((48, 384), F32),
        pltpu.VMEM((108, 128), F32),
        pltpu.VMEM((128 * 32, 128), F32),
        pltpu.VMEM((COUNT, 2, 128), F32),
        pltpu.VMEM((COUNT, 2, 128), F32),
        pltpu.VMEM((128, 512), F32),
        pltpu.VMEM((GZ, GY, 4, 128), F32),
        pltpu.VMEM((COUNT, 4, 128), F32),
        pltpu.VMEM((4, 128, WIDE), F32),
        pltpu.VMEM((GROUP, 384, WIDE), BF16),
        pltpu.VMEM((GROUP, 128, WIDE), BF16),
        pltpu.VMEM((1, 1, 128), F32),
        pltpu.VMEM((COUNT, 1, 128), F32),
        pltpu.VMEM((2, 4, 2, ROWS, 128), F32),
    ] + held[1:] + [
        pltpu.SemaphoreType.DMA((15,)),
        pltpu.SemaphoreType.DMA((15,)),
        pltpu.SemaphoreType.DMA((3,)),
        pltpu.SemaphoreType.DMA((3,)),
        pltpu.SemaphoreType.DMA((19,)),
    ]
    operands = [pltpu.with_memory_space_constraint(value, pltpu.HBM) for value in operands]
    factored, latent, log_density = pl.pallas_call(
        flow_kernel,
        out_shape=(
            jax.ShapeDtypeStruct((16, 1, 32, 128), F32),
            jax.ShapeDtypeStruct((16, 1, 32, 128), F32),
            jax.ShapeDtypeStruct((1, 1), F32),
        ),
        in_specs=specs,
        out_specs=(vmem, vmem, smem),
        scratch_shapes=buffers,
        compiler_params=pltpu.CompilerParams(
            collective_id=0, has_side_effects=True, vmem_limit_bytes=52 * 1024 * 1024
        ),
        name="flow",
    )(*operands)
    return factored, latent, log_density.reshape(())


def solution(mesh):
    assert mesh.shape["gz"] == GZ and mesh.shape["gy"] == GY
    in_specs = (P(None, "gz", "gy", None), P(), P(), P(), P(), P(), P(), P())
    out_specs = (P(None, "gz", "gy", None), P(None, "gz", "gy", None), P())
    return jax.shard_map(
        functools.partial(shards, tables()),
        mesh=mesh, in_specs=in_specs, out_specs=out_specs, check_vma=False,
    )
```

```python
import functools
import math

import jax
import jax.numpy as jnp
import ml_dtypes
import numpy as np
from jax import lax
from jax.experimental import pallas as pl
from jax.experimental.pallas import tpu as pltpu
from jax.sharding import PartitionSpec as P

MESH = pl.DeviceIdType.MESH
LOGICAL = pl.DeviceIdType.LOGICAL
F32 = jnp.float32
BF16 = jnp.bfloat16

SLOTS = 40
ROWS = 64
WIDE = 256
GZ = 32
GY = 4
COUNT = GZ * GY
OWN_ROWS = ROWS + 2
CHUNK = 16
CHUNKS = ROWS // CHUNK
GROUP = 11
GROUPS = OWN_ROWS // GROUP


def real_basis(length):
    cells = np.arange(length)
    rows = [np.full(length, 1.0 / math.sqrt(length))]
    for m in range(1, length // 2):
        rows.append(math.sqrt(2.0 / length) * np.cos(2.0 * math.pi * m * cells / length))
        rows.append(math.sqrt(2.0 / length) * np.sin(2.0 * math.pi * m * cells / length))
    rows.append(np.where(cells % 2 == 0, 1.0, -1.0) / math.sqrt(length))
    return np.stack(rows)


def split_pair(table):
    table = np.asarray(table, np.float32)
    high = table.astype(ml_dtypes.bfloat16)
    low = (table - high.astype(np.float32)).astype(ml_dtypes.bfloat16)
    return np.stack([high, low])


def tables():
    fx, fy, fz = real_basis(128), real_basis(128), real_basis(32)
    forward_x = np.zeros((128, 2, 128, 2))
    for k in range(2):
        forward_x[:, k, :, k] = fx
    forward_x = forward_x.reshape(256, 256)
    forward_z = np.einsum("kz,qp->qkzp", fz, np.eye(8)).reshape(256, 256)
    forward_y = np.einsum("kgy,cd->gcydk", fy.reshape(128, 4, 32), np.eye(4)).reshape(512, 512)
    spread = np.zeros((128, 2, 2, 128))
    for k in range(2):
        spread[np.arange(128), k, k, np.arange(128)] = 1.0
    spread = spread.reshape(256, 256).astype(ml_dtypes.bfloat16)
    pick = np.zeros((64, 4, 128))
    for plane in range(4):
        for c in range(2):
            for a in range(3):
                for b in range(3):
                    for e in range(3):
                        row = 27 * c + 9 * a + 3 * b + e
                        pick[row, plane, b * SLOTS + e * 12 + (a + plane) * 2 + c] = 1.0
        for piece in range(3):
            pick[54 + piece, plane, piece * SLOTS + 36] = 1.0
    pick = pick.reshape(64, 512).astype(ml_dtypes.bfloat16)
    half_z = (np.arange(32) + 1) // 2 / 32.0
    half_y = (np.arange(128) + 1) // 2 / 128.0
    squares = (half_z[:, None] ** 2 + half_y[None, :] ** 2).reshape(1, 4096).astype(np.float32)
    return {
        "forward_x": split_pair(forward_x),
        "forward_z": split_pair(forward_z),
        "backward_z": split_pair(forward_z.T),
        "forward_y": split_pair(forward_y),
        "backward_x": split_pair(fx.T),
        "spread": spread,
        "pick": pick,
        "squares": squares,
    }


def split2(values):
    high = values.astype(BF16)
    return high, (values - high.astype(F32)).astype(BF16)


def split3(values):
    high = values.astype(BF16)
    rest = values - high.astype(F32)
    mid = rest.astype(BF16)
    return high, mid, (rest - mid.astype(F32)).astype(BF16)


def mul(a, b, dims=((1,), (0,))):
    return lax.dot_general(a, b, (dims, ((), ())), preferred_element_type=F32)


def table_times(table, values):
    high, low = split2(values)
    columns = values.shape[1]
    both = mul(table[0], jnp.concatenate([high, low], axis=1))
    return both[:, :columns] + (both[:, columns:] + mul(table[1], high))


def times_table(values, table, turned=False):
    dims = ((1,), (1,)) if turned else ((1,), (0,))
    high, low = split2(values)
    rows = values.shape[0]
    both = mul(jnp.concatenate([high, low], axis=0), table[0], dims)
    return both[:rows] + (both[rows:] + mul(high, table[1], dims))


def shift_right(values):
    lane = lax.broadcasted_iota(jnp.int32, values.shape, values.ndim - 1)
    return jnp.where(lane == 0, 0.0, pltpu.roll(values, 1, values.ndim - 1))


def shift_left(values):
    last = values.shape[-1] - 1
    lane = lax.broadcasted_iota(jnp.int32, values.shape, values.ndim - 1)
    return jnp.where(lane == last, 0.0, pltpu.roll(values, last, values.ndim - 1))


def flow_kernel(
    dens_hbm, first_w_hbm, first_b_hbm, middle_w_hbm, middle_b_hbm, output_w_hbm, output_b_hbm,
    radial_hbm, forward_x_hbm, forward_z_hbm, backward_z_hbm, forward_y_hbm, backward_x_hbm,
    spread_hbm, pick_hbm, squares_hbm,
    factored, latent, log_density,
    lower_send, edge_send, lower_prev, lower_next, edge_recv,
    window, hidden, acc0, acc1, wide_w, w1, w2, b2, w3, ow32, profile,
    x_send, z_recv, mixed, zb_send, x_recv,
    kept, first_held, last_held, sum_send, sum_recv, dens2,
    first_w, first_b, middle_w, middle_b, output_w, output_b,
    radial, forward_x, forward_z, backward_z, forward_y, backward_x, spread, pick, squares,
    halo_ssem, halo_rsem, all_ssem, all_rsem, in_sem,
):
    me_z = lax.axis_index("gz")
    me_y = lax.axis_index("gy")

    me = me_z * GY + me_y

    def near(step):
        return lax.rem(me + step, COUNT)

    def near_z(step):
        return lax.rem(me_z + step + GZ, GZ)

    def near_y(step):
        return lax.rem(me_y + step + GY, GY)

    barrier = pltpu.get_barrier_semaphore()
    sides = [(dz, dy) for dz in (-1, 0, 1) for dy in (-1, 0, 1) if (dz, dy) != (0, 0)]
    for dz, dy in sides:
        pl.semaphore_signal(
            barrier, inc=1, device_id=(near_z(dz), near_y(dy)), device_id_type=MESH
        )
    def fetch(src, dst, index):
        copy = pltpu.make_async_copy(src, dst, in_sem.at[index])
        copy.start()
        return copy

    lower_in = [
        fetch(
            dens_hbm.at[pl.ds(0, 2), :, :, pl.ds(half * 128, 128)],
            dens2.at[half, pl.ds(0, 2)], half,
        )
        for half in range(2)
    ]

    def greet(i, carry):
        pl.semaphore_signal(barrier, inc=1, device_id=near(i), device_id_type=LOGICAL)
        return carry

    lax.fori_loop(1, COUNT, greet, 0)

    for copy in lower_in:
        copy.wait()
    for z in range(2):
        for c in range(2):
            for half in range(2):
                lower_send[z, c, :, pl.ds(half * 128, 128)] = dens2[half, c, z].astype(BF16)
    for side in range(2):
        for row in range(2):
            for z in range(2):
                for c in range(2):
                    source_row = row if side == 0 else ROWS - 2 + row
                    for half in range(2):
                        line = dens2[half, c, z, pl.ds(source_row, 1), :]
                        edge_send[
                            side, pl.ds(row * 4 + z * 2 + c, 1), pl.ds(half * 128, 128)
                        ] = line.astype(BF16).astype(F32)

    pl.semaphore_wait(barrier, COUNT - 1 + len(sides))

    halo = []

    def halo_copy(src, dst, index, to):
        return pltpu.make_async_remote_copy(
            src_ref=src, dst_ref=dst, send_sem=halo_ssem.at[index], recv_sem=halo_rsem.at[index],
            device_id=to, device_id_type=MESH,
        )

    def chunk_copies(chunk):
        rows = pl.ds(pl.multiple_of(chunk * CHUNK, CHUNK), CHUNK)
        return (
            halo_copy(
                lower_send.at[:, :, rows], lower_next.at[:, :, rows], 6 + chunk,
                (near_z(-1), me_y),
            ),
            halo_copy(
                lower_send.at[1, :, rows], lower_prev.at[1, :, rows], 10 + chunk,
                (near_z(1), me_y),
            ),
        )

    def start_halo(copies):
        for copy in copies:
            copy.start()
            halo.append(copy)

    edges = [
        [
            halo_copy(
                edge_send.at[side], edge_recv.at[1 - side, 1 - dz], side * 3 + dz + 1,
                (near_z(dz), near_y(-1) if side == 0 else near_y(1)),
            )
            for dz in (-1, 0, 1)
        ]
        for side in range(2)
    ]
    far_plane = halo_copy(lower_send.at[0], lower_prev.at[0], 14, (near_z(1), me_y))
    start_halo(edges[1])
    start_halo(chunk_copies(0))
    start_halo(edges[0])
    for chunk in range(1, CHUNKS):
        start_halo(chunk_copies(chunk))
    start_halo([far_plane])

    weights_in = [
        fetch(src, dst, 2 + i)
        for i, (src, dst) in enumerate(
            (
                (first_w_hbm, first_w), (first_b_hbm, first_b), (pick_hbm, pick),
                (middle_w_hbm, middle_w), (middle_b_hbm, middle_b), (output_w_hbm, output_w),
            )
        )
    ]
    filter_in = [fetch(radial_hbm, radial, 8), fetch(squares_hbm, squares, 9)]
    late_in = [
        fetch(
            dens_hbm.at[pl.ds(2, 2), :, :, pl.ds(half * 128, 128)],
            dens2.at[half, pl.ds(2, 2)], 10 + half,
        )
        for half in range(2)
    ] + [
        fetch(src, dst, 12 + i)
        for i, (src, dst) in enumerate(
            (
                (output_b_hbm, output_b), (forward_x_hbm, forward_x), (forward_z_hbm, forward_z),
                (forward_y_hbm, forward_y), (backward_z_hbm, backward_z),
                (backward_x_hbm, backward_x), (spread_hbm, spread),
            )
        )
    ]

    for copy in weights_in:
        copy.wait()
    wide_w[...] = jnp.zeros_like(wide_w)
    wide_w[pl.ds(0, 54), :] = first_w[...].astype(F32)
    for piece, part in enumerate(split3(first_b[...])):
        wide_w[pl.ds(54 + piece, 1), :] = part.astype(F32)
    turned = jnp.transpose(wide_w[...]).astype(BF16)
    for plane in range(4):
        w1[pl.ds(plane * 128, 128), :] = mul(
            turned, pick[:, pl.ds(plane * 128, 128)]
        ).astype(BF16)
    w2[...] = jnp.transpose(middle_w[...].astype(F32)).astype(BF16)
    b2[...] = jnp.transpose(jnp.broadcast_to(middle_b[...], (128, 128)))
    ow32[...] = output_w[...].astype(F32)
    w3[...] = jnp.zeros_like(w3)
    for a in range(3):
        for b in range(3):
            w3[pl.ds(b * 16, 12), pl.ds(a * 128, 128)] = ow32[pl.ds(36 * a + 12 * b, 12), :]

    def put(first, count, slot, values):
        for e, shifted in enumerate((shift_right(values), values, shift_left(values))):
            for half in range(2):
                window[half, pl.ds(first * SLOTS + e * 12 + slot, count, stride=SLOTS), :] = shifted[
                    :, half * 128 : (half + 1) * 128
                ]

    for half in range(2):
        window[half, pl.ds(36, 72, stride=SLOTS), :] = jnp.ones((72, 128), F32)
        for slot in range(37, 40):
            window[half, pl.ds(slot, 72, stride=SLOTS), :] = jnp.zeros((72, 128), F32)
        window[half, pl.ds(68 * SLOTS, 36), :] = jnp.zeros((36, 128), F32)
        for slot in (0, 1, 12, 13, 24, 25):
            window[half, pl.ds(2 * SLOTS + slot, ROWS, stride=SLOTS), :] = jnp.zeros((ROWS, 128), F32)
    for z in range(2):
        for c in range(2):
            put(2, ROWS, (z + 2) * 2 + c, lower_send[z, c].astype(F32))

    step_x = (me + 1) // 2
    freq_x = step_x.astype(F32) * (1.0 / 128.0)
    for copy in filter_in:
        copy.wait()
    weights = radial[...]
    centres = lax.broadcasted_iota(jnp.int32, (32, 512), 0).astype(F32)

    def filter_part(part, carry):
        lanes = pl.ds(pl.multiple_of(part * 512, 512), 512)
        kappa = jnp.sqrt(squares[:, lanes] + freq_x * freq_x) * (2.0 / math.sqrt(3.0))
        scaled = kappa * 31.0 - centres
        basis = jnp.exp(-scaled * scaled)
        values = table_times(split2(weights), basis)
        for j in range(4):
            profile[pl.ds(part * 4 + j, 128, stride=32), :] = values[:, j * 128 : (j + 1) * 128]
        return carry

    lax.fori_loop(0, 8, filter_part, 0)

    for copy in late_in:
        copy.wait()

    has_prev = me_z > 0
    has_next = me_z < GZ - 1
    has_up = me_y > 0
    has_down = me_y < GY - 1

    def fill_chunk(chunk):
        for copy in chunk_copies(chunk):
            copy.wait_recv()
        rows = pl.ds(pl.multiple_of(chunk * CHUNK, CHUNK), CHUNK)
        first = 2 + chunk * CHUNK
        for c in range(2):
            values = lower_prev[1, c, rows, :].astype(F32)
            put(first, CHUNK, 2 + c, jnp.where(has_prev, values, 0.0))
            for z in range(2):
                values = lower_next[z, c, rows, :].astype(F32)
                put(first, CHUNK, (z + 4) * 2 + c, jnp.where(has_next, values, 0.0))

    def fill_edge(side):
        for copy in edges[1 - side]:
            copy.wait_recv()
        for offset in range(3):
            valid = has_up if side == 0 else has_down
            if offset == 0:
                valid = jnp.logical_and(valid, has_prev)
            if offset == 2:
                valid = jnp.logical_and(valid, has_next)
            for row in range(2):
                lines = edge_recv[side, offset, pl.ds(row * 4, 4), :]
                lines = jnp.where(valid, lines, 0.0)
                at = (row if side == 0 else ROWS + 2 + row) * SLOTS + offset * 4
                for e, shifted in enumerate((shift_right(lines), lines, shift_left(lines))):
                    for half in range(2):
                        window[half, pl.ds(at + e * 12, 4), :] = shifted[
                            :, half * 128 : (half + 1) * 128
                        ]

    fill_edge(0)
    fill_chunk(0)

    w3_lane = lax.broadcasted_iota(jnp.int32, (48, 384), 1)
    w3_first = jnp.where(jnp.logical_and(w3_lane < 128, me_z == 0), 0.0, w3[...]).astype(BF16)
    w3_second = jnp.where(
        jnp.logical_and(w3_lane >= 256, me_z == GZ - 1), 0.0, w3[...]
    ).astype(BF16)

    def columns(r):
        start = pl.multiple_of((r - 1) * SLOTS, 8)
        return jnp.concatenate(
            [window[0, pl.ds(start, 128), :], window[1, pl.ds(start, 128), :]], axis=1
        ).astype(BF16)

    def second(first_layer):
        values = mul(w2[...], first_layer) + jnp.concatenate([b2[...]] * 2, axis=1)
        return jnp.maximum(values, 0.0).astype(BF16)

    def add_taps(acc, r, taps):
        valid = jnp.logical_not(
            jnp.logical_or(
                jnp.logical_and(r == 1, me_y == 0),
                jnp.logical_and(r == OWN_ROWS, me_y == GY - 1),
            )
        )
        taps = jnp.where(valid, taps, 0.0)
        for half in range(2):
            part = taps[:, half * 128 : (half + 1) * 128]
            at = [pl.ds(pl.multiple_of((r + 1 - b) * 16, 16), 16) for b in range(3)]
            acc[half, at[0], :] = part[0:16]
            acc[half, at[1], :] += part[16:32]
            acc[half, at[2], :] += part[32:48]

    for acc in (acc0, acc1):
        for half in range(2):
            acc[half, pl.ds(0, 32), :] = jnp.zeros((32, 128), F32)

    def group_rows(group):
        return [(sub, group * GROUP + 1 + sub) for sub in range(GROUP)]

    def later_first(group):
        for sub, r in group_rows(group):
            values = mul(w1[pl.ds(128, 384), :], columns(r))
            first_held[sub] = jnp.maximum(values, 0.0).astype(BF16)

    def later_second(group):
        for sub, r in group_rows(group):
            first_layer = first_held[sub]
            layers = [second(first_layer[p * 128 : (p + 1) * 128]) for p in range(3)]
            hidden[r] = jnp.concatenate(layers[0:2], axis=0)
            last_held[sub] = layers[2]

    def later_last(group):
        for sub, r in group_rows(group):
            stacked = jnp.concatenate([hidden[r], last_held[sub]], axis=0)
            add_taps(acc1, r, mul(w3_second, stacked))

    def early_first(group):
        for sub, r in group_rows(group):
            values = mul(w1[pl.ds(0, 128), :], columns(r))
            first_held[sub, pl.ds(0, 128)] = jnp.maximum(values, 0.0).astype(BF16)

    def early_second(group):
        for sub, r in group_rows(group):
            last_held[sub] = second(first_held[sub, pl.ds(0, 128)])

    def early_last(group):
        for sub, r in group_rows(group):
            stacked = jnp.concatenate([last_held[sub], hidden[r]], axis=0)
            add_taps(acc0, r, mul(w3_first, stacked))

    def start_groups(first, middle, last):
        first(0)
        middle(0)
        first(1)

    def run_groups(first, middle, last, begin, end):
        def step(group, carry):
            last(group - 2)
            middle(group - 1)
            first(group)
            return carry

        lax.fori_loop(begin, end, step, 0)

    def end_groups(first, middle, last):
        last(GROUPS - 2)
        middle(GROUPS - 1)
        last(GROUPS - 1)

    later = (later_first, later_second, later_last)
    early = (early_first, early_second, early_last)

    later_first(0)
    fill_edge(1)
    fill_chunk(1)
    later_second(0)
    later_first(1)
    fill_chunk(2)
    run_groups(*later, 2, 4)
    fill_chunk(3)
    run_groups(*later, 4, GROUPS)
    end_groups(*later)

    def couple(acc, z, parity):
        raw = []
        for o in range(4):
            taps = [
                jnp.concatenate(
                    [
                        acc[half, pl.ds((2 + parity) * 16 + e * 4 + o, 32, stride=32), :]
                        for half in range(2)
                    ],
                    axis=1,
                )
                for e in range(3)
            ]
            raw.append(shift_right(taps[0]) + taps[1] + shift_left(taps[2]) + output_b[o])
        lines = [
            jnp.concatenate(
                [
                    dens2[half, c, z, pl.ds(parity, 32, stride=2), :]
                    for half in range(2)
                ],
                axis=1,
            )
            for c in range(4)
        ]
        scales = [jnp.tanh(raw[0]), jnp.tanh(raw[1])]
        for o in range(2):
            lines[2 + o] = lines[2 + o] * jnp.exp(scales[o]) + raw[2 + o]
        return jnp.concatenate(lines, axis=0), scales[0] + scales[1]

    def spread_x(values):
        high, mid, low = split3(values)
        return mul(high, spread[...]) + (mul(mid, spread[...]) + mul(low, spread[...]))

    def fold(values):
        rows, lanes = values.shape
        total = values[:, 0:128]
        for at in range(128, lanes, 128):
            total = total + values[:, at : at + 128]
        return jnp.sum(total.reshape(rows // 8, 8, 128), axis=0)

    source, scale_sum = couple(acc1, 1, 0)
    kept[0] = source
    total = fold(scale_sum)
    high, low = split2(source)
    both = mul(forward_x[0], jnp.concatenate([high, low], axis=0), ((1,), (1,)))
    x_modes = both[:, :128] + (both[:, 128:] + mul(forward_x[1], high, ((1,), (1,))))
    x_send[...] = x_modes.reshape(COUNT, 2, 128)

    sent = list(halo)

    def send_one(part, dst, stage, step):
        to = near(step)
        pltpu.make_async_remote_copy(
            src_ref=part(to), dst_ref=dst.at[me], send_sem=all_ssem.at[stage],
            recv_sem=all_rsem.at[stage], device_id=to, device_id_type=LOGICAL,
        ).start()

    def send_all(part, dst, stage):
        def one(i, carry):
            send_one(part, dst, stage, i)
            return carry

        lax.fori_loop(1, COUNT, one, 0)
        dst[me] = part(me)[...]

    def wait_all(dst, stage):
        copy = pltpu.make_async_remote_copy(
            src_ref=dst.at[pl.ds(0, COUNT - 1)], dst_ref=dst.at[pl.ds(0, COUNT - 1)],
            send_sem=all_ssem.at[stage], recv_sem=all_rsem.at[stage],
            device_id=near(1), device_id_type=LOGICAL,
        )
        copy.wait_recv()
        sent.append(copy)

    def x_part(to):
        return x_send.at[to]

    send_all(x_part, z_recv, 0)
    far_plane.wait_recv()
    for c in range(2):
        put(2, ROWS, c, jnp.where(has_prev, lower_prev[0, c].astype(F32), 0.0))
    start_groups(*early)
    run_groups(*early, 2, 4)
    kept[1], scale_sum = couple(acc1, 1, 1)
    total = total + fold(scale_sum)
    wait_all(z_recv, 0)

    z_modes = table_times(forward_z, z_recv[...].reshape(256, 128))

    lines = jnp.concatenate([z_modes[g * 64 : (g + 1) * 64] for g in range(GY)], axis=1)
    modes = times_table(lines, forward_y)
    parts = [
        modes[k * 32 : (k + 1) * 32, c * 128 : (c + 1) * 128] for k in range(2) for c in range(4)
    ]
    for o in range(16):
        value = profile[pl.ds(o * 256, 32), :] * parts[0]
        for c in range(1, 8):
            value = value + profile[pl.ds(o * 256 + c * 32, 32), :] * parts[c]
        mixed[pl.ds((o // 4) * 32, 32), pl.ds((o % 4) * 128, 128)] = value
    back = times_table(mixed[...], forward_y, turned=True)
    lines = jnp.concatenate(
        [
            jnp.concatenate(
                [back[:, g * 128 : (g + 1) * 128] for g in (2 * pair, 2 * pair + 1)], axis=0
            )
            for pair in range(2)
        ],
        axis=1,
    )
    planes = table_times(backward_z, lines)
    for pair in range(2):
        part = planes[:, pair * 128 : (pair + 1) * 128]
        zb_send[:, pl.ds(pair * 2, 2)] = part.reshape(GZ, 2, 4, 128)

    send_all(lambda to: zb_send.at[to // GY, lax.rem(to, GY)], x_recv, 1)

    run_groups(*early, 4, GROUPS)
    end_groups(*early)
    squares_sum = fold(kept[0] * kept[0])
    for parity in range(2):
        coupled, scale_sum = couple(acc0, 0, parity)
        kept[2 + parity] = coupled
        total = total + fold(scale_sum)
        squares_sum = squares_sum + fold(coupled * coupled)
    target = spread_x(kept[1])
    wait_all(x_recv, 1)

    lines = jnp.concatenate([x_recv[:, og, :] for og in range(4)], axis=1)
    moved = table_times(backward_x, lines)
    shifts = [jnp.transpose(moved[:, og * 128 : (og + 1) * 128]) for og in range(4)]
    for k in range(2):
        scale = jnp.tanh(shifts[k])
        total = total + fold(scale)
        moved = target[:, k * 128 : (k + 1) * 128] * jnp.exp(scale) + shifts[2 + k]
        squares_sum = squares_sum + fold(moved * moved)
        latent[pl.ds(8 + k * 4, 4), 0] = moved.reshape(4, 32, 128)

    total = total - 0.5 * squares_sum
    sum_send[0] = jnp.sum(total, axis=0, keepdims=True)

    send_all(lambda to: sum_send.at[0], sum_recv, 2)
    for parity in range(2):
        coupled = spread_x(kept[2 + parity])
        for k in range(2):
            at = (2 * parity + k) * 4
            factored[pl.ds(at, 4), 0] = coupled[:, k * 128 : (k + 1) * 128].reshape(4, 32, 128)
    source = spread_x(kept[0])
    for k in range(2):
        latent[pl.ds(k * 4, 4), 0] = source[:, k * 128 : (k + 1) * 128].reshape(4, 32, 128)
    wait_all(sum_recv, 2)
    total = jnp.sum(sum_recv[...], axis=0)
    for copy in sent:
        copy.wait_send()
    count = 4.0 * 64 * 256 * 256
    log_density[0, 0] = jnp.sum(total) / count - 0.5 * math.log(2.0 * math.pi)


def shards(consts, density_field, first_weight, first_bias, middle_weight, middle_bias, output_weight, output_bias, radial_weights):
    vmem = pl.BlockSpec(memory_space=pltpu.VMEM)
    smem = pl.BlockSpec(memory_space=pltpu.SMEM)
    hbm = pl.BlockSpec(memory_space=pltpu.HBM)
    operands = [
        density_field, first_weight, first_bias.reshape(1, 128), middle_weight,
        middle_bias.reshape(1, 128), output_weight, output_bias, radial_weights.reshape(128, 32),
    ] + [jnp.asarray(value) for value in consts.values()]
    specs = [hbm] * len(operands)
    held = [pltpu.VMEM(value.shape, value.dtype) for value in operands]
    held[6] = pltpu.SMEM(output_bias.shape, F32)
    buffers = [
        pltpu.VMEM((2, 2, ROWS, WIDE), BF16),
        pltpu.VMEM((2, 8, WIDE), F32),
        pltpu.VMEM((2, 2, ROWS, WIDE), BF16),
        pltpu.VMEM((2, 2, ROWS, WIDE), BF16),
        pltpu.VMEM((2, 3, 8, WIDE), F32),
        pltpu.VMEM((2, 72 * SLOTS, 128), F32),
        pltpu.VMEM((OWN_ROWS + 2, 256, WIDE), BF16),
        pltpu.VMEM((2, 70 * 16, 128), F32),
        pltpu.VMEM((2, 70 * 16, 128), F32),
        pltpu.VMEM((64, 128), F32),
        pltpu.VMEM((512, 128), BF16),
        pltpu.VMEM((128, 128), BF16),
        pltpu.VMEM((128, 128), F32),
        pltpu.VMEM((48, 384), F32),
        pltpu.VMEM((108, 128), F32),
        pltpu.VMEM((128 * 32, 128), F32),
        pltpu.VMEM((COUNT, 2, 128), F32),
        pltpu.VMEM((COUNT, 2, 128), F32),
        pltpu.VMEM((128, 512), F32),
        pltpu.VMEM((GZ, GY, 4, 128), F32),
        pltpu.VMEM((COUNT, 4, 128), F32),
        pltpu.VMEM((4, 128, WIDE), F32),
        pltpu.VMEM((GROUP, 384, WIDE), BF16),
        pltpu.VMEM((GROUP, 128, WIDE), BF16),
        pltpu.VMEM((1, 1, 128), F32),
        pltpu.VMEM((COUNT, 1, 128), F32),
        pltpu.VMEM((2, 4, 2, ROWS, 128), F32),
    ] + held[1:] + [
        pltpu.SemaphoreType.DMA((15,)),
        pltpu.SemaphoreType.DMA((15,)),
        pltpu.SemaphoreType.DMA((3,)),
        pltpu.SemaphoreType.DMA((3,)),
        pltpu.SemaphoreType.DMA((19,)),
    ]
    operands = [pltpu.with_memory_space_constraint(value, pltpu.HBM) for value in operands]
    factored, latent, log_density = pl.pallas_call(
        flow_kernel,
        out_shape=(
            jax.ShapeDtypeStruct((16, 1, 32, 128), F32),
            jax.ShapeDtypeStruct((16, 1, 32, 128), F32),
            jax.ShapeDtypeStruct((1, 1), F32),
        ),
        in_specs=specs,
        out_specs=(vmem, vmem, smem),
        scratch_shapes=buffers,
        compiler_params=pltpu.CompilerParams(
            collective_id=0, has_side_effects=True, vmem_limit_bytes=52 * 1024 * 1024
        ),
        name="flow",
    )(*operands)
    return factored, latent, log_density.reshape(())


def solution(mesh):
    assert mesh.shape["gz"] == GZ and mesh.shape["gy"] == GY
    in_specs = (P(None, "gz", "gy", None), P(), P(), P(), P(), P(), P(), P())
    out_specs = (P(None, "gz", "gy", None), P(None, "gz", "gy", None), P())
    return jax.shard_map(
        functools.partial(shards, tables()),
        mesh=mesh, in_specs=in_specs, out_specs=out_specs, check_vma=False,
    )
```

```python
import functools
import math

import jax
import jax.numpy as jnp
import ml_dtypes
import numpy as np
from jax import lax
from jax.experimental import pallas as pl
from jax.experimental.pallas import tpu as pltpu
from jax.sharding import PartitionSpec as P

MESH = pl.DeviceIdType.MESH
LOGICAL = pl.DeviceIdType.LOGICAL
F32 = jnp.float32
BF16 = jnp.bfloat16

SLOTS = 40
ROWS = 64
WIDE = 256
GZ = 32
GY = 4
COUNT = GZ * GY
OWN_ROWS = ROWS + 2
CHUNK = 16
CHUNKS = ROWS // CHUNK
GROUP = 11
GROUPS = OWN_ROWS // GROUP


def real_basis(length):
    cells = np.arange(length)
    rows = [np.full(length, 1.0 / math.sqrt(length))]
    for m in range(1, length // 2):
        rows.append(math.sqrt(2.0 / length) * np.cos(2.0 * math.pi * m * cells / length))
        rows.append(math.sqrt(2.0 / length) * np.sin(2.0 * math.pi * m * cells / length))
    rows.append(np.where(cells % 2 == 0, 1.0, -1.0) / math.sqrt(length))
    return np.stack(rows)


def split_pair(table):
    table = np.asarray(table, np.float32)
    high = table.astype(ml_dtypes.bfloat16)
    low = (table - high.astype(np.float32)).astype(ml_dtypes.bfloat16)
    return np.stack([high, low])


def tables():
    fx, fy, fz = real_basis(128), real_basis(128), real_basis(32)
    forward_x = np.zeros((128, 2, 128, 2))
    for k in range(2):
        forward_x[:, k, :, k] = fx
    forward_x = forward_x.reshape(256, 256)
    forward_z = np.einsum("kz,qp->qkzp", fz, np.eye(8)).reshape(256, 256)
    forward_y = np.einsum("kgy,cd->gcydk", fy.reshape(128, 4, 32), np.eye(4)).reshape(512, 512)
    spread = np.zeros((128, 2, 2, 128))
    for k in range(2):
        spread[np.arange(128), k, k, np.arange(128)] = 1.0
    spread = spread.reshape(256, 256).astype(ml_dtypes.bfloat16)
    pick = np.zeros((64, 4, 128))
    for plane in range(4):
        for c in range(2):
            for a in range(3):
                for b in range(3):
                    for e in range(3):
                        row = 27 * c + 9 * a + 3 * b + e
                        pick[row, plane, b * SLOTS + e * 12 + (a + plane) * 2 + c] = 1.0
        for piece in range(3):
            pick[54 + piece, plane, piece * SLOTS + 36] = 1.0
    pick = pick.reshape(64, 512).astype(ml_dtypes.bfloat16)
    half_z = (np.arange(32) + 1) // 2 / 32.0
    half_y = (np.arange(128) + 1) // 2 / 128.0
    squares = (half_z[:, None] ** 2 + half_y[None, :] ** 2).reshape(1, 4096).astype(np.float32)
    return {
        "forward_x": split_pair(forward_x),
        "forward_z": split_pair(forward_z),
        "backward_z": split_pair(forward_z.T),
        "forward_y": split_pair(forward_y),
        "backward_x": split_pair(fx.T),
        "spread": spread,
        "pick": pick,
        "squares": squares,
    }


def split2(values):
    high = values.astype(BF16)
    return high, (values - high.astype(F32)).astype(BF16)


def split3(values):
    high = values.astype(BF16)
    rest = values - high.astype(F32)
    mid = rest.astype(BF16)
    return high, mid, (rest - mid.astype(F32)).astype(BF16)


def mul(a, b, dims=((1,), (0,))):
    return lax.dot_general(a, b, (dims, ((), ())), preferred_element_type=F32)


def table_times(table, values):
    high, low = split2(values)
    columns = values.shape[1]
    both = mul(table[0], jnp.concatenate([high, low], axis=1))
    return both[:, :columns] + (both[:, columns:] + mul(table[1], high))


def times_table(values, table, turned=False):
    dims = ((1,), (1,)) if turned else ((1,), (0,))
    high, low = split2(values)
    rows = values.shape[0]
    both = mul(jnp.concatenate([high, low], axis=0), table[0], dims)
    return both[:rows] + (both[rows:] + mul(high, table[1], dims))


def shift_right(values):
    lane = lax.broadcasted_iota(jnp.int32, values.shape, values.ndim - 1)
    return jnp.where(lane == 0, 0.0, pltpu.roll(values, 1, values.ndim - 1))


def shift_left(values):
    last = values.shape[-1] - 1
    lane = lax.broadcasted_iota(jnp.int32, values.shape, values.ndim - 1)
    return jnp.where(lane == last, 0.0, pltpu.roll(values, last, values.ndim - 1))


def flow_kernel(
    dens_hbm, first_w_hbm, first_b_hbm, middle_w_hbm, middle_b_hbm, output_w_hbm, output_b_hbm,
    radial_hbm, forward_x_hbm, forward_z_hbm, backward_z_hbm, forward_y_hbm, backward_x_hbm,
    spread_hbm, pick_hbm, squares_hbm,
    factored, latent, log_density,
    lower_send, edge_send, lower_prev, lower_next, edge_recv,
    window, hidden, acc0, acc1, wide_w, w1, w2, b2, w3, ow32, profile,
    x_send, z_recv, mixed, zb_send, x_recv,
    kept, first_held, last_held, sum_send, sum_recv, dens2,
    first_w, first_b, middle_w, middle_b, output_w, output_b,
    radial, forward_x, forward_z, backward_z, forward_y, backward_x, spread, pick, squares,
    halo_ssem, halo_rsem, all_ssem, all_rsem, in_sem, known,
):
    me_z = lax.axis_index("gz")
    me_y = lax.axis_index("gy")

    me = me_z * GY + me_y

    def near(step):
        return lax.rem(me + step, COUNT)

    def near_z(step):
        return lax.rem(me_z + step + GZ, GZ)

    def near_y(step):
        return lax.rem(me_y + step + GY, GY)

    barrier = pltpu.get_barrier_semaphore()
    sides = [(dz, dy) for dz in (-1, 0, 1) for dy in (-1, 0, 1) if (dz, dy) != (0, 0)]
    for dz, dy in sides:
        pl.semaphore_signal(
            barrier, inc=1, device_id=(near_z(dz), near_y(dy)), device_id_type=MESH
        )
    def fetch(src, dst, index):
        copy = pltpu.make_async_copy(src, dst, in_sem.at[index])
        copy.start()
        return copy

    lower_in = [
        fetch(
            dens_hbm.at[pl.ds(0, 2), :, :, pl.ds(half * 128, 128)],
            dens2.at[half, pl.ds(0, 2)], half,
        )
        for half in range(2)
    ]

    for copy in lower_in:
        copy.wait()
    for z in range(2):
        for c in range(2):
            for half in range(2):
                lower_send[z, c, :, pl.ds(half * 128, 128)] = dens2[half, c, z].astype(BF16)
    for side in range(2):
        for row in range(2):
            for z in range(2):
                for c in range(2):
                    source_row = row if side == 0 else ROWS - 2 + row
                    for half in range(2):
                        line = dens2[half, c, z, pl.ds(source_row, 1), :]
                        edge_send[
                            side, pl.ds(row * 4 + z * 2 + c, 1), pl.ds(half * 128, 128)
                        ] = line.astype(BF16).astype(F32)

    pl.semaphore_wait(barrier, len(sides))

    reach = [sides, [(-2, 0), (2, 0)], [(-4, 0), (4, 0)], [(-8, 0), (8, 0)]]

    def tell(turn):
        for dz, dy in reach[turn]:
            pl.semaphore_signal(
                known.at[turn], inc=1, device_id=(near_z(dz), near_y(dy)), device_id_type=MESH
            )

    def hear(turn):
        pl.semaphore_wait(known.at[turn], len(reach[turn]))

    tell(0)
    halo = []

    def halo_copy(src, dst, index, to):
        return pltpu.make_async_remote_copy(
            src_ref=src, dst_ref=dst, send_sem=halo_ssem.at[index], recv_sem=halo_rsem.at[index],
            device_id=to, device_id_type=MESH,
        )

    def chunk_copies(chunk):
        rows = pl.ds(pl.multiple_of(chunk * CHUNK, CHUNK), CHUNK)
        return (
            halo_copy(
                lower_send.at[:, :, rows], lower_next.at[:, :, rows], 6 + chunk,
                (near_z(-1), me_y),
            ),
            halo_copy(
                lower_send.at[1, :, rows], lower_prev.at[1, :, rows], 10 + chunk,
                (near_z(1), me_y),
            ),
        )

    def start_halo(copies):
        for copy in copies:
            copy.start()
            halo.append(copy)

    edges = [
        [
            halo_copy(
                edge_send.at[side], edge_recv.at[1 - side, 1 - dz], side * 3 + dz + 1,
                (near_z(dz), near_y(-1) if side == 0 else near_y(1)),
            )
            for dz in (-1, 0, 1)
        ]
        for side in range(2)
    ]
    far_plane = halo_copy(lower_send.at[0], lower_prev.at[0], 14, (near_z(1), me_y))
    start_halo(edges[1])
    start_halo(chunk_copies(0))
    start_halo(edges[0])
    for chunk in range(1, CHUNKS):
        start_halo(chunk_copies(chunk))
    start_halo([far_plane])

    weights_in = [
        fetch(src, dst, 2 + i)
        for i, (src, dst) in enumerate(
            (
                (first_w_hbm, first_w), (first_b_hbm, first_b), (pick_hbm, pick),
                (middle_w_hbm, middle_w), (middle_b_hbm, middle_b), (output_w_hbm, output_w),
            )
        )
    ]
    filter_in = [fetch(radial_hbm, radial, 8), fetch(squares_hbm, squares, 9)]
    late_in = [
        fetch(
            dens_hbm.at[pl.ds(2, 2), :, :, pl.ds(half * 128, 128)],
            dens2.at[half, pl.ds(2, 2)], 10 + half,
        )
        for half in range(2)
    ] + [
        fetch(src, dst, 12 + i)
        for i, (src, dst) in enumerate(
            (
                (output_b_hbm, output_b), (forward_x_hbm, forward_x), (forward_z_hbm, forward_z),
                (forward_y_hbm, forward_y), (backward_z_hbm, backward_z),
                (backward_x_hbm, backward_x), (spread_hbm, spread),
            )
        )
    ]

    for copy in weights_in:
        copy.wait()
    wide_w[...] = jnp.zeros_like(wide_w)
    wide_w[pl.ds(0, 54), :] = first_w[...].astype(F32)
    for piece, part in enumerate(split3(first_b[...])):
        wide_w[pl.ds(54 + piece, 1), :] = part.astype(F32)
    turned = jnp.transpose(wide_w[...]).astype(BF16)
    for plane in range(4):
        w1[pl.ds(plane * 128, 128), :] = mul(
            turned, pick[:, pl.ds(plane * 128, 128)]
        ).astype(BF16)
    w2[...] = jnp.transpose(middle_w[...].astype(F32)).astype(BF16)
    b2[...] = jnp.transpose(jnp.broadcast_to(middle_b[...], (128, 128)))
    ow32[...] = output_w[...].astype(F32)
    w3[...] = jnp.zeros_like(w3)
    for a in range(3):
        for b in range(3):
            w3[pl.ds(b * 16, 12), pl.ds(a * 128, 128)] = ow32[pl.ds(36 * a + 12 * b, 12), :]

    def put(first, count, slot, values):
        for e, shifted in enumerate((shift_right(values), values, shift_left(values))):
            for half in range(2):
                window[half, pl.ds(first * SLOTS + e * 12 + slot, count, stride=SLOTS), :] = shifted[
                    :, half * 128 : (half + 1) * 128
                ]

    for half in range(2):
        window[half, pl.ds(36, 72, stride=SLOTS), :] = jnp.ones((72, 128), F32)
        for slot in range(37, 40):
            window[half, pl.ds(slot, 72, stride=SLOTS), :] = jnp.zeros((72, 128), F32)
        window[half, pl.ds(68 * SLOTS, 36), :] = jnp.zeros((36, 128), F32)
        for slot in (0, 1, 12, 13, 24, 25):
            window[half, pl.ds(2 * SLOTS + slot, ROWS, stride=SLOTS), :] = jnp.zeros((ROWS, 128), F32)
    for z in range(2):
        for c in range(2):
            put(2, ROWS, (z + 2) * 2 + c, lower_send[z, c].astype(F32))

    step_x = (me + 1) // 2
    freq_x = step_x.astype(F32) * (1.0 / 128.0)
    for copy in filter_in:
        copy.wait()
    weights = radial[...]
    centres = lax.broadcasted_iota(jnp.int32, (32, 512), 0).astype(F32)

    def filter_part(part, carry):
        lanes = pl.ds(pl.multiple_of(part * 512, 512), 512)
        kappa = jnp.sqrt(squares[:, lanes] + freq_x * freq_x) * (2.0 / math.sqrt(3.0))
        scaled = kappa * 31.0 - centres
        basis = jnp.exp(-scaled * scaled)
        values = table_times(split2(weights), basis)
        for j in range(4):
            profile[pl.ds(part * 4 + j, 128, stride=32), :] = values[:, j * 128 : (j + 1) * 128]
        return carry

    lax.fori_loop(0, 8, filter_part, 0)

    for copy in late_in:
        copy.wait()

    has_prev = me_z > 0
    has_next = me_z < GZ - 1
    has_up = me_y > 0
    has_down = me_y < GY - 1

    def fill_chunk(chunk):
        for copy in chunk_copies(chunk):
            copy.wait_recv()
        rows = pl.ds(pl.multiple_of(chunk * CHUNK, CHUNK), CHUNK)
        first = 2 + chunk * CHUNK
        for c in range(2):
            values = lower_prev[1, c, rows, :].astype(F32)
            put(first, CHUNK, 2 + c, jnp.where(has_prev, values, 0.0))
            for z in range(2):
                values = lower_next[z, c, rows, :].astype(F32)
                put(first, CHUNK, (z + 4) * 2 + c, jnp.where(has_next, values, 0.0))

    def fill_edge(side):
        for copy in edges[1 - side]:
            copy.wait_recv()
        for offset in range(3):
            valid = has_up if side == 0 else has_down
            if offset == 0:
                valid = jnp.logical_and(valid, has_prev)
            if offset == 2:
                valid = jnp.logical_and(valid, has_next)
            for row in range(2):
                lines = edge_recv[side, offset, pl.ds(row * 4, 4), :]
                lines = jnp.where(valid, lines, 0.0)
                at = (row if side == 0 else ROWS + 2 + row) * SLOTS + offset * 4
                for e, shifted in enumerate((shift_right(lines), lines, shift_left(lines))):
                    for half in range(2):
                        window[half, pl.ds(at + e * 12, 4), :] = shifted[
                            :, half * 128 : (half + 1) * 128
                        ]

    hear(0)
    tell(1)
    fill_edge(0)
    fill_chunk(0)

    w3_lane = lax.broadcasted_iota(jnp.int32, (48, 384), 1)
    w3_first = jnp.where(jnp.logical_and(w3_lane < 128, me_z == 0), 0.0, w3[...]).astype(BF16)
    w3_second = jnp.where(
        jnp.logical_and(w3_lane >= 256, me_z == GZ - 1), 0.0, w3[...]
    ).astype(BF16)

    def columns(r):
        start = pl.multiple_of((r - 1) * SLOTS, 8)
        return jnp.concatenate(
            [window[0, pl.ds(start, 128), :], window[1, pl.ds(start, 128), :]], axis=1
        ).astype(BF16)

    def second(first_layer):
        values = mul(w2[...], first_layer) + jnp.concatenate([b2[...]] * 2, axis=1)
        return jnp.maximum(values, 0.0).astype(BF16)

    def add_taps(acc, r, taps):
        valid = jnp.logical_not(
            jnp.logical_or(
                jnp.logical_and(r == 1, me_y == 0),
                jnp.logical_and(r == OWN_ROWS, me_y == GY - 1),
            )
        )
        taps = jnp.where(valid, taps, 0.0)
        for half in range(2):
            part = taps[:, half * 128 : (half + 1) * 128]
            at = [pl.ds(pl.multiple_of((r + 1 - b) * 16, 16), 16) for b in range(3)]
            acc[half, at[0], :] = part[0:16]
            acc[half, at[1], :] += part[16:32]
            acc[half, at[2], :] += part[32:48]

    for acc in (acc0, acc1):
        for half in range(2):
            acc[half, pl.ds(0, 32), :] = jnp.zeros((32, 128), F32)

    def group_rows(group):
        return [(sub, group * GROUP + 1 + sub) for sub in range(GROUP)]

    def later_first(group):
        for sub, r in group_rows(group):
            values = mul(w1[pl.ds(128, 384), :], columns(r))
            first_held[sub] = jnp.maximum(values, 0.0).astype(BF16)

    def later_second(group):
        for sub, r in group_rows(group):
            first_layer = first_held[sub]
            layers = [second(first_layer[p * 128 : (p + 1) * 128]) for p in range(3)]
            hidden[r] = jnp.concatenate(layers[0:2], axis=0)
            last_held[sub] = layers[2]

    def later_last(group):
        for sub, r in group_rows(group):
            stacked = jnp.concatenate([hidden[r], last_held[sub]], axis=0)
            add_taps(acc1, r, mul(w3_second, stacked))

    def early_first(group):
        for sub, r in group_rows(group):
            values = mul(w1[pl.ds(0, 128), :], columns(r))
            first_held[sub, pl.ds(0, 128)] = jnp.maximum(values, 0.0).astype(BF16)

    def early_second(group):
        for sub, r in group_rows(group):
            last_held[sub] = second(first_held[sub, pl.ds(0, 128)])

    def early_last(group):
        for sub, r in group_rows(group):
            stacked = jnp.concatenate([last_held[sub], hidden[r]], axis=0)
            add_taps(acc0, r, mul(w3_first, stacked))

    def start_groups(first, middle, last):
        first(0)
        middle(0)
        first(1)

    def run_groups(first, middle, last, begin, end):
        def step(group, carry):
            last(group - 2)
            middle(group - 1)
            first(group)
            return carry

        lax.fori_loop(begin, end, step, 0)

    def end_groups(first, middle, last):
        last(GROUPS - 2)
        middle(GROUPS - 1)
        last(GROUPS - 1)

    later = (later_first, later_second, later_last)
    early = (early_first, early_second, early_last)

    later_first(0)
    fill_edge(1)
    fill_chunk(1)
    later_second(0)
    later_first(1)
    fill_chunk(2)
    hear(1)
    tell(2)
    run_groups(*later, 2, 4)
    fill_chunk(3)
    hear(2)
    tell(3)
    run_groups(*later, 4, GROUPS)
    end_groups(*later)
    hear(3)

    def couple(acc, z, parity):
        raw = []
        for o in range(4):
            taps = [
                jnp.concatenate(
                    [
                        acc[half, pl.ds((2 + parity) * 16 + e * 4 + o, 32, stride=32), :]
                        for half in range(2)
                    ],
                    axis=1,
                )
                for e in range(3)
            ]
            raw.append(shift_right(taps[0]) + taps[1] + shift_left(taps[2]) + output_b[o])
        lines = [
            jnp.concatenate(
                [
                    dens2[half, c, z, pl.ds(parity, 32, stride=2), :]
                    for half in range(2)
                ],
                axis=1,
            )
            for c in range(4)
        ]
        scales = [jnp.tanh(raw[0]), jnp.tanh(raw[1])]
        for o in range(2):
            lines[2 + o] = lines[2 + o] * jnp.exp(scales[o]) + raw[2 + o]
        return jnp.concatenate(lines, axis=0), scales[0] + scales[1]

    def spread_x(values):
        high, mid, low = split3(values)
        return mul(high, spread[...]) + (mul(mid, spread[...]) + mul(low, spread[...]))

    def fold(values):
        rows, lanes = values.shape
        total = values[:, 0:128]
        for at in range(128, lanes, 128):
            total = total + values[:, at : at + 128]
        return jnp.sum(total.reshape(rows // 8, 8, 128), axis=0)

    source, scale_sum = couple(acc1, 1, 0)
    kept[0] = source
    total = fold(scale_sum)
    high, low = split2(source)
    both = mul(forward_x[0], jnp.concatenate([high, low], axis=0), ((1,), (1,)))
    x_modes = both[:, :128] + (both[:, 128:] + mul(forward_x[1], high, ((1,), (1,))))
    x_send[...] = x_modes.reshape(COUNT, 2, 128)

    sent = list(halo)

    def send_one(part, dst, stage, step):
        to = near(step)
        pltpu.make_async_remote_copy(
            src_ref=part(to), dst_ref=dst.at[me], send_sem=all_ssem.at[stage],
            recv_sem=all_rsem.at[stage], device_id=to, device_id_type=LOGICAL,
        ).start()

    def send_all(part, dst, stage):
        def one(i, carry):
            send_one(part, dst, stage, i)
            return carry

        lax.fori_loop(1, COUNT, one, 0)
        dst[me] = part(me)[...]

    def wait_all(dst, stage):
        copy = pltpu.make_async_remote_copy(
            src_ref=dst.at[pl.ds(0, COUNT - 1)], dst_ref=dst.at[pl.ds(0, COUNT - 1)],
            send_sem=all_ssem.at[stage], recv_sem=all_rsem.at[stage],
            device_id=near(1), device_id_type=LOGICAL,
        )
        copy.wait_recv()
        sent.append(copy)

    def x_part(to):
        return x_send.at[to]

    send_all(x_part, z_recv, 0)
    far_plane.wait_recv()
    for c in range(2):
        put(2, ROWS, c, jnp.where(has_prev, lower_prev[0, c].astype(F32), 0.0))
    start_groups(*early)
    run_groups(*early, 2, 4)
    kept[1], scale_sum = couple(acc1, 1, 1)
    total = total + fold(scale_sum)
    wait_all(z_recv, 0)

    z_modes = table_times(forward_z, z_recv[...].reshape(256, 128))

    lines = jnp.concatenate([z_modes[g * 64 : (g + 1) * 64] for g in range(GY)], axis=1)
    modes = times_table(lines, forward_y)
    parts = [
        modes[k * 32 : (k + 1) * 32, c * 128 : (c + 1) * 128] for k in range(2) for c in range(4)
    ]
    for o in range(16):
        value = profile[pl.ds(o * 256, 32), :] * parts[0]
        for c in range(1, 8):
            value = value + profile[pl.ds(o * 256 + c * 32, 32), :] * parts[c]
        mixed[pl.ds((o // 4) * 32, 32), pl.ds((o % 4) * 128, 128)] = value
    back = times_table(mixed[...], forward_y, turned=True)
    lines = jnp.concatenate(
        [
            jnp.concatenate(
                [back[:, g * 128 : (g + 1) * 128] for g in (2 * pair, 2 * pair + 1)], axis=0
            )
            for pair in range(2)
        ],
        axis=1,
    )
    planes = table_times(backward_z, lines)
    for pair in range(2):
        part = planes[:, pair * 128 : (pair + 1) * 128]
        zb_send[:, pl.ds(pair * 2, 2)] = part.reshape(GZ, 2, 4, 128)

    send_all(lambda to: zb_send.at[to // GY, lax.rem(to, GY)], x_recv, 1)

    run_groups(*early, 4, GROUPS)
    end_groups(*early)
    squares_sum = fold(kept[0] * kept[0])
    for parity in range(2):
        coupled, scale_sum = couple(acc0, 0, parity)
        kept[2 + parity] = coupled
        total = total + fold(scale_sum)
        squares_sum = squares_sum + fold(coupled * coupled)
    target = spread_x(kept[1])
    wait_all(x_recv, 1)

    lines = jnp.concatenate([x_recv[:, og, :] for og in range(4)], axis=1)
    moved = table_times(backward_x, lines)
    shifts = [jnp.transpose(moved[:, og * 128 : (og + 1) * 128]) for og in range(4)]
    for k in range(2):
        scale = jnp.tanh(shifts[k])
        total = total + fold(scale)
        moved = target[:, k * 128 : (k + 1) * 128] * jnp.exp(scale) + shifts[2 + k]
        squares_sum = squares_sum + fold(moved * moved)
        latent[pl.ds(8 + k * 4, 4), 0] = moved.reshape(4, 32, 128)

    total = total - 0.5 * squares_sum
    sum_send[0] = jnp.sum(total, axis=0, keepdims=True)

    send_all(lambda to: sum_send.at[0], sum_recv, 2)
    for parity in range(2):
        coupled = spread_x(kept[2 + parity])
        for k in range(2):
            at = (2 * parity + k) * 4
            factored[pl.ds(at, 4), 0] = coupled[:, k * 128 : (k + 1) * 128].reshape(4, 32, 128)
    source = spread_x(kept[0])
    for k in range(2):
        latent[pl.ds(k * 4, 4), 0] = source[:, k * 128 : (k + 1) * 128].reshape(4, 32, 128)
    wait_all(sum_recv, 2)
    total = jnp.sum(sum_recv[...], axis=0)
    for copy in sent:
        copy.wait_send()
    count = 4.0 * 64 * 256 * 256
    log_density[0, 0] = jnp.sum(total) / count - 0.5 * math.log(2.0 * math.pi)


def shards(consts, density_field, first_weight, first_bias, middle_weight, middle_bias, output_weight, output_bias, radial_weights):
    vmem = pl.BlockSpec(memory_space=pltpu.VMEM)
    smem = pl.BlockSpec(memory_space=pltpu.SMEM)
    hbm = pl.BlockSpec(memory_space=pltpu.HBM)
    operands = [
        density_field, first_weight, first_bias.reshape(1, 128), middle_weight,
        middle_bias.reshape(1, 128), output_weight, output_bias, radial_weights.reshape(128, 32),
    ] + [jnp.asarray(value) for value in consts.values()]
    specs = [hbm] * len(operands)
    held = [pltpu.VMEM(value.shape, value.dtype) for value in operands]
    held[6] = pltpu.SMEM(output_bias.shape, F32)
    buffers = [
        pltpu.VMEM((2, 2, ROWS, WIDE), BF16),
        pltpu.VMEM((2, 8, WIDE), F32),
        pltpu.VMEM((2, 2, ROWS, WIDE), BF16),
        pltpu.VMEM((2, 2, ROWS, WIDE), BF16),
        pltpu.VMEM((2, 3, 8, WIDE), F32),
        pltpu.VMEM((2, 72 * SLOTS, 128), F32),
        pltpu.VMEM((OWN_ROWS + 2, 256, WIDE), BF16),
        pltpu.VMEM((2, 70 * 16, 128), F32),
        pltpu.VMEM((2, 70 * 16, 128), F32),
        pltpu.VMEM((64, 128), F32),
        pltpu.VMEM((512, 128), BF16),
        pltpu.VMEM((128, 128), BF16),
        pltpu.VMEM((128, 128), F32),
        pltpu.VMEM((48, 384), F32),
        pltpu.VMEM((108, 128), F32),
        pltpu.VMEM((128 * 32, 128), F32),
        pltpu.VMEM((COUNT, 2, 128), F32),
        pltpu.VMEM((COUNT, 2, 128), F32),
        pltpu.VMEM((128, 512), F32),
        pltpu.VMEM((GZ, GY, 4, 128), F32),
        pltpu.VMEM((COUNT, 4, 128), F32),
        pltpu.VMEM((4, 128, WIDE), F32),
        pltpu.VMEM((GROUP, 384, WIDE), BF16),
        pltpu.VMEM((GROUP, 128, WIDE), BF16),
        pltpu.VMEM((1, 1, 128), F32),
        pltpu.VMEM((COUNT, 1, 128), F32),
        pltpu.VMEM((2, 4, 2, ROWS, 128), F32),
    ] + held[1:] + [
        pltpu.SemaphoreType.DMA((15,)),
        pltpu.SemaphoreType.DMA((15,)),
        pltpu.SemaphoreType.DMA((3,)),
        pltpu.SemaphoreType.DMA((3,)),
        pltpu.SemaphoreType.DMA((19,)),
        pltpu.SemaphoreType.REGULAR((4,)),
    ]
    operands = [pltpu.with_memory_space_constraint(value, pltpu.HBM) for value in operands]
    factored, latent, log_density = pl.pallas_call(
        flow_kernel,
        out_shape=(
            jax.ShapeDtypeStruct((16, 1, 32, 128), F32),
            jax.ShapeDtypeStruct((16, 1, 32, 128), F32),
            jax.ShapeDtypeStruct((1, 1), F32),
        ),
        in_specs=specs,
        out_specs=(vmem, vmem, smem),
        scratch_shapes=buffers,
        compiler_params=pltpu.CompilerParams(
            collective_id=0, has_side_effects=True, vmem_limit_bytes=52 * 1024 * 1024
        ),
        name="flow",
    )(*operands)
    return factored, latent, log_density.reshape(())


def solution(mesh):
    assert mesh.shape["gz"] == GZ and mesh.shape["gy"] == GY
    in_specs = (P(None, "gz", "gy", None), P(), P(), P(), P(), P(), P(), P())
    out_specs = (P(None, "gz", "gy", None), P(None, "gz", "gy", None), P())
    return jax.shard_map(
        functools.partial(shards, tables()),
        mesh=mesh, in_specs=in_specs, out_specs=out_specs, check_vma=False,
    )
```

```python
import functools
import math

import jax
import jax.numpy as jnp
import ml_dtypes
import numpy as np
from jax import lax
from jax.experimental import pallas as pl
from jax.experimental.pallas import tpu as pltpu
from jax.sharding import PartitionSpec as P

MESH = pl.DeviceIdType.MESH
LOGICAL = pl.DeviceIdType.LOGICAL
F32 = jnp.float32
BF16 = jnp.bfloat16

SLOTS = 40
ROWS = 64
WIDE = 256
GZ = 32
GY = 4
COUNT = GZ * GY
OWN_ROWS = ROWS + 2
CHUNK = 16
CHUNKS = ROWS // CHUNK
GROUP = 11
GROUPS = OWN_ROWS // GROUP


def real_basis(length):
    cells = np.arange(length)
    rows = [np.full(length, 1.0 / math.sqrt(length))]
    for m in range(1, length // 2):
        rows.append(math.sqrt(2.0 / length) * np.cos(2.0 * math.pi * m * cells / length))
        rows.append(math.sqrt(2.0 / length) * np.sin(2.0 * math.pi * m * cells / length))
    rows.append(np.where(cells % 2 == 0, 1.0, -1.0) / math.sqrt(length))
    return np.stack(rows)


def split_pair(table):
    table = np.asarray(table, np.float32)
    high = table.astype(ml_dtypes.bfloat16)
    low = (table - high.astype(np.float32)).astype(ml_dtypes.bfloat16)
    return np.stack([high, low])


def tables():
    fx, fy, fz = real_basis(128), real_basis(128), real_basis(32)
    forward_x = np.zeros((128, 2, 128, 2))
    for k in range(2):
        forward_x[:, k, :, k] = fx
    forward_x = forward_x.reshape(256, 256)
    forward_z = np.einsum("kz,qp->qkzp", fz, np.eye(8)).reshape(256, 256)
    forward_y = np.einsum("kgy,cd->gcydk", fy.reshape(128, 4, 32), np.eye(4)).reshape(512, 512)
    spread = np.zeros((128, 2, 2, 128))
    for k in range(2):
        spread[np.arange(128), k, k, np.arange(128)] = 1.0
    spread = spread.reshape(256, 256).astype(ml_dtypes.bfloat16)
    pick = np.zeros((64, 4, 128))
    for plane in range(4):
        for c in range(2):
            for a in range(3):
                for b in range(3):
                    for e in range(3):
                        row = 27 * c + 9 * a + 3 * b + e
                        pick[row, plane, b * SLOTS + e * 12 + (a + plane) * 2 + c] = 1.0
        for piece in range(3):
            pick[54 + piece, plane, piece * SLOTS + 36] = 1.0
    pick = pick.reshape(64, 512).astype(ml_dtypes.bfloat16)
    half_z = (np.arange(32) + 1) // 2 / 32.0
    half_y = (np.arange(128) + 1) // 2 / 128.0
    squares = (half_z[:, None] ** 2 + half_y[None, :] ** 2).reshape(1, 4096).astype(np.float32)
    return {
        "forward_x": split_pair(forward_x),
        "forward_z": split_pair(forward_z),
        "backward_z": split_pair(forward_z.T),
        "forward_y": split_pair(forward_y),
        "backward_x": split_pair(fx.T),
        "spread": spread,
        "pick": pick,
        "squares": squares,
    }


def split2(values):
    high = values.astype(BF16)
    return high, (values - high.astype(F32)).astype(BF16)


def split3(values):
    high = values.astype(BF16)
    rest = values - high.astype(F32)
    mid = rest.astype(BF16)
    return high, mid, (rest - mid.astype(F32)).astype(BF16)


def mul(a, b, dims=((1,), (0,))):
    return lax.dot_general(a, b, (dims, ((), ())), preferred_element_type=F32)


def table_times(table, values):
    high, low = split2(values)
    columns = values.shape[1]
    both = mul(table[0], jnp.concatenate([high, low], axis=1))
    return both[:, :columns] + (both[:, columns:] + mul(table[1], high))


def times_table(values, table, turned=False):
    dims = ((1,), (1,)) if turned else ((1,), (0,))
    high, low = split2(values)
    rows = values.shape[0]
    both = mul(jnp.concatenate([high, low], axis=0), table[0], dims)
    return both[:rows] + (both[rows:] + mul(high, table[1], dims))


def shift_right(values):
    lane = lax.broadcasted_iota(jnp.int32, values.shape, values.ndim - 1)
    return jnp.where(lane == 0, 0.0, pltpu.roll(values, 1, values.ndim - 1))


def shift_left(values):
    last = values.shape[-1] - 1
    lane = lax.broadcasted_iota(jnp.int32, values.shape, values.ndim - 1)
    return jnp.where(lane == last, 0.0, pltpu.roll(values, last, values.ndim - 1))


def flow_kernel(
    dens_hbm, first_w_hbm, first_b_hbm, middle_w_hbm, middle_b_hbm, output_w_hbm, output_b_hbm,
    radial_hbm, forward_x_hbm, forward_z_hbm, backward_z_hbm, forward_y_hbm, backward_x_hbm,
    spread_hbm, pick_hbm, squares_hbm,
    factored, latent, log_density,
    lower_send, edge_send, lower_prev, lower_next, edge_recv,
    window, hidden, acc0, acc1, wide_w, w1, w2, b2, w3, ow32, profile,
    x_send, z_recv, mixed, zb_send, x_recv,
    kept, first_held, last_held, sum_send, sum_recv, dens2,
    first_w, first_b, middle_w, middle_b, output_w, output_b,
    radial, forward_x, forward_z, backward_z, forward_y, backward_x, spread, pick, squares,
    halo_ssem, halo_rsem, all_ssem, all_rsem, in_sem, known,
):
    me_z = lax.axis_index("gz")
    me_y = lax.axis_index("gy")

    me = me_z * GY + me_y

    def near(step):
        return lax.rem(me + step, COUNT)

    def near_z(step):
        return lax.rem(me_z + step + GZ, GZ)

    def near_y(step):
        return lax.rem(me_y + step + GY, GY)

    barrier = pltpu.get_barrier_semaphore()
    sides = [(dz, dy) for dz in (-1, 0, 1) for dy in (-1, 0, 1) if (dz, dy) != (0, 0)]
    for dz, dy in sides:
        pl.semaphore_signal(
            barrier, inc=1, device_id=(near_z(dz), near_y(dy)), device_id_type=MESH
        )
    def fetch(src, dst, index):
        copy = pltpu.make_async_copy(src, dst, in_sem.at[index])
        copy.start()
        return copy

    lower_in = [
        fetch(
            dens_hbm.at[pl.ds(0, 2), :, :, pl.ds(half * 128, 128)],
            dens2.at[half, pl.ds(0, 2)], half,
        )
        for half in range(2)
    ]

    for copy in lower_in:
        copy.wait()
    for z in range(2):
        for c in range(2):
            for half in range(2):
                lower_send[z, c, :, pl.ds(half * 128, 128)] = dens2[half, c, z].astype(BF16)
    for side in range(2):
        for row in range(2):
            for z in range(2):
                for c in range(2):
                    source_row = row if side == 0 else ROWS - 2 + row
                    for half in range(2):
                        line = dens2[half, c, z, pl.ds(source_row, 1), :]
                        edge_send[
                            side, pl.ds(row * 4 + z * 2 + c, 1), pl.ds(half * 128, 128)
                        ] = line.astype(BF16).astype(F32)

    pl.semaphore_wait(barrier, len(sides))

    reach = [sides, [(-2, 0), (2, 0)], [(-4, 0), (4, 0)], [(-8, 0), (8, 0)]]

    def tell(turn):
        for dz, dy in reach[turn]:
            pl.semaphore_signal(
                known.at[turn], inc=1, device_id=(near_z(dz), near_y(dy)), device_id_type=MESH
            )

    def hear(turn):
        pl.semaphore_wait(known.at[turn], len(reach[turn]))

    tell(0)
    halo = []

    def halo_copy(src, dst, index, to):
        return pltpu.make_async_remote_copy(
            src_ref=src, dst_ref=dst, send_sem=halo_ssem.at[index], recv_sem=halo_rsem.at[index],
            device_id=to, device_id_type=MESH,
        )

    def chunk_copies(chunk):
        rows = pl.ds(pl.multiple_of(chunk * CHUNK, CHUNK), CHUNK)
        return (
            halo_copy(
                lower_send.at[:, :, rows], lower_next.at[:, :, rows], 6 + chunk,
                (near_z(-1), me_y),
            ),
            halo_copy(
                lower_send.at[1, :, rows], lower_prev.at[1, :, rows], 10 + chunk,
                (near_z(1), me_y),
            ),
        )

    def start_halo(copies):
        for copy in copies:
            copy.start()
            halo.append(copy)

    edges = [
        [
            halo_copy(
                edge_send.at[side], edge_recv.at[1 - side, 1 - dz], side * 3 + dz + 1,
                (near_z(dz), near_y(-1) if side == 0 else near_y(1)),
            )
            for dz in (-1, 0, 1)
        ]
        for side in range(2)
    ]
    far_plane = halo_copy(lower_send.at[0], lower_prev.at[0], 14, (near_z(1), me_y))
    start_halo(edges[1])
    start_halo(chunk_copies(0))
    start_halo(edges[0])
    for chunk in range(1, CHUNKS):
        start_halo(chunk_copies(chunk))
    start_halo([far_plane])

    weights_in = [
        fetch(src, dst, 2 + i)
        for i, (src, dst) in enumerate(
            (
                (first_w_hbm, first_w), (first_b_hbm, first_b), (pick_hbm, pick),
                (middle_w_hbm, middle_w), (middle_b_hbm, middle_b), (output_w_hbm, output_w),
            )
        )
    ]
    filter_in = [fetch(radial_hbm, radial, 8), fetch(squares_hbm, squares, 9)]
    late_in = [
        fetch(
            dens_hbm.at[pl.ds(2, 2), :, :, pl.ds(half * 128, 128)],
            dens2.at[half, pl.ds(2, 2)], 10 + half,
        )
        for half in range(2)
    ] + [
        fetch(src, dst, 12 + i)
        for i, (src, dst) in enumerate(
            (
                (output_b_hbm, output_b), (forward_x_hbm, forward_x), (forward_z_hbm, forward_z),
                (forward_y_hbm, forward_y), (backward_z_hbm, backward_z),
                (backward_x_hbm, backward_x), (spread_hbm, spread),
            )
        )
    ]

    for copy in weights_in:
        copy.wait()
    wide_w[...] = jnp.zeros_like(wide_w)
    wide_w[pl.ds(0, 54), :] = first_w[...].astype(F32)
    for piece, part in enumerate(split3(first_b[...])):
        wide_w[pl.ds(54 + piece, 1), :] = part.astype(F32)
    turned = jnp.transpose(wide_w[...]).astype(BF16)
    for plane in range(4):
        w1[pl.ds(plane * 128, 128), :] = mul(
            turned, pick[:, pl.ds(plane * 128, 128)]
        ).astype(BF16)
    w2[...] = jnp.transpose(middle_w[...].astype(F32)).astype(BF16)
    b2[...] = jnp.transpose(jnp.broadcast_to(middle_b[...], (128, 128)))
    ow32[...] = output_w[...].astype(F32)
    w3[...] = jnp.zeros_like(w3)
    for a in range(3):
        for b in range(3):
            w3[pl.ds(b * 16, 12), pl.ds(a * 128, 128)] = ow32[pl.ds(36 * a + 12 * b, 12), :]

    def put(first, count, slot, values):
        for e, shifted in enumerate((shift_right(values), values, shift_left(values))):
            for half in range(2):
                window[half, pl.ds(first * SLOTS + e * 12 + slot, count, stride=SLOTS), :] = shifted[
                    :, half * 128 : (half + 1) * 128
                ]

    for half in range(2):
        window[half, pl.ds(36, 72, stride=SLOTS), :] = jnp.ones((72, 128), F32)
        for slot in range(37, 40):
            window[half, pl.ds(slot, 72, stride=SLOTS), :] = jnp.zeros((72, 128), F32)
        window[half, pl.ds(68 * SLOTS, 36), :] = jnp.zeros((36, 128), F32)
        for slot in (0, 1, 12, 13, 24, 25):
            window[half, pl.ds(2 * SLOTS + slot, ROWS, stride=SLOTS), :] = jnp.zeros((ROWS, 128), F32)
    for z in range(2):
        for c in range(2):
            put(2, ROWS, (z + 2) * 2 + c, lower_send[z, c].astype(F32))

    step_x = (me + 1) // 2
    freq_x = step_x.astype(F32) * (1.0 / 128.0)
    for copy in filter_in:
        copy.wait()
    weights = radial[...]
    centres = lax.broadcasted_iota(jnp.int32, (32, 512), 0).astype(F32)

    def filter_part(part, carry):
        lanes = pl.ds(pl.multiple_of(part * 512, 512), 512)
        kappa = jnp.sqrt(squares[:, lanes] + freq_x * freq_x) * (2.0 / math.sqrt(3.0))
        scaled = kappa * 31.0 - centres
        basis = jnp.exp(-scaled * scaled)
        values = table_times(split2(weights), basis)
        for j in range(4):
            profile[pl.ds(part * 4 + j, 128, stride=32), :] = values[:, j * 128 : (j + 1) * 128]
        return carry

    lax.fori_loop(0, 8, filter_part, 0)

    for copy in late_in:
        copy.wait()

    has_prev = me_z > 0
    has_next = me_z < GZ - 1
    has_up = me_y > 0
    has_down = me_y < GY - 1

    def fill_chunk(chunk):
        for copy in chunk_copies(chunk):
            copy.wait_recv()
        rows = pl.ds(pl.multiple_of(chunk * CHUNK, CHUNK), CHUNK)
        first = 2 + chunk * CHUNK
        for c in range(2):
            values = lower_prev[1, c, rows, :].astype(F32)
            put(first, CHUNK, 2 + c, jnp.where(has_prev, values, 0.0))
            for z in range(2):
                values = lower_next[z, c, rows, :].astype(F32)
                put(first, CHUNK, (z + 4) * 2 + c, jnp.where(has_next, values, 0.0))

    def fill_edge(side):
        for copy in edges[1 - side]:
            copy.wait_recv()
        for offset in range(3):
            valid = has_up if side == 0 else has_down
            if offset == 0:
                valid = jnp.logical_and(valid, has_prev)
            if offset == 2:
                valid = jnp.logical_and(valid, has_next)
            for row in range(2):
                lines = edge_recv[side, offset, pl.ds(row * 4, 4), :]
                lines = jnp.where(valid, lines, 0.0)
                at = (row if side == 0 else ROWS + 2 + row) * SLOTS + offset * 4
                for e, shifted in enumerate((shift_right(lines), lines, shift_left(lines))):
                    for half in range(2):
                        window[half, pl.ds(at + e * 12, 4), :] = shifted[
                            :, half * 128 : (half + 1) * 128
                        ]

    hear(0)
    tell(1)
    fill_edge(0)
    fill_chunk(0)

    w3_lane = lax.broadcasted_iota(jnp.int32, (48, 384), 1)
    w3_first = jnp.where(jnp.logical_and(w3_lane < 128, me_z == 0), 0.0, w3[...]).astype(BF16)
    w3_second = jnp.where(
        jnp.logical_and(w3_lane >= 256, me_z == GZ - 1), 0.0, w3[...]
    ).astype(BF16)

    def columns(r):
        start = pl.multiple_of((r - 1) * SLOTS, 8)
        return jnp.concatenate(
            [window[0, pl.ds(start, 128), :], window[1, pl.ds(start, 128), :]], axis=1
        ).astype(BF16)

    def second(first_layer):
        values = mul(w2[...], first_layer) + jnp.concatenate([b2[...]] * 2, axis=1)
        return jnp.maximum(values, 0.0).astype(BF16)

    def add_taps(acc, r, taps):
        valid = jnp.logical_not(
            jnp.logical_or(
                jnp.logical_and(r == 1, me_y == 0),
                jnp.logical_and(r == OWN_ROWS, me_y == GY - 1),
            )
        )
        taps = jnp.where(valid, taps, 0.0)
        for half in range(2):
            part = taps[:, half * 128 : (half + 1) * 128]
            at = [pl.ds(pl.multiple_of((r + 1 - b) * 16, 16), 16) for b in range(3)]
            acc[half, at[0], :] = part[0:16]
            acc[half, at[1], :] += part[16:32]
            acc[half, at[2], :] += part[32:48]

    for acc in (acc0, acc1):
        for half in range(2):
            acc[half, pl.ds(0, 32), :] = jnp.zeros((32, 128), F32)

    def group_rows(group):
        return [(sub, group * GROUP + 1 + sub) for sub in range(GROUP)]

    def later_first(group):
        for sub, r in group_rows(group):
            values = mul(w1[pl.ds(128, 384), :], columns(r))
            first_held[sub] = jnp.maximum(values, 0.0).astype(BF16)

    def later_second(group):
        for sub, r in group_rows(group):
            first_layer = first_held[sub]
            layers = [second(first_layer[p * 128 : (p + 1) * 128]) for p in range(3)]
            hidden[r] = jnp.concatenate(layers[0:2], axis=0)
            last_held[sub] = layers[2]

    def later_last(group):
        for sub, r in group_rows(group):
            stacked = jnp.concatenate([hidden[r], last_held[sub]], axis=0)
            add_taps(acc1, r, mul(w3_second, stacked))

    def early_first(group):
        for sub, r in group_rows(group):
            values = mul(w1[pl.ds(0, 128), :], columns(r))
            first_held[sub, pl.ds(0, 128)] = jnp.maximum(values, 0.0).astype(BF16)

    def early_second(group):
        for sub, r in group_rows(group):
            last_held[sub] = second(first_held[sub, pl.ds(0, 128)])

    def early_last(group):
        for sub, r in group_rows(group):
            stacked = jnp.concatenate([last_held[sub], hidden[r]], axis=0)
            add_taps(acc0, r, mul(w3_first, stacked))

    def start_groups(first, middle, last):
        first(0)
        middle(0)
        first(1)

    def run_groups(first, middle, last, begin, end):
        def step(group, carry):
            last(group - 2)
            middle(group - 1)
            first(group)
            return carry

        lax.fori_loop(begin, end, step, 0)

    def end_groups(first, middle, last):
        last(GROUPS - 2)
        middle(GROUPS - 1)
        last(GROUPS - 1)

    later = (later_first, later_second, later_last)
    early = (early_first, early_second, early_last)

    later_first(0)
    fill_edge(1)
    fill_chunk(1)
    later_second(0)
    later_first(1)
    fill_chunk(2)
    hear(1)
    tell(2)
    run_groups(*later, 2, 4)
    fill_chunk(3)
    hear(2)
    tell(3)
    run_groups(*later, 4, GROUPS)
    end_groups(*later)
    hear(3)

    def couple(acc, z, parity):
        raw = []
        for o in range(4):
            taps = [
                jnp.concatenate(
                    [
                        acc[half, pl.ds((2 + parity) * 16 + e * 4 + o, 32, stride=32), :]
                        for half in range(2)
                    ],
                    axis=1,
                )
                for e in range(3)
            ]
            raw.append(shift_right(taps[0]) + taps[1] + shift_left(taps[2]) + output_b[o])
        lines = [
            jnp.concatenate(
                [
                    dens2[half, c, z, pl.ds(parity, 32, stride=2), :]
                    for half in range(2)
                ],
                axis=1,
            )
            for c in range(4)
        ]
        scales = [jnp.tanh(raw[0]), jnp.tanh(raw[1])]
        for o in range(2):
            lines[2 + o] = lines[2 + o] * jnp.exp(scales[o]) + raw[2 + o]
        return jnp.concatenate(lines, axis=0), scales[0] + scales[1]

    def spread_x(values):
        high, mid, low = split3(values)
        return mul(high, spread[...]) + (mul(mid, spread[...]) + mul(low, spread[...]))

    def fold(values):
        rows, lanes = values.shape
        total = values[:, 0:128]
        for at in range(128, lanes, 128):
            total = total + values[:, at : at + 128]
        return jnp.sum(total.reshape(rows // 8, 8, 128), axis=0)

    source, scale_sum = couple(acc1, 1, 0)
    kept[0] = source
    total = fold(scale_sum)
    high, low = split2(source)
    both = mul(forward_x[0], jnp.concatenate([high, low], axis=0), ((1,), (1,)))
    x_modes = both[:, :128] + (both[:, 128:] + mul(forward_x[1], high, ((1,), (1,))))
    x_send[...] = x_modes.reshape(COUNT, 2, 128)

    sent = list(halo)

    def send_one(part, dst, stage, step):
        to = near(step)
        pltpu.make_async_remote_copy(
            src_ref=part(to), dst_ref=dst.at[me], send_sem=all_ssem.at[stage],
            recv_sem=all_rsem.at[stage], device_id=to, device_id_type=LOGICAL,
        ).start()

    def send_all(part, dst, stage):
        def one(i, carry):
            for sub in range(4):
                send_one(part, dst, stage, 4 * i + sub)
            return carry

        for step in range(1, 4):
            send_one(part, dst, stage, step)
        lax.fori_loop(1, COUNT // 4, one, 0)
        dst[me] = part(me)[...]

    def wait_all(dst, stage):
        copy = pltpu.make_async_remote_copy(
            src_ref=dst.at[pl.ds(0, COUNT - 1)], dst_ref=dst.at[pl.ds(0, COUNT - 1)],
            send_sem=all_ssem.at[stage], recv_sem=all_rsem.at[stage],
            device_id=near(1), device_id_type=LOGICAL,
        )
        copy.wait_recv()
        sent.append(copy)

    def x_part(to):
        return x_send.at[to]

    send_all(x_part, z_recv, 0)
    far_plane.wait_recv()
    for c in range(2):
        put(2, ROWS, c, jnp.where(has_prev, lower_prev[0, c].astype(F32), 0.0))
    start_groups(*early)
    run_groups(*early, 2, 4)
    kept[1], scale_sum = couple(acc1, 1, 1)
    total = total + fold(scale_sum)
    wait_all(z_recv, 0)

    z_modes = table_times(forward_z, z_recv[...].reshape(256, 128))

    lines = jnp.concatenate([z_modes[g * 64 : (g + 1) * 64] for g in range(GY)], axis=1)
    modes = times_table(lines, forward_y)
    parts = [
        modes[k * 32 : (k + 1) * 32, c * 128 : (c + 1) * 128] for k in range(2) for c in range(4)
    ]
    for o in range(16):
        value = profile[pl.ds(o * 256, 32), :] * parts[0]
        for c in range(1, 8):
            value = value + profile[pl.ds(o * 256 + c * 32, 32), :] * parts[c]
        mixed[pl.ds((o // 4) * 32, 32), pl.ds((o % 4) * 128, 128)] = value
    back = times_table(mixed[...], forward_y, turned=True)
    lines = jnp.concatenate(
        [
            jnp.concatenate(
                [back[:, g * 128 : (g + 1) * 128] for g in (2 * pair, 2 * pair + 1)], axis=0
            )
            for pair in range(2)
        ],
        axis=1,
    )
    planes = table_times(backward_z, lines)
    for pair in range(2):
        part = planes[:, pair * 128 : (pair + 1) * 128]
        zb_send[:, pl.ds(pair * 2, 2)] = part.reshape(GZ, 2, 4, 128)

    send_all(lambda to: zb_send.at[to // GY, lax.rem(to, GY)], x_recv, 1)

    run_groups(*early, 4, GROUPS)
    end_groups(*early)
    squares_sum = fold(kept[0] * kept[0])
    for parity in range(2):
        coupled, scale_sum = couple(acc0, 0, parity)
        kept[2 + parity] = coupled
        total = total + fold(scale_sum)
        squares_sum = squares_sum + fold(coupled * coupled)
    target = spread_x(kept[1])
    wait_all(x_recv, 1)

    lines = jnp.concatenate([x_recv[:, og, :] for og in range(4)], axis=1)
    moved = table_times(backward_x, lines)
    shifts = [jnp.transpose(moved[:, og * 128 : (og + 1) * 128]) for og in range(4)]
    for k in range(2):
        scale = jnp.tanh(shifts[k])
        total = total + fold(scale)
        moved = target[:, k * 128 : (k + 1) * 128] * jnp.exp(scale) + shifts[2 + k]
        squares_sum = squares_sum + fold(moved * moved)
        latent[pl.ds(8 + k * 4, 4), 0] = moved.reshape(4, 32, 128)

    total = total - 0.5 * squares_sum
    sum_send[0] = jnp.sum(total, axis=0, keepdims=True)

    send_all(lambda to: sum_send.at[0], sum_recv, 2)
    for parity in range(2):
        coupled = spread_x(kept[2 + parity])
        for k in range(2):
            at = (2 * parity + k) * 4
            factored[pl.ds(at, 4), 0] = coupled[:, k * 128 : (k + 1) * 128].reshape(4, 32, 128)
    source = spread_x(kept[0])
    for k in range(2):
        latent[pl.ds(k * 4, 4), 0] = source[:, k * 128 : (k + 1) * 128].reshape(4, 32, 128)
    wait_all(sum_recv, 2)
    total = jnp.sum(sum_recv[...], axis=0)
    for copy in sent:
        copy.wait_send()
    count = 4.0 * 64 * 256 * 256
    log_density[0, 0] = jnp.sum(total) / count - 0.5 * math.log(2.0 * math.pi)


def shards(consts, density_field, first_weight, first_bias, middle_weight, middle_bias, output_weight, output_bias, radial_weights):
    vmem = pl.BlockSpec(memory_space=pltpu.VMEM)
    smem = pl.BlockSpec(memory_space=pltpu.SMEM)
    hbm = pl.BlockSpec(memory_space=pltpu.HBM)
    operands = [
        density_field, first_weight, first_bias.reshape(1, 128), middle_weight,
        middle_bias.reshape(1, 128), output_weight, output_bias, radial_weights.reshape(128, 32),
    ] + [jnp.asarray(value) for value in consts.values()]
    specs = [hbm] * len(operands)
    held = [pltpu.VMEM(value.shape, value.dtype) for value in operands]
    held[6] = pltpu.SMEM(output_bias.shape, F32)
    buffers = [
        pltpu.VMEM((2, 2, ROWS, WIDE), BF16),
        pltpu.VMEM((2, 8, WIDE), F32),
        pltpu.VMEM((2, 2, ROWS, WIDE), BF16),
        pltpu.VMEM((2, 2, ROWS, WIDE), BF16),
        pltpu.VMEM((2, 3, 8, WIDE), F32),
        pltpu.VMEM((2, 72 * SLOTS, 128), F32),
        pltpu.VMEM((OWN_ROWS + 2, 256, WIDE), BF16),
        pltpu.VMEM((2, 70 * 16, 128), F32),
        pltpu.VMEM((2, 70 * 16, 128), F32),
        pltpu.VMEM((64, 128), F32),
        pltpu.VMEM((512, 128), BF16),
        pltpu.VMEM((128, 128), BF16),
        pltpu.VMEM((128, 128), F32),
        pltpu.VMEM((48, 384), F32),
        pltpu.VMEM((108, 128), F32),
        pltpu.VMEM((128 * 32, 128), F32),
        pltpu.VMEM((COUNT, 2, 128), F32),
        pltpu.VMEM((COUNT, 2, 128), F32),
        pltpu.VMEM((128, 512), F32),
        pltpu.VMEM((GZ, GY, 4, 128), F32),
        pltpu.VMEM((COUNT, 4, 128), F32),
        pltpu.VMEM((4, 128, WIDE), F32),
        pltpu.VMEM((GROUP, 384, WIDE), BF16),
        pltpu.VMEM((GROUP, 128, WIDE), BF16),
        pltpu.VMEM((1, 1, 128), F32),
        pltpu.VMEM((COUNT, 1, 128), F32),
        pltpu.VMEM((2, 4, 2, ROWS, 128), F32),
    ] + held[1:] + [
        pltpu.SemaphoreType.DMA((15,)),
        pltpu.SemaphoreType.DMA((15,)),
        pltpu.SemaphoreType.DMA((3,)),
        pltpu.SemaphoreType.DMA((3,)),
        pltpu.SemaphoreType.DMA((19,)),
        pltpu.SemaphoreType.REGULAR((4,)),
    ]
    operands = [pltpu.with_memory_space_constraint(value, pltpu.HBM) for value in operands]
    factored, latent, log_density = pl.pallas_call(
        flow_kernel,
        out_shape=(
            jax.ShapeDtypeStruct((16, 1, 32, 128), F32),
            jax.ShapeDtypeStruct((16, 1, 32, 128), F32),
            jax.ShapeDtypeStruct((1, 1), F32),
        ),
        in_specs=specs,
        out_specs=(vmem, vmem, smem),
        scratch_shapes=buffers,
        compiler_params=pltpu.CompilerParams(
            collective_id=0, has_side_effects=True, vmem_limit_bytes=52 * 1024 * 1024
        ),
        name="flow",
    )(*operands)
    return factored, latent, log_density.reshape(())


def solution(mesh):
    assert mesh.shape["gz"] == GZ and mesh.shape["gy"] == GY
    in_specs = (P(None, "gz", "gy", None), P(), P(), P(), P(), P(), P(), P())
    out_specs = (P(None, "gz", "gy", None), P(None, "gz", "gy", None), P())
    return jax.shard_map(
        functools.partial(shards, tables()),
        mesh=mesh, in_specs=in_specs, out_specs=out_specs, check_vma=False,
    )
```
